32 devices in a mesh: dp: 4 (over x, core), replica: 8 (over z, y).
Axes of the slice: x: 2, y: 2, z: 4, core: 2. Of those that a mesh axis runs over, the one named last changes fastest.
Arguments:
- tokens: bfloat16 [16384, 768], P(('dp', 'replica')), may hold values from -6 to 6
- segments: int32 [64, 256], P(('dp', 'replica')), may hold values from 0 to 7, never falling along the last dimension, each value on 1 to 64 neighbouring positions
- picked: int32 [64, 8, 10], P(('dp', 'replica')), may hold values from 0 to 255
- offsets: int32 [511], replicated, may hold values from 0 to 31
- memory_bank: bfloat16 [256, 2, 768], replicated, may hold values from -6 to 6
- side_tokens: bfloat16 [8192, 768], P(('dp', 'replica')), may hold values from -6 to 6
- side_segments: int32 [32, 256], P(('dp', 'replica')), may hold values from 0 to 7, never falling along the last dimension, each value on 1 to 64 neighbouring positions
- w_query: bfloat16 [768, 768], replicated, may hold values from -0.02734375 to 0.02734375
- w_key: bfloat16 [768, 768], replicated, may hold values from -0.21875 to 0.21875
- w_value: bfloat16 [768, 768], replicated, may hold values from -0.21875 to 0.21875
- w_attn_out: bfloat16 [768, 768], replicated, may hold values from -0.625 to 0.625
- w_inner: bfloat16 [768, 3072], replicated, may hold values from -0.21875 to 0.21875
- w_outer: bfloat16 [3072, 768], replicated, may hold values from -0.109375 to 0.109375
- bias_table: float32 [32, 12], replicated, may hold values from -4 to 4
- gain_one: float32 [768], replicated, may hold values from 0.5 to 1.5
- gain_two: float32 [768], replicated, may hold values from 0.5 to 1.5
- cotangent: bfloat16 [16384, 768], P(('dp', 'replica')), may hold values from -6 to 6
- side_cotangent: bfloat16 [8192, 768], P(('dp', 'replica')), may hold values from -6 to 6
Outputs:
- output: bfloat16 [16384, 768], P(('dp', 'replica'))
- grad_tokens: bfloat16 [16384, 768], P(('dp', 'replica'))
- side_output: bfloat16 [8192, 768], P(('dp', 'replica'))
- grad_side_tokens: bfloat16 [8192, 768], P(('dp', 'replica'))
- grad_w_query: float32 [768, 768], replicated
- grad_w_key: float32 [768, 768], replicated
- grad_w_value: float32 [768, 768], replicated
- grad_w_attn_out: float32 [768, 768], replicated
- grad_w_inner: float32 [768, 3072], replicated
- grad_w_outer: float32 [3072, 768], replicated
- grad_bias_table: float32 [32, 12], replicated
- grad_gain_one: float32 [768], replicated
- grad_gain_two: float32 [768], replicated
The draws below stay inside these ranges and needn't reach their ends.
Inputs may be any that keep to these rules, and one draw needn't show every extreme that they name: `segments`: in each row the segment ids number its 8 questions in order of position, every question holding at least one token. `side_segments`: in each side row the ids number its 8 pairs in order of position, every pair holding at least one token.
All inputs are finite; a program needn't handle non-finite values.
Results may differ from the reference program's by a relative error of at most 0.013.
Values sent between devices are 32-bit elements; how exact they have to be, the bound alone decides.
A program may use at most 256 MiB of HBM per device.

```python
import math
import jax
import jax.numpy as jnp
import numpy as np
from jax import lax

D = 768
H = 12
DH = 64
FF = 3072
NBUCKETS = 32
TOPK = 10
ROW_LEN = 256
QUESTIONS = 8
Q_MOST = 64
BANK = 256
SIDE_LEN = 256
SIDE_PAIRS = 8
SIDE_MOST = 64
ROWS = 64
TOKENS = 16384
SIDE_ROWS = 32
SIDE_TOKENS = 8192


def place_ends(values, key, low, high):
    longest = values.shape.index(max(values.shape))
    spots = []
    for shift in (0, 1):
        where = [jax.random.randint(jax.random.fold_in(key, axis), (), 0, length) for axis, length in enumerate(values.shape)]
        where[longest] = (where[longest] + shift) % values.shape[longest]
        spots.append(tuple(where))
    return values.at[spots[0]].set(low).at[spots[1]].set(high)


def level_of(own_key, extent, split, smallest, top_value):
    def one(dim, shards_of):
        heights = jax.random.uniform(jax.random.fold_in(jax.random.fold_in(own_key, 6), dim), (shards_of,), jnp.float32, smallest / len(split), top_value / len(split))
        return jnp.repeat(jnp.exp(heights), extent[dim] // shards_of).reshape((-1,) + (1,) * (len(extent) - dim - 1))

    level = one(*split[0])
    for cut in split[1:]:
        level = level * one(*cut)
    return level


def split_up(amount, total, reach, lean):
    portions = [(1 << 20) // math.isqrt(grade ** lean) + 1 for grade in range(2, amount + 1)]
    surplus, given = total - reach - (amount - 1), [1] * (amount - 1)
    while surplus > 0:
        candidates = [i for i in range(amount - 1) if given[i] < reach]
        pool, left = sum([portions[i] for i in candidates]), surplus
        for i in candidates:
            more = min(reach - given[i], max(1, left * portions[i] // pool), surplus)
            given[i] = given[i] + more
            surplus = surplus - more
    return np.array([reach] + given)


def ragged(key, number_of, total, most, slope):
    if number_of == 2:
        one = jax.random.randint(key, (), max(1, total - most), min(most, total - 1) + 1)
        return jnp.stack([one, total - one])
    lengths = jnp.asarray(split_up(number_of, total, most, slope), jnp.int32)
    couples = (number_of - 1) // 2
    giver, sink = lengths[1:1 + 2 * couples:2], lengths[2:2 + 2 * couples:2]
    margin = jnp.minimum(giver - 1, most - sink)
    passed = jax.random.randint(jax.random.fold_in(key, 1), (couples,), 0, 1 << 20) % (margin + 1)
    lengths = lengths.at[1:1 + 2 * couples:2].set(giver - passed).at[2:2 + 2 * couples:2].set(sink + passed)
    return lengths[jax.random.permutation(jax.random.fold_in(key, 2), number_of)]


def gaussian(stream_key, dims, scale, limit, shards=(), held_as=jnp.bfloat16):
    values = jax.random.normal(stream_key, dims, jnp.float32) * scale
    if len(shards) > 0:
        values = level_of(stream_key, dims, shards, -0.22, 0.18) * values
    return jnp.clip(values, min=-limit, max=limit).astype(held_as)


def setup_inputs(seed: int = 0) -> dict:
    key_of = jax.random.split(jax.random.key(seed), 19)
    tokens = gaussian(key_of[0], (TOKENS, D), 1.0, 6.0, ((0, 32),))
    segments = jax.vmap(lambda own: jnp.searchsorted(jnp.cumsum(ragged(own, QUESTIONS, ROW_LEN, Q_MOST, 0)), jnp.arange(ROW_LEN), side="right"))(jax.random.split(key_of[1], ROWS)).reshape((ROWS, ROW_LEN)).astype(jnp.int32)
    picked = place_ends(jax.random.randint(key_of[2], (ROWS, QUESTIONS, TOPK), 0, BANK), jax.random.fold_in(key_of[2], 1), 0, BANK - 1).astype(jnp.int32)
    offsets = place_ends(jax.random.randint(key_of[3], (2 * ROW_LEN - 1,), 0, NBUCKETS), jax.random.fold_in(key_of[3], 1), 0, NBUCKETS - 1).astype(jnp.int32)
    memory_bank = gaussian(key_of[4], (BANK, 2, D), 1.0, 6.0)
    side_tokens = gaussian(key_of[5], (SIDE_TOKENS, D), 1.0, 6.0, ((0, 32),))
    side_segments = jax.vmap(lambda own: jnp.searchsorted(jnp.cumsum(ragged(own, SIDE_PAIRS, SIDE_LEN, SIDE_MOST, 0)), jnp.arange(SIDE_LEN), side="right"))(jax.random.split(key_of[6], SIDE_ROWS)).reshape((SIDE_ROWS, SIDE_LEN)).astype(jnp.int32)
    w_query = gaussian(key_of[7], (D, H * DH), (D * DH) ** -0.5, 0.02734375)
    w_key = gaussian(key_of[8], (D, H * DH), D ** -0.5, 0.21875)
    w_value = gaussian(key_of[9], (D, H * DH), D ** -0.5, 0.21875)
    w_attn_out = gaussian(key_of[10], (H * DH, D), (H * DH // 8) ** -0.5, 0.625)
    w_inner = gaussian(key_of[11], (D, FF), D ** -0.5, 0.21875)
    w_outer = gaussian(key_of[12], (FF, D), FF ** -0.5, 0.109375)
    bias_table = gaussian(key_of[13], (NBUCKETS, H), 1.0, 4.0, (), jnp.float32)
    gain_one = jnp.clip(1.0 + 0.1 * jax.random.normal(key_of[14], (D,), jnp.float32), 0.5, 1.5)
    gain_two = jnp.clip(1.0 + 0.1 * jax.random.normal(key_of[15], (D,), jnp.float32), 0.5, 1.5)
    cotangent = gaussian(key_of[16], (TOKENS, D), 1.0, 6.0, ((0, 32),))
    side_cotangent = gaussian(key_of[17], (SIDE_TOKENS, D), 1.0, 6.0, ((0, 32),))
    return dict(tokens=tokens, segments=segments, picked=picked, offsets=offsets, memory_bank=memory_bank, side_tokens=side_tokens, side_segments=side_segments, w_query=w_query, w_key=w_key, w_value=w_value, w_attn_out=w_attn_out, w_inner=w_inner, w_outer=w_outer, bias_table=bias_table, gain_one=gain_one, gain_two=gain_two, cotangent=cotangent, side_cotangent=side_cotangent)


epsilon = 1e-06
masked_value = -1e+30
highest = lax.Precision.HIGHEST

@jax.custom_vjp
def low(v):
    return lax.optimization_barrier(v.astype(jnp.bfloat16)).astype(jnp.float32)

@jax.custom_vjp
def low_back(v):
    return v

def low_keep(v):
    return (low(v), None)

def low_pass(kept, grad):
    return (grad,)

def back_keep(v):
    return (v, None)

def back_low(kept, grad):
    return (low(grad),)
low.defvjp(low_keep, low_pass)
low_back.defvjp(back_keep, back_low)

def rms_scale(values, gain):
    return values * lax.rsqrt(lax.optimization_barrier(jnp.mean(values * values, axis=-1, keepdims=True)) + epsilon) * gain

def product(left, right):
    return jnp.dot(left, right, precision=highest)

def row_forward(weights, row_input, segment_row, picked_row, offsets, bank_float):
    w_query, w_key, w_value, w_attn_out, w_inner, w_outer, bias_table, gain_one, gain_two = weights
    row_length = row_input.shape[0]
    model_width = row_input.shape[1]
    head_count = bias_table.shape[1]
    center = (offsets.shape[0] - 1) // 2
    slot_count = picked_row.shape[0] * picked_row.shape[1] * 2
    memory = bank_float[picked_row.reshape(-1)].reshape(slot_count, model_width)
    normed = low(rms_scale(row_input, gain_one))
    mem_normed = low(rms_scale(memory, gain_one))
    both_normed = jnp.concatenate([normed, mem_normed], axis=0)
    queries = low(low_back(product(normed, w_query)))
    keys_all = low(low_back(product(both_normed, w_key)))
    values_all = low(low_back(product(both_normed, w_value)))
    query_heads = queries.reshape(row_length, head_count, -1)
    key_heads = keys_all.reshape(keys_all.shape[0], head_count, -1)
    value_heads = values_all.reshape(values_all.shape[0], head_count, -1)
    slot_question = jnp.arange(slot_count, dtype=jnp.int32) // (picked_row.shape[1] * 2)
    block_rows = min(512, row_length)

    def one_block(block_index):
        block_start = (block_index * block_rows).astype(jnp.int32)
        query_block = lax.dynamic_slice_in_dim(query_heads, block_start, block_rows, 0)
        segment_block = lax.dynamic_slice_in_dim(segment_row, block_start, block_rows, 0)
        scores = jnp.einsum('qhd,khd->hqk', query_block, key_heads, precision=highest)
        query_pos = block_start + jnp.arange(block_rows, dtype=jnp.int32)
        key_pos = jnp.arange(row_length, dtype=jnp.int32)
        bucket = offsets[key_pos[None, :] - query_pos[:, None] + center]
        bias = jnp.transpose(bias_table[bucket], (2, 0, 1))
        scores = jnp.concatenate([scores[:, :, :row_length] + bias, scores[:, :, row_length:]], axis=2)
        allowed = jnp.concatenate([segment_block[:, None] == segment_row[None, :], segment_block[:, None] == slot_question[None, :]], axis=1)
        scores = low_back(scores)
        scores = jnp.where(allowed[None], scores, masked_value)
        soft = low(jax.nn.softmax(scores, axis=2))
        mixed_rows = jnp.einsum('hqk,khd->qhd', soft, value_heads, precision=highest)
        return mixed_rows.reshape(block_rows, -1)
    mixed_rows = lax.map(jax.checkpoint(one_block), jnp.arange(row_length // block_rows, dtype=jnp.int32))
    attended = low(low_back(mixed_rows.reshape(row_length, -1)))
    hidden_one = row_input + low_back(product(attended, w_attn_out))
    normed_two = low(rms_scale(hidden_one, gain_two))
    inner_pre = low_back(product(normed_two, w_inner))
    activated = low(jax.nn.gelu(inner_pre))
    return hidden_one + product(activated, w_outer)

def run_rows(weights, totals, inputs, segment_rows, picked_rows, cotangents, offsets, bank_float):
    row_count = segment_rows.shape[0]
    row_length = segment_rows.shape[1]
    model_width = inputs.shape[1]
    row_inputs = inputs.astype(jnp.float32).reshape(row_count, row_length, model_width)
    row_cotangents = cotangents.astype(jnp.float32).reshape(row_count, row_length, model_width)

    def one_row(carry, members):
        row_input, segment_row, picked_row, row_cotangent = members

        def forward(weight_set, input_rows):
            return row_forward(weight_set, input_rows, segment_row, picked_row, offsets, bank_float)
        output_row, pullback = jax.vjp(forward, weights, row_input)
        weight_grads, input_grad = pullback(row_cotangent)
        carry = jax.tree.map(jnp.add, carry, weight_grads)
        return (carry, (output_row.astype(jnp.bfloat16), input_grad.astype(jnp.bfloat16)))
    totals, (outputs, input_grads) = lax.scan(one_row, totals, (row_inputs, segment_rows, picked_rows, row_cotangents))
    return (totals, outputs.reshape(-1, model_width), input_grads.reshape(-1, model_width))

def reference(tokens, segments, picked, offsets, memory_bank, side_tokens, side_segments, w_query, w_key, w_value, w_attn_out, w_inner, w_outer, bias_table, gain_one, gain_two, cotangent, side_cotangent):
    weights = tuple((member.astype(jnp.float32) for member in (w_query, w_key, w_value, w_attn_out, w_inner, w_outer, bias_table, gain_one, gain_two)))
    bank_float = memory_bank.astype(jnp.float32)
    zero_grads = jax.tree.map(jnp.zeros_like, weights)
    totals, outputs, input_grads = run_rows(weights, zero_grads, tokens, segments, picked, cotangent, offsets, bank_float)
    no_memory = jnp.zeros((side_segments.shape[0], 0, picked.shape[2]), jnp.int32)
    totals, side_outputs, side_grads = run_rows(weights, totals, side_tokens, side_segments, no_memory, side_cotangent, offsets, bank_float)
    return (outputs, input_grads, side_outputs, side_grads, totals[0], totals[1], totals[2], totals[3], totals[4], totals[5], totals[6], totals[7], totals[8])
```

```python
import functools

import jax
import jax.numpy as jnp
from jax import lax
from jax.experimental import pallas as pl
from jax.experimental.pallas import tpu as pltpu
from jax.sharding import PartitionSpec as P

MESH = pl.DeviceIdType.MESH

BLK = 384
STG = ['P','A','B','C1','C2','C3','D','E','F1','F2','F3','G','H']
GAPS = (1, 2, 1, 1, 3, 2, 2, 2, 1, 2, 2, 1)
def offsets_of(gaps):
    o, a = {}, 0
    for s, g in zip(STG, (0,)+tuple(gaps)):
        a += g; o[s] = a
    return o

class Place:
    def __init__(self):
        dp = lax.axis_index("dp"); rep = lax.axis_index("replica")
        self.core = lax.rem(dp, 2); x = dp // 2; z = rep // 2; y = lax.rem(rep, 2)
        c = self.core
        self.partner = (dp + 1 - 2 * c, rep)
        xn = (dp + 2 - 4 * x, rep); yn = (dp, rep + 1 - 2 * y)
        pick = lambda a, b: tuple(jnp.where(c == 0, i, j) for i, j in zip(a, b))
        self.n1 = pick(xn, yn); self.n2 = pick(yn, xn)
        self.b1 = jnp.where(c == 0, x, y); self.b2 = jnp.where(c == 0, y, x)
        self.end = (z == 0) | (z == 3)
        self.mid = (z == 1) | (z == 2)
        left = jnp.where(z < 2, 1, 0)
        near = z + 1 - 2 * lax.rem(z, 2)
        far = 3 - z
        self.near = (dp, near * 2 + y)
        self.far = (dp, far * 2 + y)
        self.fh = left
        self.bh = 1 - left

class Comm:
    NP = 4; N0 = 4; N1 = 6; NZ = 6; N3 = 6
    def __init__(self, units, gaps):
        self.n = units; self.off = offsets_of(gaps); self.NW = self.off['F1'] + 1
        self.steps = units + self.off['H']
    def scratch(self):
        n = self.n; D = pltpu.SemaphoreType.DMA; V = lambda *s: pltpu.VMEM(s, jnp.float32)
        return dict(
            W=V(self.NW, BLK, BLK), L0=V(self.N0, BLK, BLK), L1=V(self.N1, BLK//2, BLK),
            LA=V(self.NZ, BLK//4, BLK), LB=V(self.NZ, BLK//4, BLK), L3=V(self.N3, BLK//8, BLK),
            s0=D((self.N0,)), r0=D((self.N0,)), s1=D((self.NW,)), r1=D((self.N1,)),
            sz=D((self.NW, 2)), rA=D((self.NZ,)), rB=D((self.NZ,)), s3=D((self.NW,)), r3=D((self.N3,)),
            s4=D((self.NW,)), r4=D((n,)), lo=D((self.NW,)),
            sg=D((n, 2)), gA=D((n,)), gB=D((n,)), s6=D((n, 2)), r6=D((n, 2)), s7=D((n,)), r7=D((n,)),
            c0=pltpu.SemaphoreType.REGULAR, c1=pltpu.SemaphoreType.REGULAR,
            cA=pltpu.SemaphoreType.REGULAR, cB=pltpu.SemaphoreType.REGULAR, c3=pltpu.SemaphoreType.REGULAR)
    def bind(self, s, out, src0):
        self.s = s; self.out = out; self.src0 = src0; self.p = Place()
    def entry(self):
        p = self.p; b = pltpu.get_barrier_semaphore()
        for d in (p.partner, p.n1, p.n2, p.near):
            pl.semaphore_signal(b, inc=1, device_id=d, device_id_type=MESH)
        @pl.when(p.mid)
        def _():
            pl.semaphore_signal(b, inc=1, device_id=p.far, device_id_type=MESH)
            pl.semaphore_wait(b, 5)
        @pl.when(p.end)
        def _():
            pl.semaphore_wait(b, 4)
    def rc(self, src, dst, ss, rs, dev):
        return pltpu.make_async_remote_copy(src_ref=src, dst_ref=dst, send_sem=ss, recv_sem=rs, device_id=dev, device_id_type=MESH)
    def k0(self, u):
        s = self.s; i = lax.rem(u, self.N0)
        return self.rc(self.src0(u), s['L0'].at[i], s['s0'].at[i], s['r0'].at[i], self.p.partner)
    def w(self, u): return lax.rem(u, self.NW)
    def k1(self, u):
        s = self.s; w = self.w(u); i = lax.rem(u, self.N1)
        return self.rc(s['W'].at[w, pl.ds((1 - self.p.b1) * 192, 192)], s['L1'].at[i], s['s1'].at[w], s['r1'].at[i], self.p.n1)
    def zrow(self, h): return self.p.b1 * 192 + h * 96
    def kz(self, u, h, L, r, dev, j):
        s = self.s; w = self.w(u); i = lax.rem(u, self.NZ)
        return self.rc(s['W'].at[w, pl.ds(self.zrow(h), 96)], s[L].at[i], s['sz'].at[w, j], s[r].at[i], dev)
    def k3(self, u):
        s = self.s; w = self.w(u); i = lax.rem(u, self.N3)
        return self.rc(s['W'].at[w, pl.ds(self.zrow(self.p.bh) + (1 - self.p.b2) * 48, 48)], s['L3'].at[i], s['s3'].at[w], s['r3'].at[i], self.p.n2)
    def own(self): return pl.ds(self.zrow(self.p.bh) + self.p.b2 * 48, 48)
    def k4(self, u):
        s = self.s; w = self.w(u)
        return self.rc(s['W'].at[w, self.own()], self.out.at[u, self.p.core, self.own()], s['s4'].at[w], s['r4'].at[u], self.p.n2)
    def kl(self, u):
        s = self.s; w = self.w(u)
        return pltpu.make_async_copy(s['W'].at[w, self.own()], self.out.at[u, self.p.core, self.own()], s['lo'].at[w])
    def piece(self, u, h): return self.out.at[u, self.p.core, pl.ds(self.zrow(h), 96)]
    def kg(self, u, h, r, dev, j):
        s = self.s
        return self.rc(self.piece(u, h), self.piece(u, h), s['sg'].at[u, j], s[r].at[u], dev)
    def k6(self, u, h):
        s = self.s
        return self.rc(self.piece(u, h), self.piece(u, h), s['s6'].at[u, h], s['r6'].at[u, h], self.p.n1)
    def k7(self, u):
        s = self.s; o = self.out.at[u, self.p.core]
        return self.rc(o, o, s['s7'].at[u], s['r7'].at[u], self.p.partner)
    def give(self, name, u, N, dev):
        @pl.when(u + N < self.n)
        def _(): pl.semaphore_signal(self.s[name], inc=1, device_id=dev, device_id_type=MESH)
    def take(self, name, u, N):
        @pl.when(u >= N)
        def _(): pl.semaphore_wait(self.s[name], 1)
    def send0(self, u):
        self.take('c0', u, self.N0)
        self.k0(u).start()
    def A(self, u):
        s = self.s; p = self.p; w = self.w(u); i = lax.rem(u, self.N0)
        self.k0(u).wait()
        s['W'][w] = s['W'][w] + s['L0'][i]
        self.give('c0', u, self.N0, p.partner)
        self.take('c1', u, self.N1)
        self.k1(u).start()
    def B(self, u):
        s = self.s; p = self.p; w = self.w(u); i = lax.rem(u, self.N1)
        self.k1(u).wait_recv()
        rows = pl.ds(p.b1 * 192, 192)
        s['W'][w, rows] = s['W'][w, rows] + s['L1'][i]
        self.give('c1', u, self.N1, p.n1)
        @pl.when(p.end)
        def _():
            self.take('cA', u, self.NZ)
            self.kz(u, p.fh, 'LA', 'rA', p.near, 0).start()
    def zadd(self, u, h, L, r):
        s = self.s; w = self.w(u); i = lax.rem(u, self.NZ)
        self.kz(u, h, L, r, self.p.near, 0).wait_recv()
        rows = pl.ds(self.zrow(h), 96)
        s['W'][w, rows] = s['W'][w, rows] + s[L][i]
    def C1(self, u):
        p = self.p
        @pl.when(p.mid)
        def _():
            self.zadd(u, p.fh, 'LA', 'rA')
            self.give('cA', u, self.NZ, p.near)
            self.take('cB', u, self.NZ)
            self.kz(u, p.fh, 'LB', 'rB', p.far, 0).start()
    def C2(self, u):
        p = self.p
        @pl.when(p.mid)
        def _():
            self.zadd(u, p.bh, 'LB', 'rB')
            self.give('cB', u, self.NZ, p.far)
            self.take('cA', u, self.NZ)
            self.kz(u, p.bh, 'LA', 'rA', p.near, 1).start()
    def C3(self, u):
        p = self.p
        @pl.when(p.end)
        def _():
            self.zadd(u, p.bh, 'LA', 'rA')
            self.give('cA', u, self.NZ, p.near)
            self.take('c3', u, self.N3)
            self.k3(u).start()
    def D(self, u):
        s = self.s; p = self.p; w = self.w(u); i = lax.rem(u, self.N3)
        @pl.when(p.end)
        def _():
            self.k3(u).wait_recv()
            s['W'][w, self.own()] = s['W'][w, self.own()] + s['L3'][i]
            self.give('c3', u, self.N3, p.n2)
            self.k4(u).start(); self.kl(u).start()
    def E(self, u):
        p = self.p
        self.k1(u).wait_send()
        self.kz(u, p.fh, 'LB', 'rB', p.far, 0).wait_send()
        @pl.when(p.mid)
        def _(): self.kz(u, p.bh, 'LA', 'rA', p.near, 1).wait_send()
        @pl.when(p.end)
        def _():
            self.k3(u).wait_send()
            self.kl(u).wait()
            self.k4(u).wait()
            self.kg(u, p.bh, 'gA', p.near, 0).start()
            self.k6(u, p.bh).start()
    def F1(self, u):
        p = self.p
        @pl.when(p.mid)
        def _():
            self.kg(u, p.bh, 'gA', p.near, 0).wait_recv()
            self.kg(u, p.bh, 'gB', p.far, 0).start()
            self.k6(u, p.bh).start()
    def F2(self, u):
        p = self.p
        @pl.when(p.mid)
        def _():
            self.kg(u, p.fh, 'gB', p.far, 1).wait_recv()
            self.kg(u, p.fh, 'gA', p.near, 1).start()
            self.k6(u, p.fh).start()
    def F3(self, u):
        p = self.p
        @pl.when(p.end)
        def _():
            self.kg(u, p.fh, 'gA', p.near, 1).wait_recv()
            self.k6(u, p.fh).start()
    def G(self, u):
        for h in (0, 1): self.k6(u, h).wait()
        self.k7(u).start()
    def H(self, u):
        p = self.p
        self.k7(u).wait()
        self.kg(u, p.bh, 'gA', p.near, 0).wait_send()
        @pl.when(p.mid)
        def _(): self.kg(u, p.fh, 'gA', p.near, 1).wait_send()
    def step(self, t, skip=('P',), lo=None, hi=None):
        for st in STG:
            if st in skip: continue
            u = t - self.off[st]
            f = getattr(self, st)
            pl.when((u >= 0) & (u < self.n))(lambda f=f, u=u: f(u))


epsilon = 1e-06
masked_value = -1e30


def rms_parts(values, gain):
    scale = lax.rsqrt(jnp.mean(values * values, axis=-1, keepdims=True) + epsilon)
    return (values * scale * gain, scale)


def rms_back(grad_normed, values, scale, gain):
    grad_gain = jnp.sum(grad_normed * values * scale, axis=0)
    scaled = grad_normed * gain
    average = jnp.mean(scaled * values, axis=-1, keepdims=True)
    return (scale * scaled - values * scale * scale * scale * average, grad_gain)


def project(left, right):
    return jnp.dot(left, right, preferred_element_type=jnp.float32)


def contract_rows(left, right):
    return lax.dot_general(
        left, right, (((0,), (0,)), ((), ())), preferred_element_type=jnp.float32
    )


def contract_cols(left, right):
    return lax.dot_general(
        left, right, (((1,), (1,)), ((), ())), preferred_element_type=jnp.float32
    )


def flat_buffer(members):
    joined = jnp.concatenate([member.reshape(-1) for member in members])
    return joined


def split_buffer(joined, members):
    pieces = []
    position = 0
    for member in members:
        pieces.append(joined[position : position + member.size].reshape(member.shape))
        position = position + member.size
    return tuple(pieces)


def reduce_ffn(members):
    buffer = flat_buffer(members)
    shares = lax.psum_scatter(buffer, ("dp", "replica"), scatter_dimension=0, tiled=True)
    joined = lax.all_gather(shares, ("dp", "replica"), axis=0, tiled=True)
    return split_buffer(joined, members)


def reduce_attn(members):
    buffer = flat_buffer(members)
    shares = lax.psum_scatter(buffer, ("dp", "replica"), scatter_dimension=0, tiled=True)
    joined = lax.all_gather(shares, ("dp", "replica"), axis=0, tiled=True)
    return split_buffer(joined, members)


def comm_kernel(plan, names, g, out, *refs):
    s = dict(zip(names, refs))
    lsem = refs[-1]
    plan.bind(s, out, lambda u: g.at[u, 1 - plan.p.core])
    plan.entry()

    def load(u):
        return pltpu.make_async_copy(
            g.at[u, plan.p.core], s["W"].at[plan.w(u)], lsem.at[plan.w(u)]
        )

    def one(t, carry):
        @pl.when(t < plan.n)
        def _():
            load(t).start()
            plan.send0(t)
            load(t).wait()

        plan.step(t)
        return carry

    lax.fori_loop(0, plan.steps, one, 0)


def reduce_all(members):
    plan = Comm(24, GAPS)
    scratch = plan.scratch()
    square = lambda m: m.reshape(2, BLK, 2, BLK).transpose(0, 2, 1, 3)
    inner, outer = members[4], members[5]
    wide = inner.reshape(2, BLK, 8, BLK).transpose(2, 0, 1, 3)
    tall = outer.reshape(8, BLK, 2, BLK).transpose(0, 2, 1, 3)
    joined = jnp.concatenate([wide, tall] + [square(m) for m in members[:4]])
    joined = pl.pallas_call(
        functools.partial(comm_kernel, plan, list(scratch)),
        out_shape=jax.ShapeDtypeStruct(joined.shape, jnp.float32),
        in_specs=[pl.BlockSpec(memory_space=pl.ANY)],
        out_specs=pl.BlockSpec(memory_space=pl.ANY),
        scratch_shapes=list(scratch.values()) + [pltpu.SemaphoreType.DMA((plan.NW,))],
        compiler_params=pltpu.CompilerParams(
            collective_id=0, has_side_effects=True, vmem_limit_bytes=56 * 2**20
        ),
    )(joined)
    wide = joined[:8].transpose(1, 2, 0, 3).reshape(inner.shape)
    tall = joined[8:16].transpose(0, 2, 1, 3).reshape(outer.shape)
    unsquare = lambda k: joined[k : k + 2].transpose(0, 2, 1, 3).reshape(2 * BLK, 2 * BLK)
    return tuple(unsquare(16 + 2 * k) for k in range(4)) + (wide, tall)


def block_scores(
    query_block,
    block_start,
    keys_row,
    segment_block,
    segment_row,
    slot_question,
    bias_table,
    offsets,
):
    block_rows = query_block.shape[0]
    row_length = segment_row.shape[0]
    head_count = bias_table.shape[1]
    center = (offsets.shape[0] - 1) // 2
    query_heads = query_block.reshape(block_rows, head_count, -1)
    key_heads = keys_row.reshape(keys_row.shape[0], head_count, -1)
    scores = jnp.einsum("qhd,khd->hqk", query_heads, key_heads, preferred_element_type=jnp.float32)
    query_pos = block_start + lax.iota(jnp.int32, block_rows)
    key_pos = lax.iota(jnp.int32, row_length)
    bucket = offsets[key_pos[None, :] - query_pos[:, None] + center]
    length = offsets.shape[0]
    flat = jnp.tile(bias_table[offsets].T, (1, block_rows + 1))
    flat = flat[:, center : center + block_rows * (length - 1)]
    bias = flat.reshape(head_count, block_rows, length - 1)[:, :, :row_length]
    scores = jnp.concatenate([scores[:, :, :row_length] + bias, scores[:, :, row_length:]], axis=2)
    allowed = jnp.concatenate(
        [
            segment_block[:, None] == segment_row[None, :],
            segment_block[:, None] == slot_question[None, :],
        ],
        axis=1,
    )
    return (jnp.where(allowed[None], scores, masked_value), bucket)


def attend_row(query_row, keys_row, values_row, segment_row, slot_question, bias_table, offsets):
    row_length = query_row.shape[0]
    head_count = bias_table.shape[1]
    block_rows = min(512, row_length)
    value_heads = values_row.reshape(values_row.shape[0], head_count, -1)

    def one_block(block_index):
        block_start = block_index * block_rows
        scores, bucket = block_scores(
            query_row,
            block_start,
            keys_row,
            segment_row,
            segment_row,
            slot_question,
            bias_table,
            offsets,
        )
        row_top = jnp.max(scores, axis=2, keepdims=True)
        row_total = jnp.sum(jnp.exp(scores - row_top), axis=2, keepdims=True)
        log_total = row_top + jnp.log(row_total)
        soft = jnp.exp(scores - log_total).astype(jnp.bfloat16)
        mixed_rows = jnp.einsum(
            "hqk,khd->qhd", soft, value_heads, preferred_element_type=jnp.float32
        )
        return (mixed_rows.reshape(block_rows, -1).astype(jnp.bfloat16), log_total[:, :, 0])

    mixed_rows, log_totals = lax.map(one_block, lax.iota(jnp.int32, row_length // block_rows))
    return (mixed_rows.reshape(row_length, -1), log_totals)


def attend_back(
    query_row,
    keys_row,
    values_row,
    segment_row,
    slot_question,
    bias_table,
    offsets,
    log_totals,
    grad_row,
):
    row_length, head_width = query_row.shape
    head_count = bias_table.shape[1]
    key_count = keys_row.shape[0]
    block_rows = min(512, row_length)
    key_heads = keys_row.reshape(key_count, head_count, -1)
    value_heads = values_row.reshape(key_count, head_count, -1)
    bucket_ids = lax.iota(jnp.int32, bias_table.shape[0])

    def one_block(carry, block_index):
        grad_keys, grad_values, grad_bias = carry
        block_start = block_index * block_rows
        scores, bucket = block_scores(
            query_row,
            block_start,
            keys_row,
            segment_row,
            segment_row,
            slot_question,
            bias_table,
            offsets,
        )
        soft = jnp.exp(scores - log_totals[block_index][:, :, None])
        grad_block = grad_row.reshape(block_rows, head_count, -1)
        query_heads = query_row.reshape(block_rows, head_count, -1)
        grad_soft = jnp.einsum(
            "qhd,khd->hqk", grad_block, value_heads, preferred_element_type=jnp.float32
        )
        row_delta = jnp.sum(soft * grad_soft, axis=2, keepdims=True)
        grad_scores = (soft * (grad_soft - row_delta)).astype(jnp.bfloat16)
        grad_query = jnp.einsum(
            "hqk,khd->qhd", grad_scores, key_heads, preferred_element_type=jnp.float32
        )
        grad_keys = grad_keys + jnp.einsum(
            "hqk,qhd->khd", grad_scores, query_heads, preferred_element_type=jnp.float32
        )
        grad_values = grad_values + jnp.einsum(
            "hqk,qhd->khd",
            soft.astype(jnp.bfloat16),
            grad_block,
            preferred_element_type=jnp.float32,
        )
        onehot = (bucket[:, :, None] == bucket_ids[None, None, :]).astype(jnp.bfloat16)
        grad_bias = grad_bias + jnp.einsum(
            "hqk,qkb->bh",
            grad_scores[:, :, :row_length],
            onehot,
            preferred_element_type=jnp.float32,
        )
        return (
            (grad_keys, grad_values, grad_bias),
            grad_query.reshape(block_rows, -1).astype(jnp.bfloat16),
        )

    start_carry = (
        jnp.zeros((key_count, head_count, head_width // head_count), jnp.float32),
        jnp.zeros((key_count, head_count, head_width // head_count), jnp.float32),
        jnp.zeros(bias_table.shape, jnp.float32),
    )
    (grad_keys, grad_values, grad_bias), grad_query = lax.scan(
        one_block, start_carry, lax.iota(jnp.int32, row_length // block_rows)
    )
    return (
        grad_query.reshape(row_length, head_width),
        grad_keys.reshape(key_count, head_width).astype(jnp.bfloat16),
        grad_values.reshape(key_count, head_width).astype(jnp.bfloat16),
        grad_bias,
    )


def local_layer(
    tokens,
    segments,
    picked,
    cotangent,
    offsets,
    memory_bank,
    w_query,
    w_key,
    w_value,
    w_attn_out,
    w_inner,
    w_outer,
    bias_table,
    gain_one,
    gain_two,
):
    row_count, row_length = segments.shape
    model_width = tokens.shape[1]
    slot_count = picked.shape[1] * picked.shape[2] * 2
    slot_question = lax.iota(jnp.int32, slot_count) // (picked.shape[2] * 2)
    inputs = tokens.astype(jnp.float32)
    normed_float, scale_one = rms_parts(inputs, gain_one)
    normed = normed_float.astype(jnp.bfloat16)
    memory = (
        memory_bank[picked.reshape(-1)]
        .reshape(row_count * slot_count, model_width)
        .astype(jnp.float32)
    )
    mem_float, scale_mem = rms_parts(memory, gain_one)
    mem_normed = mem_float.astype(jnp.bfloat16)
    queries = project(normed, w_query).astype(jnp.bfloat16)
    head_width = queries.shape[1]
    key_tokens = project(normed, w_key).astype(jnp.bfloat16)
    value_tokens = project(normed, w_value).astype(jnp.bfloat16)
    key_memory = project(mem_normed, w_key).astype(jnp.bfloat16)
    value_memory = project(mem_normed, w_value).astype(jnp.bfloat16)
    keys_all = jnp.concatenate(
        [
            key_tokens.reshape(row_count, row_length, head_width),
            key_memory.reshape(row_count, slot_count, head_width),
        ],
        axis=1,
    )
    values_all = jnp.concatenate(
        [
            value_tokens.reshape(row_count, row_length, head_width),
            value_memory.reshape(row_count, slot_count, head_width),
        ],
        axis=1,
    )
    query_rows = queries.reshape(row_count, row_length, head_width)

    def forward_row(query_row, keys_row, values_row, segment_row):
        return attend_row(
            query_row, keys_row, values_row, segment_row, slot_question, bias_table, offsets
        )

    mixed_rows, log_totals = jax.vmap(forward_row)(query_rows, keys_all, values_all, segments)
    attended = mixed_rows.reshape(row_count * row_length, head_width)
    hidden_one = inputs + project(attended, w_attn_out)
    normed_two_float, scale_two = rms_parts(hidden_one, gain_two)
    normed_two = normed_two_float.astype(jnp.bfloat16)
    inner_pre = project(normed_two, w_inner)
    activated_float, gelu_back = jax.vjp(jax.nn.gelu, inner_pre)
    activated = activated_float.astype(jnp.bfloat16)
    output = (hidden_one + project(activated, w_outer)).astype(jnp.bfloat16)
    grad_w_outer = contract_rows(activated, cotangent)
    grad_activated = contract_cols(cotangent, w_outer)
    grad_inner = gelu_back(grad_activated)[0].astype(jnp.bfloat16)
    grad_w_inner = contract_rows(normed_two, grad_inner)
    grad_normed_two = contract_cols(grad_inner, w_inner)
    hidden_back, grad_gain_two = rms_back(grad_normed_two, hidden_one, scale_two, gain_two)
    grad_hidden = cotangent.astype(jnp.float32) + hidden_back
    grad_branch = grad_hidden.astype(jnp.bfloat16)
    grad_w_attn_out = contract_rows(attended, grad_branch)
    grad_attended = contract_cols(grad_branch, w_attn_out).astype(jnp.bfloat16)

    def backward_row(query_row, keys_row, values_row, segment_row, log_row, grad_row):
        return attend_back(
            query_row,
            keys_row,
            values_row,
            segment_row,
            slot_question,
            bias_table,
            offsets,
            log_row,
            grad_row,
        )

    grad_queries, grad_keys, grad_values, grad_bias = jax.vmap(backward_row)(
        query_rows,
        keys_all,
        values_all,
        segments,
        log_totals,
        grad_attended.reshape(row_count, row_length, head_width),
    )
    grad_queries = grad_queries.reshape(row_count * row_length, head_width)
    grad_key_tokens = grad_keys[:, :row_length].reshape(row_count * row_length, head_width)
    grad_key_memory = grad_keys[:, row_length:].reshape(row_count * slot_count, head_width)
    grad_value_tokens = grad_values[:, :row_length].reshape(row_count * row_length, head_width)
    grad_value_memory = grad_values[:, row_length:].reshape(row_count * slot_count, head_width)
    grad_w_query = contract_rows(normed, grad_queries)
    grad_w_key = contract_rows(normed, grad_key_tokens) + contract_rows(mem_normed, grad_key_memory)
    grad_w_value = contract_rows(normed, grad_value_tokens) + contract_rows(
        mem_normed, grad_value_memory
    )
    grad_normed = (
        contract_cols(grad_queries, w_query)
        + contract_cols(grad_key_tokens, w_key)
        + contract_cols(grad_value_tokens, w_value)
    )
    grad_mem_normed = contract_cols(grad_key_memory, w_key) + contract_cols(
        grad_value_memory, w_value
    )
    input_back, gain_from_tokens = rms_back(grad_normed, inputs, scale_one, gain_one)
    gain_from_memory = jnp.sum(grad_mem_normed * memory * scale_mem, axis=0)
    grad_tokens = (grad_hidden + input_back).astype(jnp.bfloat16)
    grads = (
        grad_w_query,
        grad_w_key,
        grad_w_value,
        grad_w_attn_out,
        grad_w_inner,
        grad_w_outer,
        jnp.sum(grad_bias, axis=0),
        gain_from_tokens + gain_from_memory,
        grad_gain_two,
    )
    return (output, grad_tokens, grads)


def body(
    groups,
    tokens,
    segments,
    picked,
    offsets,
    memory_bank,
    side_tokens,
    side_segments,
    w_query,
    w_key,
    w_value,
    w_attn_out,
    w_inner,
    w_outer,
    bias_table,
    gain_one,
    gain_two,
    cotangent,
    side_cotangent,
):
    weights = (
        w_query,
        w_key,
        w_value,
        w_attn_out,
        w_inner,
        w_outer,
        bias_table,
        gain_one,
        gain_two,
    )
    no_memory = jnp.zeros((side_segments.shape[0], 0, picked.shape[2]), jnp.int32)
    side_output, grad_side_tokens, side_grads = local_layer(
        side_tokens, side_segments, no_memory, side_cotangent, offsets, memory_bank, *weights
    )
    output, grad_tokens, main_grads = local_layer(
        tokens, segments, picked, cotangent, offsets, memory_bank, *weights
    )
    summed = tuple((first + second for first, second in zip(main_grads, side_grads)))
    if groups == (4, 8):
        grad_w_query, grad_w_key, grad_w_value, grad_w_attn_out, grad_w_inner, grad_w_outer = (
            reduce_all(summed[:6])
        )
    else:
        grad_w_inner, grad_w_outer = reduce_ffn((summed[4], summed[5]))
        grad_w_query, grad_w_key, grad_w_value, grad_w_attn_out = reduce_attn(
            (summed[0], summed[1], summed[2], summed[3])
        )
    grad_bias_table, grad_gain_one, grad_gain_two = lax.psum(
        (summed[6], summed[7], summed[8]), ("dp", "replica")
    )
    return (
        output,
        grad_tokens,
        side_output,
        grad_side_tokens,
        grad_w_query,
        grad_w_key,
        grad_w_value,
        grad_w_attn_out,
        grad_w_inner,
        grad_w_outer,
        grad_bias_table,
        grad_gain_one,
        grad_gain_two,
    )


def solution(mesh):
    in_specs = (
        P(("dp", "replica"), None),
        P(("dp", "replica"), None),
        P(("dp", "replica"), None, None),
        P(),
        P(),
        P(("dp", "replica"), None),
        P(("dp", "replica"), None),
        P(),
        P(),
        P(),
        P(),
        P(),
        P(),
        P(),
        P(),
        P(),
        P(("dp", "replica"), None),
        P(("dp", "replica"), None),
    )
    out_specs = (
        P(("dp", "replica"), None),
        P(("dp", "replica"), None),
        P(("dp", "replica"), None),
        P(("dp", "replica"), None),
        P(),
        P(),
        P(),
        P(),
        P(),
        P(),
        P(),
        P(),
        P(),
    )
    one = functools.partial(body, (mesh.shape['dp'], mesh.shape['replica']))
    return jax.shard_map(one, mesh=mesh, in_specs=in_specs, out_specs=out_specs, check_vma=False)
```

```python
import functools
from types import SimpleNamespace

import jax
import jax.numpy as jnp
from jax import lax
from jax.experimental import pallas as pl
from jax.experimental.pallas import tpu as pltpu
from jax.sharding import PartitionSpec as P

MESH = pl.DeviceIdType.MESH
epsilon = 1e-06
masked_value = -1e30
AXES = ("dp", "replica")

BLK = 384
STG = ["P", "A", "B", "C1", "C2", "C3", "E", "F1", "F2", "F3", "G", "H"]
GAPS = (1, 3, 1, 1, 2, 3, 2, 1, 2, 3, 1)
KEEP = 3
def offsets_of(gaps):
    o, a = {}, 0
    for s, g in zip(STG, (0,)+tuple(gaps)):
        a += g; o[s] = a
    return o

class Place:
    def __init__(self):
        dp = lax.axis_index("dp"); rep = lax.axis_index("replica")
        self.core = lax.rem(dp, 2); x = dp // 2; z = rep // 2; y = lax.rem(rep, 2)
        c = self.core
        self.partner = (dp + 1 - 2 * c, rep)
        xn = (dp + 2 - 4 * x, rep); yn = (dp, rep + 1 - 2 * y)
        pick = lambda a, b: tuple(jnp.where(c == 0, i, j) for i, j in zip(a, b))
        self.xn = xn; self.yn = yn
        self.n1 = pick(xn, yn); self.n2 = pick(yn, xn)
        self.b1 = jnp.where(c == 0, x, y); self.b2 = jnp.where(c == 0, y, x)
        self.end = (z == 0) | (z == 3)
        self.mid = (z == 1) | (z == 2)
        left = jnp.where(z < 2, 1, 0)
        near = z + 1 - 2 * lax.rem(z, 2)
        far = 3 - z
        self.near = (dp, near * 2 + y)
        self.far = (dp, far * 2 + y)
        self.fh = left
        self.bh = 1 - left

class Comm:
    NP = 4; N0 = 4; N1 = 8; NZ = 6; N3 = 6
    def __init__(self, units, gaps, first=0, pause=0):
        self.n = units; self.off = offsets_of(gaps)
        self.off["K"] = self.off["E"] + KEEP
        self.NW = self.off["K"] + 1
        self.first = first; self.pause = pause
        self.steps = units + pause + self.off['H']
    def scratch(self):
        n = self.n; D = pltpu.SemaphoreType.DMA; V = lambda *s: pltpu.VMEM(s, jnp.float32)
        return dict(
            W=V(self.NW, BLK, BLK), L0=V(self.N0, BLK, BLK), L1=V(self.N1, BLK//2, BLK),
            LA=V(self.NZ, BLK//4, BLK), LB=V(self.NZ, BLK//4, BLK), L3=V(self.N3, BLK//4, BLK),
            s0=D((self.N0,)), r0=D((self.N0,)), s1=D((self.NW,)), r1=D((self.N1,)),
            sz=D((self.NW, 2)), rA=D((self.NZ,)), rB=D((self.NZ,)), s3=D((self.NW,)), r3=D((self.N3,)),
            lo=D((self.NW,)), sg=D((n, 2)), gA=D((n,)), gB=D((n,)), s6=D((n, 2)), r6=D((n, 2)), s7=D((n,)), r7=D((n,)),
            c0=pltpu.SemaphoreType.REGULAR, c1=pltpu.SemaphoreType.REGULAR,
            cA=pltpu.SemaphoreType.REGULAR, cB=pltpu.SemaphoreType.REGULAR, c3=pltpu.SemaphoreType.REGULAR)
    def bind(self, s, out, src0):
        self.s = s; self.out = out; self.src0 = src0; self.p = Place()
    def entry(self):
        p = self.p; b = pltpu.get_barrier_semaphore()
        for d in (p.partner, p.xn, p.yn, p.near, p.far):
            pl.semaphore_signal(b, inc=1, device_id=d, device_id_type=MESH)
        pl.semaphore_wait(b, 5)
    def rc(self, src, dst, ss, rs, dev):
        return pltpu.make_async_remote_copy(src_ref=src, dst_ref=dst, send_sem=ss, recv_sem=rs, device_id=dev, device_id_type=MESH)
    def k0(self, u):
        s = self.s; i = lax.rem(u, self.N0)
        return self.rc(self.src0(u), s.L0.at[i], s.s0.at[i], s.r0.at[i], self.p.partner)
    def w(self, u): return lax.rem(u, self.NW)
    def k1(self, u):
        s = self.s; w = self.w(u); i = lax.rem(u, self.N1)
        return self.rc(s.W.at[w, pl.ds((1 - self.p.b1) * 192, 192)], s.L1.at[i], s.s1.at[w], s.r1.at[i], self.p.n1)
    def zrow(self, h): return self.p.b1 * 192 + h * 96
    def kz(self, u, h, L, r, dev, j):
        s = self.s; w = self.w(u); i = lax.rem(u, self.NZ)
        return self.rc(s.W.at[w, pl.ds(self.zrow(h), 96)], getattr(s, L).at[i], s.sz.at[w, j], getattr(s, r).at[i], dev)
    def k3(self, u):
        s = self.s; w = self.w(u); i = lax.rem(u, self.N3)
        return self.rc(self.held(u), s.L3.at[i], s.s3.at[w], s.r3.at[i], self.p.n2)
    def held(self, u): return self.s.W.at[self.w(u), pl.ds(self.zrow(self.p.bh), 96)]
    def kl(self, u):
        return pltpu.make_async_copy(self.held(u), self.piece(u, self.p.bh), self.s.lo.at[self.w(u)])
    def piece(self, u, h): return self.out.at[u, self.p.core, pl.ds(self.zrow(h), 96)]
    def kg(self, u, h, r, dev, j, src=None):
        s = self.s
        return self.rc(self.piece(u, h) if src is None else src, self.piece(u, h), s.sg.at[u, j], getattr(s, r).at[u], dev)
    def k6(self, u, h, src=None):
        s = self.s
        return self.rc(self.piece(u, h) if src is None else src, self.piece(u, h), s.s6.at[u, h], s.r6.at[u, h], self.p.n1)
    def k7(self, u):
        s = self.s; o = self.out.at[u, self.p.core]
        return self.rc(o, o, s.s7.at[u], s.r7.at[u], self.p.partner)
    def give(self, name, u, N, dev):
        @pl.when(u + N < self.n)
        def _(): pl.semaphore_signal(getattr(self.s, name), inc=1, device_id=dev, device_id_type=MESH)
    def take(self, name, u, N):
        @pl.when(u >= N)
        def _(): pl.semaphore_wait(getattr(self.s, name), 1)
    def send0(self, u):
        self.take('c0', u, self.N0)
        self.k0(u).start()
    def A(self, u):
        s = self.s; p = self.p; w = self.w(u); i = lax.rem(u, self.N0)
        self.k0(u).wait()
        s.W[w] = s.W[w] + s.L0[i]
        self.give('c0', u, self.N0, p.partner)
        self.take('c1', u, self.N1)
        self.k1(u).start()
    def B(self, u):
        s = self.s; p = self.p; w = self.w(u); i = lax.rem(u, self.N1)
        self.k1(u).wait_recv()
        rows = pl.ds(p.b1 * 192, 192)
        s.W[w, rows] = s.W[w, rows] + s.L1[i]
        self.give('c1', u, self.N1, p.n1)
        @pl.when(p.end)
        def _():
            self.take('cA', u, self.NZ)
            self.kz(u, p.fh, 'LA', 'rA', p.near, 0).start()
    def zadd(self, u, h, L, r):
        s = self.s; w = self.w(u); i = lax.rem(u, self.NZ)
        self.kz(u, h, L, r, self.p.near, 0).wait_recv()
        rows = pl.ds(self.zrow(h), 96)
        s.W[w, rows] = s.W[w, rows] + getattr(s, L)[i]
    def C1(self, u):
        p = self.p
        @pl.when(p.mid)
        def _():
            self.zadd(u, p.fh, 'LA', 'rA')
            self.give('cA', u, self.NZ, p.near)
            self.take('cB', u, self.NZ)
            self.kz(u, p.fh, 'LB', 'rB', p.far, 0).start()
    def C2(self, u):
        p = self.p
        @pl.when(p.mid)
        def _():
            self.zadd(u, p.bh, 'LB', 'rB')
            self.give('cB', u, self.NZ, p.far)
            self.take('cA', u, self.NZ)
            self.kz(u, p.bh, 'LA', 'rA', p.near, 1).start()
    def C3(self, u):
        p = self.p
        @pl.when(p.end)
        def _():
            self.zadd(u, p.bh, 'LA', 'rA')
            self.give('cA', u, self.NZ, p.near)
            self.take('c3', u, self.N3)
            self.k3(u).start()
    def E(self, u):
        s = self.s; p = self.p; w = self.w(u); i = lax.rem(u, self.N3)
        @pl.when(p.end)
        def _():
            self.k3(u).wait()
            rows = pl.ds(self.zrow(p.bh), 96)
            s.W[w, rows] = s.W[w, rows] + s.L3[i]
            self.give('c3', u, self.N3, p.n2)
            self.kg(u, p.bh, 'gA', p.near, 0, self.held(u)).start()
            self.k6(u, p.bh, self.held(u)).start()
            self.kl(u).start()
    def K(self, u):
        p = self.p
        self.k1(u).wait_send()
        self.kz(u, p.fh, 'LB', 'rB', p.far, 0).wait_send()
        @pl.when(p.mid)
        def _(): self.kz(u, p.bh, 'LA', 'rA', p.near, 1).wait_send()
        @pl.when(p.end)
        def _():
            self.kl(u).wait()
            self.kg(u, p.bh, 'gA', p.near, 0, self.held(u)).wait_send()
            self.k6(u, p.bh, self.held(u)).wait_send()
    def F1(self, u):
        p = self.p
        @pl.when(p.mid)
        def _():
            self.kg(u, p.bh, 'gA', p.near, 0).wait_recv()
            self.kg(u, p.bh, 'gB', p.far, 0).start()
            self.k6(u, p.bh).start()
    def F2(self, u):
        p = self.p
        @pl.when(p.mid)
        def _():
            self.kg(u, p.fh, 'gB', p.far, 1).wait_recv()
            self.kg(u, p.fh, 'gA', p.near, 1).start()
            self.k6(u, p.fh).start()
    def F3(self, u):
        p = self.p
        @pl.when(p.end)
        def _():
            self.kg(u, p.fh, 'gA', p.near, 1).wait_recv()
            self.k6(u, p.fh).start()
    def G(self, u):
        for h in (0, 1): self.k6(u, h).wait_recv()
        self.k7(u).start()
    def H(self, u):
        p = self.p
        self.k7(u).wait()
        self.k6(u, p.fh).wait_send()
        @pl.when(p.mid)
        def _():
            self.k6(u, p.bh).wait_send()
            self.kg(u, p.bh, 'gB', p.far, 0).wait_send()
            self.kg(u, p.fh, 'gA', p.near, 1).wait_send()
    def step(self, t):
        for st in STG[1:] + ["K"]:
            at = t - self.off[st]
            late = at >= self.first + self.pause
            u = jnp.where(late, at - self.pause, at)
            f = getattr(self, st)
            live = (at >= 0) & ((at < self.first) | late) & (u < self.n)
            pl.when(live)(lambda f=f, u=u: f(u))


def spread(values, gain):
    scale = lax.rsqrt(jnp.mean(values * values, axis=-1, keepdims=True) + epsilon)
    return values * scale * gain, scale


def dot_nn(a, b):
    return jnp.dot(a, b, preferred_element_type=jnp.float32)


def dot_nt(a, b):
    return lax.dot_general(a, b, (((1,), (1,)), ((), ())), preferred_element_type=jnp.float32)


def dot_tn(a, b):
    return lax.dot_general(a, b, (((0,), (0,)), ((), ())), preferred_element_type=jnp.float32)


def exact(a, b, dims):
    return lax.dot_general(
        a, b, (dims, ((), ())), precision=lax.Precision.HIGHEST,
        preferred_element_type=jnp.float32,
    )


class Layer:
    def __init__(self, plan, sizes):
        self.plan = plan
        self.z = sizes

    def scratch(self):
        z = self.z
        n, mem, d, ff = z.n, z.mem, z.d, z.ff
        all_rows = n + mem
        b16 = lambda *s: pltpu.VMEM(s, jnp.bfloat16)
        f32 = lambda *s: pltpu.VMEM(s, jnp.float32)
        L = z.L
        pairs = z.heads // 2
        DMA = pltpu.SemaphoreType.DMA
        own = dict(
            xb=b16(n, d), cb=b16(n, d), bk=b16(z.bank, 2, d),
            wq=b16(d, d), wk=b16(d, d), wv=b16(d, d), wo=b16(d, d),
            wib=b16(2, d, d), wub=b16(2, d, d),
            nall=b16(all_rows, d), qs=b16(n, d), ks=b16(all_rows, d), vs=b16(all_rows, d),
            att=b16(n, d), hid=f32(n, d), n2=b16(n, d), n2T=b16(d, n),
            oacc=f32(n, d), gacc=f32(n, d),
            act=b16(n, d), gib=b16(n, d),
            bias=f32(pairs, 2 * L, L), lse=f32(z.rows, 2 * L, 128),
            MT=f32(2 * L, L), MM=f32(2 * L, z.slots),
            dB=f32(pairs, 2 * L, L), dq=b16(n, d),
            seg=pltpu.VMEM((8, L), jnp.int32),
            sm=f32(16, d), lines=f32(16, 2 * L),
            isem=DMA((16,)), wsem=DMA((2, 2)), osem=DMA((6,)),
        )
        if self.plan is not None:
            own.update(self.plan.scratch())
            own.update(P=f32(self.plan.NP, BLK, BLK), L5=f32(5, 16, d), s5=DMA((5,)), r5=DMA((5,)))
        else:
            own.update(W=f32(2, BLK, BLK), P=f32(2, BLK, BLK), esem=DMA((2,)))
        return own

    def slots(self, u):
        if self.plan is None:
            return lax.rem(u, 2), lax.rem(u, 2)
        return self.plan.w(u), lax.rem(u, self.plan.NP)

    def emit(self, u):
        s = self.s
        if self.plan is not None:
            self.plan.send0(u)
            return
        w, p = self.slots(u)
        one = pltpu.make_async_copy(s.W.at[w], self.out.at[u, 0], s.esem.at[0])
        two = pltpu.make_async_copy(s.P.at[p], self.out.at[u, 1], s.esem.at[1])
        one.start()
        two.start()
        one.wait()
        two.wait()

    def emit_cols(self, u, value):
        s = self.s
        w, p = self.slots(u)

        @pl.when(self.core == 0)
        def _():
            s.W[w] = value[:, :BLK]
            s.P[p] = value[:, BLK:]

        @pl.when(self.core != 0)
        def _():
            s.W[w] = value[:, BLK:]
            s.P[p] = value[:, :BLK]

        self.emit(u)

    def step(self, t):
        if self.plan is not None:
            self.plan.step(t)

    def kernel(self, names, *refs):
        z = self.z
        ins = SimpleNamespace(**dict(zip(INS, refs)))
        outs = SimpleNamespace(**dict(zip(OUTS, refs[18:])))
        s = SimpleNamespace(**dict(zip(names, refs[24:])))
        s.gb, s.dk, s.dv = s.wub.at[0], s.wib.at[0], s.wib.at[1]
        s.dkm, s.dvm = s.wub.at[1, pl.ds(0, z.mem)], s.wub.at[1, pl.ds(z.mem, z.mem)]
        self.s, self.ins, self.outs, self.out = s, ins, outs, outs.out
        if self.plan is not None:
            self.plan.bind(s, outs.out, lambda u: s.P.at[lax.rem(u, self.plan.NP)])
            self.core = self.plan.p.core
        else:
            self.core = jnp.int32(0)
        self.load()
        if self.plan is not None:
            self.plan.entry()
        self.front()
        self.ffn()
        self.middle()
        self.attn_back()
        self.back()

    def load(self):
        s, i, z = self.s, self.ins, self.z
        n0 = z.n0
        cp = pltpu.make_async_copy
        sem = lambda k: s.isem.at[k]
        d = z.d
        self.c = SimpleNamespace(
            x0=cp(i.tok, s.xb.at[pl.ds(0, n0)], sem(0)),
            x1=cp(i.side, s.xb.at[pl.ds(n0, z.n - n0)], sem(1)),
            bk=cp(i.bank, s.bk, sem(2)),
            wq=cp(i.wq, s.wq, sem(3)), wk=cp(i.wk, s.wk, sem(4)),
            wv=cp(i.wv, s.wv, sem(5)), wo=cp(i.wo, s.wo, sem(6)),
            c0=cp(i.cot, s.cb.at[pl.ds(0, n0)], sem(7)),
            c1=cp(i.scot, s.cb.at[pl.ds(n0, z.n - n0)], sem(8)),
        )
        for k in ("x0", "x1", "bk", "wq", "wk", "wv", "wo"):
            getattr(self.c, k).start()
        for k in self.wcopy(0):
            k.start()
        self.c.c0.start()
        self.c.c1.start()

    def wcopy(self, c):
        s, i, d = self.s, self.ins, self.z.d
        slot = lax.rem(c, 2) if not isinstance(c, int) else c % 2
        cols = pl.ds(c * d if isinstance(c, int) else pl.multiple_of(c * d, d), d)
        return (
            pltpu.make_async_copy(i.wi.at[:, cols], s.wib.at[slot], s.wsem.at[slot, 0]),
            pltpu.make_async_copy(i.wu.at[cols, :], s.wub.at[slot], s.wsem.at[slot, 1]),
        )

    def tile(self, k):
        return pl.ds(pl.multiple_of(k * 256, 256), 256)

    def memory(self):
        s, z = self.s, self.z
        entries = lax.broadcasted_iota(jnp.int32, (z.mem // 2, z.bank), 1)
        hot = jnp.where(entries == self.ins.idx[...], 1.0, 0.0).astype(jnp.bfloat16)
        return tuple(dot_nn(hot, s.bk[:, part, :]) for part in range(2))

    def mem_rows(self, r, part):
        z = self.z
        return pl.ds(z.n + r * z.slots + part * (z.slots // 2), z.slots // 2)

    def heads(self, value):
        lane = lax.broadcasted_iota(jnp.int32, (1, 128), 1)
        first = jnp.where(lane < 64, 1.0, 0.0).astype(jnp.bfloat16)
        second = jnp.where(lane < 64, 0.0, 1.0).astype(jnp.bfloat16)
        return jnp.concatenate([value * first, value * second], axis=0)

    def merge(self, value):
        rows = value.shape[0] // 2
        lane = lax.broadcasted_iota(jnp.int32, (rows, 128), 1)
        return jnp.where(lane < 64, value[:rows], value[rows:])

    def masks(self, r, has_mem):
        s, z = self.s, self.z
        L = z.L
        row = s.seg[pl.ds(r, 1), :].astype(jnp.float32)
        across = jnp.broadcast_to(row, (L, L))
        down = across.T
        mask = jnp.where(across == down, 0.0, masked_value)
        s.MT[pl.ds(0, L), :] = mask
        s.MT[pl.ds(L, L), :] = mask
        if has_mem:
            slots = z.slots
            lane = lax.broadcasted_iota(jnp.int32, (L, slots), 1)
            question = jnp.zeros((L, slots), jnp.float32)
            lane = jnp.where(lane >= slots // 2, lane - slots // 2, lane)
            for q in range(1, z.questions):
                question = question + jnp.where(lane >= q * (slots // 2 // z.questions), 1.0, 0.0)
            mask = jnp.where(down[:, :slots] == question, 0.0, masked_value)
            s.MM[pl.ds(0, L), :] = mask
            s.MM[pl.ds(L, L), :] = mask

    def spans(self, r, j):
        z = self.z
        rows = pl.ds(pl.multiple_of(r * z.L, z.L), z.L)
        mem = pl.ds(pl.multiple_of(z.n + r * z.slots, 32), z.slots)
        lanes = pl.ds(pl.multiple_of(j * 128, 128), 128)
        return rows, mem, lanes

    def scores(self, r, j, has_mem):
        s = self.s
        rows, mem, lanes = self.spans(r, j)
        q2 = self.heads(s.qs[rows, lanes])
        st = dot_nt(q2, s.ks[rows, lanes]) + s.bias[j] + s.MT[...]
        sm = dot_nt(q2, s.ks[mem, lanes]) + s.MM[...] if has_mem else None
        return q2, st, sm

    def fwd_pair(self, r, j, has_mem):
        s, z = self.s, self.z
        rows, mem, lanes = self.spans(r, j)
        q2, st, sm = self.scores(r, j, has_mem)
        top = jnp.max(st, axis=1, keepdims=True)
        if has_mem:
            top = jnp.maximum(top, jnp.max(sm, axis=1, keepdims=True))
        et = jnp.exp(st - top)
        total = jnp.sum(et, axis=1, keepdims=True)
        if has_mem:
            em = jnp.exp(sm - top)
            total = total + jnp.sum(em, axis=1, keepdims=True)
        inv = 1.0 / total
        mixed = dot_nn(et.astype(jnp.bfloat16), s.vs[rows, lanes])
        if has_mem:
            mixed = mixed + dot_nn(em.astype(jnp.bfloat16), s.vs[mem, lanes])
        s.att[rows, lanes] = self.merge(mixed * inv).astype(jnp.bfloat16)
        lane = lax.broadcasted_iota(jnp.int32, (2 * z.L, 128), 1)
        s.lse[r] = jnp.where(lane == j, top + jnp.log(total), s.lse[r])

    def front(self):
        s, z, i = self.s, self.z, self.ins
        L, d, n = z.L, z.d, z.n
        offs = i.offs[...]
        spots = offs.shape[1]
        bucket = lax.broadcasted_iota(jnp.int32, (i.btab.shape[1], spots), 0)
        hot = jnp.where(bucket == offs, 1.0, 0.0)
        line = exact(i.btab[...], hot, ((1,), (0,)))
        line = jnp.concatenate([line, jnp.zeros((line.shape[0], 2 * L - spots), jnp.float32)], 1)
        for h in range(z.heads):
            wide = jnp.broadcast_to(line[h : h + 1], (L, 2 * L))
            turned = pltpu.roll(wide, L + 1, 1, stride=1, stride_axis=0)
            s.bias[h // 2, pl.ds((h % 2) * L, L), :] = turned[:, :L]
        s.seg[pl.ds(0, z.main), :] = i.segm[...]
        s.seg[pl.ds(z.main, z.rows - z.main), :] = i.segs[...]
        g1 = i.g1[...].reshape(1, d)
        self.c.x0.wait()
        self.c.x1.wait()

        def norm_row(r, carry):
            rows = pl.ds(pl.multiple_of(r * L, L), L)
            s.nall[rows, :] = spread(s.xb[rows, :].astype(jnp.float32), g1)[0].astype(jnp.bfloat16)
            return carry

        lax.fori_loop(0, z.rows, norm_row, 0)
        self.c.bk.wait()
        half = z.slots // 2
        for part, memory in enumerate(self.memory()):
            normed = spread(memory, g1)[0].astype(jnp.bfloat16)
            for r in range(z.main):
                s.nall[self.mem_rows(r, part), :] = normed[r * half : (r + 1) * half]
        for k in ("wq", "wk", "wv"):
            getattr(self.c, k).wait()

        def project(k, carry):
            cols = self.tile(k)
            s.qs[:, cols] = dot_nn(s.nall[pl.ds(0, n), :], s.wq[:, cols]).astype(jnp.bfloat16)
            s.ks[:, cols] = dot_nn(s.nall[...], s.wk[:, cols]).astype(jnp.bfloat16)
            s.vs[:, cols] = dot_nn(s.nall[...], s.wv[:, cols]).astype(jnp.bfloat16)
            return carry

        lax.fori_loop(0, d // 256, project, 0)
        pairs = z.heads // 2

        def row(has_mem, r, carry):
            self.masks(r, has_mem)

            def pair(j, inner):
                self.fwd_pair(r, j, has_mem)
                return inner

            return lax.fori_loop(0, pairs, pair, carry, unroll=FWD_UNROLL)

        lax.fori_loop(0, z.main, functools.partial(row, True), 0)
        lax.fori_loop(z.main, z.rows, functools.partial(row, False), 0)
        self.c.wo.wait()

        def attn_out(k, carry):
            cols = self.tile(k)
            s.hid[:, cols] = s.xb[:, cols].astype(jnp.float32) + dot_nn(s.att[...], s.wo[:, cols])
            return carry

        lax.fori_loop(0, d // 256, attn_out, 0)
        g2 = i.g2[...].reshape(1, d)

        def norm_two(r, carry):
            rows = pl.ds(pl.multiple_of(r * L, L), L)
            s.n2[rows, :] = spread(s.hid[rows, :], g2)[0].astype(jnp.bfloat16)
            return carry

        lax.fori_loop(0, z.rows, norm_two, 0)

    def ffn(self):
        s, z, i = self.s, self.z, self.ins
        d, n = z.d, z.n
        chunks = z.ff // d
        self.c.c0.wait()
        self.c.c1.wait()
        root = 0.7978845608028654

        def chunk(c, carry):
            slot = lax.rem(c, 2)
            for k in self.wcopy(c):
                k.wait()

            @pl.when(c + 1 < chunks)
            def _():
                for k in self.wcopy(c + 1):
                    k.start()

            def part(k, inner):
                cols = self.tile(k)
                v = dot_nn(s.n2[...], s.wib[slot, :, cols])
                ga = dot_nt(s.cb[...], s.wub[slot, cols, :])
                square = v * v
                th = jnp.tanh(root * v * (1.0 + 0.044715 * square))
                half = 0.5 * (1.0 + th)
                s.act[:, cols] = (v * half).astype(jnp.bfloat16)
                slope = half + (0.5 * root) * v * (1.0 - th * th) * (1.0 + 0.134145 * square)
                s.gib[:, cols] = (ga * slope).astype(jnp.bfloat16)
                return inner

            lax.fori_loop(0, d // 256, part, 0)

            def outer(k, inner):
                u = 4 * c + k
                cols = pl.ds(pl.multiple_of(k * BLK, BLK), BLK)
                self.emit_cols(u, dot_tn(s.act[:, cols], s.cb[...]))
                self.step(u)

                @pl.when(k == 0)
                def _():
                    lax.fori_loop(0, d // 256, gather, 0)

                return inner

            def gather(k, inner):
                cols = self.tile(k)
                po = dot_nn(s.act[...], s.wub[slot, :, cols])
                pg = dot_nt(s.gib[...], s.wib[slot, cols, :])

                @pl.when(c == 0)
                def _():
                    s.oacc[:, cols] = po
                    s.gacc[:, cols] = pg

                @pl.when(c > 0)
                def _():
                    s.oacc[:, cols] = s.oacc[:, cols] + po
                    s.gacc[:, cols] = s.gacc[:, cols] + pg

                return inner

            lax.fori_loop(0, 2, outer, 0)

            @pl.when(c == 0)
            def _():
                s.n2T[...] = s.n2[...].T

            def inner_grad(k, inner):
                self.inner_unit(4 * c + 2 + k, k)
                self.step(4 * c + 2 + k)
                return inner

            @pl.when(c + 1 < chunks)
            def _():
                lax.fori_loop(0, 2, inner_grad, 0)

            return carry

        lax.fori_loop(0, chunks, chunk, 0)

    def inner_unit(self, u, k):
        s = self.s
        w, p = self.slots(u)
        cols = pl.ds(pl.multiple_of(k * BLK, BLK), BLK)
        mine = pl.ds(pl.multiple_of(self.core * BLK, BLK), BLK)
        other = pl.ds(pl.multiple_of((1 - self.core) * BLK, BLK), BLK)
        s.P[p] = dot_nn(s.n2T[other, :], s.gib[:, cols])
        s.W[w] = dot_nn(s.n2T[mine, :], s.gib[:, cols])
        self.emit(u)

    def out_unit(self, u, k):
        s = self.s
        cols = pl.ds(pl.multiple_of(k * BLK, BLK), BLK)
        self.emit_cols(u, dot_tn(s.att[:, cols], s.gb[...]))

    def middle(self):
        s, z, i = self.s, self.z, self.ins
        L, d, n, n0 = z.L, z.d, z.n, z.n0
        g2 = i.g2[...].reshape(1, d)

        def row(r, gain):
            rows = pl.ds(pl.multiple_of(r * L, L), L)
            hid = s.hid[rows, :]
            s.dq[rows, :] = (hid + s.oacc[rows, :]).astype(jnp.bfloat16)
            scale = lax.rsqrt(jnp.mean(hid * hid, axis=-1, keepdims=True) + epsilon)
            grad = s.gacc[rows, :]
            gain = gain + jnp.sum(grad * hid * scale, axis=0, keepdims=True)
            u = grad * g2
            average = jnp.mean(u * hid, axis=-1, keepdims=True)
            full = s.cb[rows, :].astype(jnp.float32) + scale * u - hid * (scale * scale * scale * average)
            s.gacc[rows, :] = full
            s.gb[rows, :] = full.astype(jnp.bfloat16)
            return gain

        gain = lax.fori_loop(0, z.rows, row, jnp.zeros((1, d), jnp.float32))
        s.sm[...] = jnp.zeros((16, d), jnp.float32)
        s.sm[pl.ds(13, 1), :] = gain
        self.o = (
            pltpu.make_async_copy(s.dq.at[pl.ds(0, n0)], self.outs.y, s.osem.at[0]),
            pltpu.make_async_copy(s.dq.at[pl.ds(n0, n - n0)], self.outs.sy, s.osem.at[1]),
        )
        for k in self.o:
            k.start()

        def back(k, carry):
            cols = self.tile(k)
            s.n2[:, cols] = dot_nt(s.gb[...], s.wo[cols, :]).astype(jnp.bfloat16)
            return carry

        lax.fori_loop(0, d // 256, back, 0)
        for k in self.o:
            k.wait()

    def bwd_pair(self, r, j, has_mem):
        s, z = self.s, self.z
        rows, mem, lanes = self.spans(r, j)
        q2, st, sm = self.scores(r, j, has_mem)
        lane = lax.broadcasted_iota(jnp.int32, (2 * z.L, 128), 1)
        lse = jnp.sum(jnp.where(lane == j, s.lse[r], 0.0), axis=1, keepdims=True)
        d2 = self.heads(s.n2[rows, lanes])
        pt = jnp.exp(st - lse)
        gt = dot_nt(d2, s.vs[rows, lanes])
        delta = jnp.sum(pt * gt, axis=1, keepdims=True)
        if has_mem:
            pm = jnp.exp(sm - lse)
            gm = dot_nt(d2, s.vs[mem, lanes])
            delta = delta + jnp.sum(pm * gm, axis=1, keepdims=True)
        dst = (pt * (gt - delta)).astype(jnp.bfloat16)
        grad_q = dot_nn(dst, s.ks[rows, lanes])
        s.dk[rows, lanes] = dot_tn(dst, q2).astype(jnp.bfloat16)
        s.dv[rows, lanes] = dot_tn(pt.astype(jnp.bfloat16), d2).astype(jnp.bfloat16)
        if has_mem:
            dsm = (pm * (gm - delta)).astype(jnp.bfloat16)
            grad_q = grad_q + dot_nn(dsm, s.ks[mem, lanes])
            slot = pl.ds(pl.multiple_of(r * z.slots, 32), z.slots)
            s.dkm[slot, lanes] = dot_tn(dsm, q2).astype(jnp.bfloat16)
            s.dvm[slot, lanes] = dot_tn(pm.astype(jnp.bfloat16), d2).astype(jnp.bfloat16)
        s.dq[rows, lanes] = self.merge(grad_q).astype(jnp.bfloat16)
        s.dB[j] = s.dB[j] + dst.astype(jnp.float32)

    def attn_back(self):
        s, z = self.s, self.z
        pairs = z.heads // 2
        first = 4 * (z.ff // z.d) - 2

        def clear(j, carry):
            s.dB[j] = jnp.zeros(s.dB.shape[1:], jnp.float32)
            return carry

        lax.fori_loop(0, pairs, clear, 0)

        def row(has_mem, r, carry):
            self.masks(r, has_mem)

            def few(g, inner):
                def pair(k, last):
                    self.bwd_pair(r, g * 3 + k, has_mem)
                    return last

                lax.fori_loop(0, 3, pair, 0, unroll=BWD_UNROLL)
                if has_mem:
                    u = first + 2 * r + g

                    @pl.when(r == 0)
                    def _():
                        self.out_unit(u, g)

                    @pl.when(r > 0)
                    def _():
                        self.inner_unit(u, g)

                    self.step(u)
                return inner

            return lax.fori_loop(0, pairs // 3, few, carry)

        lax.fori_loop(0, z.main, functools.partial(row, True), 0)
        lax.fori_loop(z.main, z.rows, functools.partial(row, False), 0)

    def back(self):
        s, z, i = self.s, self.z, self.ins
        L, d, n, n0, mem = z.L, z.d, z.n, z.n0, z.mem
        first = 4 * (z.ff // d) + 2
        tok, mrows = pl.ds(0, n), pl.ds(n, mem)
        def difference(j):
            for side in range(2):
                grid = s.dB[j, pl.ds(side * L, L), :]
                wide = jnp.concatenate([grid, jnp.zeros((L, L), jnp.float32)], axis=1)
                wide = pltpu.roll(wide, L - 1, 1)
                half = L // 2
                while half:
                    wide = wide[:half] + pltpu.roll(wide[half:], 2 * L - half, 1)
                    half = half // 2
                s.lines[pl.ds(2 * j + side, 1), :] = wide

        u = first
        for grad, grad_mem in ((s.dq, None), (s.dk, s.dkm), (s.dv, s.dvm)):
            def one(k, carry, grad=grad, grad_mem=grad_mem, u=u):
                cols = pl.ds(pl.multiple_of(k * BLK, BLK), BLK)
                value = dot_tn(s.nall[tok, cols], grad[...])
                if grad_mem is not None:
                    value = value + dot_tn(s.nall[mrows, cols], grad_mem[...])
                self.emit_cols(u + k, value)
                self.step(u + k)
                difference(u - first + k)
                return carry

            lax.fori_loop(0, 2, one, 0)
            u = u + 2
        t = first + 6
        def grads(k, carry):
            cols = self.tile(k)
            self.step(t + k)
            s.hid[:, cols] = (
                dot_nt(s.dq[...], s.wq[cols, :])
                + dot_nt(s.dk[...], s.wk[cols, :])
                + dot_nt(s.dv[...], s.wv[cols, :])
            )
            s.oacc[pl.ds(0, mem), cols] = dot_nt(s.dkm[...], s.wk[cols, :]) + dot_nt(
                s.dvm[...], s.wv[cols, :]
            )
            return carry

        lax.fori_loop(0, d // 256, grads, 0)
        t = t + d // 256
        g1 = i.g1[...].reshape(1, d)

        def row(r, gain):
            rows = pl.ds(pl.multiple_of(r * L, L), L)
            x = s.xb[rows, :].astype(jnp.float32)
            scale = lax.rsqrt(jnp.mean(x * x, axis=-1, keepdims=True) + epsilon)
            grad = s.hid[rows, :]
            gain = gain + jnp.sum(grad * x * scale, axis=0, keepdims=True)
            v = grad * g1
            average = jnp.mean(v * x, axis=-1, keepdims=True)
            full = s.gacc[rows, :] + scale * v - x * (scale * scale * scale * average)
            s.gb[rows, :] = full.astype(jnp.bfloat16)
            self.step(t + r)
            return gain

        gain = lax.fori_loop(0, z.rows, row, jnp.zeros((1, d), jnp.float32))
        t = t + z.rows
        late = (
            pltpu.make_async_copy(s.gb.at[pl.ds(0, n0)], self.outs.gt, s.osem.at[2]),
            pltpu.make_async_copy(s.gb.at[pl.ds(n0, n - n0)], self.outs.sgt, s.osem.at[3]),
        )
        for k in late:
            k.start()
        half = z.slots // 2
        for part, memory in enumerate(self.memory()):
            scale = lax.rsqrt(jnp.mean(memory * memory, axis=-1, keepdims=True) + epsilon)
            unit = memory * scale
            for r in range(z.main):
                grad = s.oacc[pl.ds(r * z.slots + part * half, half), :]
                gain = gain + jnp.sum(grad * unit[r * half : (r + 1) * half], axis=0, keepdims=True)
        s.sm[pl.ds(12, 1), :] = gain
        offs = i.offs[...]
        bucket = lax.broadcasted_iota(jnp.int32, (128, offs.shape[1]), 0)
        hot = jnp.where(bucket == offs, 1.0, 0.0)
        s.sm[pl.ds(0, z.heads), pl.ds(0, 128)] = exact(
            s.lines[pl.ds(0, z.heads), pl.ds(0, offs.shape[1])], hot, ((1,), (1,))
        )
        if self.plan is not None:
            self.finish(t)
        for k in late:
            k.wait()
        self.outs.small[...] = s.sm[...]

    def steps_from(self, t, count):
        def one(k, carry):
            self.step(k)
            return carry

        lax.fori_loop(t, t + count, one, 0)
        return t + count

    def finish(self, t):
        plan, s = self.plan, self.s
        p = plan.p
        peers = (p.partner, p.xn, p.yn, p.near, p.far)
        for k, dev in enumerate(peers):
            copy = plan.rc(s.sm, s.L5.at[k], s.s5.at[k], s.r5.at[k], dev)
            copy.start()
            t = self.steps_from(t, SMALL_GAP)
            copy.wait()
            s.sm[...] = s.sm[...] + s.L5[k]

        def rest(k, carry):
            self.step(k)
            return carry

        lax.fori_loop(t, plan.steps, rest, 0)


def place_units(
    sizes, units, y, gt, sy, sgt, small,
    oy, ogt, osy, osgt, wq, wk, wv, wo, wi, wu, gb, gg1, gg2,
    hold, vy, vgt, vsy, vsgt, sem, late, rsem,
):
    d, ff = sizes.d, sizes.ff
    copies = []

    def put(u, half, ref, row, col):
        k = len(copies)
        place = ref.at[pl.ds(row, BLK), pl.ds(col, BLK)]
        copies.append(
            (
                pltpu.make_async_copy(units.at[u, half], hold.at[k], sem.at[k]),
                pltpu.make_async_copy(hold.at[k], place, late.at[k]),
            )
        )

    for c in range(ff // d):
        for k in range(2):
            for half in range(2):
                put(4 * c + k, half, wu, c * d + k * BLK, half * BLK)
                after = 2 if c + 1 < ff // d else 4
                put(4 * c + after + k, half, wi, half * BLK, c * d + k * BLK)
    for k in range(2):
        for half in range(2):
            put(4 * (ff // d) - 2 + k, half, wo, k * BLK, half * BLK)
    u = 4 * (ff // d) + 2
    for ref in (wq, wk, wv):
        for k in range(2):
            for half in range(2):
                put(u + k, half, ref, k * BLK, half * BLK)
        u = u + 2
    for k, (src, mid, dst) in enumerate(
        ((y, vy, oy), (gt, vgt, ogt), (sy, vsy, osy), (sgt, vsgt, osgt))
    ):
        copies.append(
            (
                pltpu.make_async_copy(src, mid, rsem.at[k, 0]),
                pltpu.make_async_copy(mid, dst, rsem.at[k, 1]),
            )
        )
    for fetch, store in copies:
        fetch.start()
    heads, buckets = gb.shape
    gb[...] = small[pl.ds(0, heads), pl.ds(0, buckets)]
    gg1[...] = small[12, :]
    gg2[...] = small[13, :]
    for fetch, store in copies:
        fetch.wait()
        store.start()
    for fetch, store in copies:
        store.wait()


def body(
    remote,
    tokens,
    segments,
    picked,
    offsets,
    memory_bank,
    side_tokens,
    side_segments,
    w_query,
    w_key,
    w_value,
    w_attn_out,
    w_inner,
    w_outer,
    bias_table,
    gain_one,
    gain_two,
    cotangent,
    side_cotangent,
):
    d, ff = w_inner.shape
    main, L = segments.shape
    heads = bias_table.shape[1]
    buckets = bias_table.shape[0]
    n0, n1 = tokens.shape[0], side_tokens.shape[0]
    slots = picked.shape[1] * picked.shape[2] * 2
    sizes = SimpleNamespace(
        n=n0 + n1, n0=n0, d=d, ff=ff, L=L, main=main, rows=main + side_segments.shape[0],
        heads=heads, slots=slots, mem=main * slots, questions=picked.shape[1],
        bank=memory_bank.shape[0],
    )
    units = 4 * (ff // d) + 8
    plan = Comm(units, GAPS) if remote else None
    layer = Layer(plan, sizes)
    scratch = layer.scratch()
    hbm = pl.BlockSpec(memory_space=pl.ANY)
    vmem = pl.BlockSpec(memory_space=pltpu.VMEM)
    shape = jax.ShapeDtypeStruct
    joined, output, grad_tokens, side_output, grad_side, small = pl.pallas_call(
        functools.partial(layer.kernel, list(scratch)),
        out_shape=(
            shape((units, 2, BLK, BLK), jnp.float32),
            shape(tokens.shape, jnp.bfloat16),
            shape(tokens.shape, jnp.bfloat16),
            shape(side_tokens.shape, jnp.bfloat16),
            shape(side_tokens.shape, jnp.bfloat16),
            shape((16, d), jnp.float32),
        ),
        in_specs=[hbm] * 11 + [vmem] * 7,
        out_specs=(hbm,) * 5 + (vmem,),
        scratch_shapes=list(scratch.values()),
        compiler_params=pltpu.CompilerParams(
            collective_id=0 if remote else None, has_side_effects=True, vmem_limit_bytes=VMEM_LIMIT
        ),
    )(
        tokens, side_tokens, cotangent, side_cotangent,
        memory_bank, w_query, w_key, w_value, w_attn_out, w_inner, w_outer,
        picked.reshape(-1, 1), segments, side_segments, offsets.reshape(1, -1), bias_table.T,
        gain_one, gain_two,
    )
    if not remote:
        joined = lax.psum(joined, AXES)
        small = lax.psum(small, AXES)
    square = shape((d, d), jnp.float32)
    wide, narrow = shape(tokens.shape, jnp.bfloat16), shape(side_tokens.shape, jnp.bfloat16)
    gain = shape((d,), jnp.float32)
    hold = pltpu.VMEM(tokens.shape, jnp.bfloat16), pltpu.VMEM(side_tokens.shape, jnp.bfloat16)
    outs = pl.pallas_call(
        functools.partial(place_units, sizes),
        out_shape=(
            wide, wide, narrow, narrow, square, square, square, square,
            shape((d, ff), jnp.float32), shape((ff, d), jnp.float32),
            shape((heads, buckets), jnp.float32), gain, gain,
        ),
        in_specs=[hbm] * 5 + [vmem],
        out_specs=(hbm,) * 10 + (vmem,) * 3,
        scratch_shapes=[
            pltpu.VMEM((2 * units, BLK, BLK), jnp.float32),
            hold[0], hold[0], hold[1], hold[1],
            pltpu.SemaphoreType.DMA((2 * units,)),
            pltpu.SemaphoreType.DMA((2 * units,)),
            pltpu.SemaphoreType.DMA((4, 2)),
        ],
        compiler_params=pltpu.CompilerParams(vmem_limit_bytes=VMEM_LIMIT),
    )(joined, output, grad_tokens, side_output, grad_side, small)
    output, grad_tokens, side_output, grad_side = outs[:4]
    return (output, grad_tokens, side_output, grad_side) + tuple(outs[4:10]) + (outs[10].T,) + tuple(outs[11:])


INS = ["tok", "side", "cot", "scot", "bank", "wq", "wk", "wv", "wo", "wi", "wu"]
INS = INS + ["idx", "segm", "segs", "offs", "btab", "g1", "g2"]
OUTS = ["out", "y", "gt", "sy", "sgt", "small"]
VMEM_LIMIT = 63 * 2**20
FWD_UNROLL = 6
BWD_UNROLL = 1
SMALL_GAP = 2


def solution(mesh):
    in_specs = (
        P(AXES, None),
        P(AXES, None),
        P(AXES, None, None),
        P(),
        P(),
        P(AXES, None),
        P(AXES, None),
        P(),
        P(),
        P(),
        P(),
        P(),
        P(),
        P(),
        P(),
        P(),
        P(AXES, None),
        P(AXES, None),
    )
    out_specs = (
        P(AXES, None),
        P(AXES, None),
        P(AXES, None),
        P(AXES, None),
        P(),
        P(),
        P(),
        P(),
        P(),
        P(),
        P(),
        P(),
        P(),
    )
    remote = dict(mesh.shape) == {'dp': 4, 'replica': 8}
    return jax.shard_map(functools.partial(body, remote), mesh=mesh, in_specs=in_specs, out_specs=out_specs, check_vma=False)
```

```python
import functools
from types import SimpleNamespace

import jax
import jax.numpy as jnp
from jax import lax
from jax.experimental import pallas as pl
from jax.experimental.pallas import tpu as pltpu
from jax.sharding import PartitionSpec as P

MESH = pl.DeviceIdType.MESH
epsilon = 1e-06
masked_value = -1e30
AXES = ("dp", "replica")

BLK = 384
STG = ["P", "A", "B", "C1", "C2", "C3", "E", "F1", "F2", "F3", "G", "H"]
GAPS = (1, 3, 1, 1, 2, 3, 2, 1, 2, 3, 1)
KEEP = 3
ORDER = STG[1:] + ["K"]
def offsets_of(gaps):
    o, a = {}, 0
    for s, g in zip(STG, (0,)+tuple(gaps)):
        a += g; o[s] = a
    return o

class Place:
    def __init__(self):
        dp = lax.axis_index("dp"); rep = lax.axis_index("replica")
        self.core = lax.rem(dp, 2); x = dp // 2; z = rep // 2; y = lax.rem(rep, 2)
        c = self.core
        self.partner = (dp + 1 - 2 * c, rep)
        xn = (dp + 2 - 4 * x, rep); yn = (dp, rep + 1 - 2 * y)
        pick = lambda a, b: tuple(jnp.where(c == 0, i, j) for i, j in zip(a, b))
        self.xn = xn; self.yn = yn
        self.n1 = pick(xn, yn); self.n2 = pick(yn, xn)
        self.b1 = jnp.where(c == 0, x, y); self.b2 = jnp.where(c == 0, y, x)
        self.end = (z == 0) | (z == 3)
        self.mid = (z == 1) | (z == 2)
        left = jnp.where(z < 2, 1, 0)
        near = z + 1 - 2 * lax.rem(z, 2)
        far = 3 - z
        self.near = (dp, near * 2 + y)
        self.far = (dp, far * 2 + y)
        self.fh = left
        self.bh = 1 - left

class Comm:
    NP = 4; N0 = 4; N1 = 8; NZ = 6; N3 = 6
    def __init__(self, units, gaps, first=0, pause=0):
        self.n = units; self.off = offsets_of(gaps)
        self.off["K"] = self.off["E"] + KEEP
        self.NW = self.off["K"] + 1
        self.first = first; self.pause = pause
        self.steps = units + pause + self.off['H']
    def scratch(self):
        n = self.n; D = pltpu.SemaphoreType.DMA; V = lambda *s: pltpu.VMEM(s, jnp.float32)
        return dict(
            W=V(self.NW, BLK, BLK), L0=V(self.N0, BLK, BLK), L1=V(self.N1, BLK//2, BLK),
            LA=V(self.NZ, BLK//4, BLK), LB=V(self.NZ, BLK//4, BLK), L3=V(self.N3, BLK//4, BLK),
            s0=D((self.N0,)), r0=D((self.N0,)), s1=D((self.NW,)), r1=D((self.N1,)),
            sz=D((self.NW, 2)), rA=D((self.NZ,)), rB=D((self.NZ,)), s3=D((self.NW,)), r3=D((self.N3,)),
            lo=D((self.NW,)), sg=D((n, 2)), gA=D((n,)), gB=D((n,)), s6=D((n, 2)), r6=D((n, 2)), s7=D((n,)), r7=D((n,)),
            c0=pltpu.SemaphoreType.REGULAR, c1=pltpu.SemaphoreType.REGULAR,
            cA=pltpu.SemaphoreType.REGULAR, cB=pltpu.SemaphoreType.REGULAR, c3=pltpu.SemaphoreType.REGULAR)
    def bind(self, s, out, src0):
        self.s = s; self.out = out; self.src0 = src0; self.p = Place()
    def entry(self):
        p = self.p; b = pltpu.get_barrier_semaphore()
        for d in (p.partner, p.xn, p.yn, p.near, p.far):
            pl.semaphore_signal(b, inc=1, device_id=d, device_id_type=MESH)
        pl.semaphore_wait(b, 5)
    def rc(self, src, dst, ss, rs, dev):
        return pltpu.make_async_remote_copy(src_ref=src, dst_ref=dst, send_sem=ss, recv_sem=rs, device_id=dev, device_id_type=MESH)
    def k0(self, u):
        s = self.s; i = lax.rem(u, self.N0)
        return self.rc(self.src0(u), s.L0.at[i], s.s0.at[i], s.r0.at[i], self.p.partner)
    def w(self, u): return lax.rem(u, self.NW)
    def k1(self, u):
        s = self.s; w = self.w(u); i = lax.rem(u, self.N1)
        return self.rc(s.W.at[w, pl.ds((1 - self.p.b1) * 192, 192)], s.L1.at[i], s.s1.at[w], s.r1.at[i], self.p.n1)
    def zrow(self, h): return self.p.b1 * 192 + h * 96
    def kz(self, u, h, L, r, dev, j):
        s = self.s; w = self.w(u); i = lax.rem(u, self.NZ)
        return self.rc(s.W.at[w, pl.ds(self.zrow(h), 96)], getattr(s, L).at[i], s.sz.at[w, j], getattr(s, r).at[i], dev)
    def k3(self, u):
        s = self.s; w = self.w(u); i = lax.rem(u, self.N3)
        return self.rc(self.held(u), s.L3.at[i], s.s3.at[w], s.r3.at[i], self.p.n2)
    def held(self, u): return self.s.W.at[self.w(u), pl.ds(self.zrow(self.p.bh), 96)]
    def kl(self, u):
        return pltpu.make_async_copy(self.held(u), self.piece(u, self.p.bh), self.s.lo.at[self.w(u)])
    def piece(self, u, h): return self.out.at[u, self.p.core, pl.ds(self.zrow(h), 96)]
    def kg(self, u, h, r, dev, j, src=None):
        s = self.s
        return self.rc(self.piece(u, h) if src is None else src, self.piece(u, h), s.sg.at[u, j], getattr(s, r).at[u], dev)
    def k6(self, u, h, src=None):
        s = self.s
        return self.rc(self.piece(u, h) if src is None else src, self.piece(u, h), s.s6.at[u, h], s.r6.at[u, h], self.p.n1)
    def k7(self, u):
        s = self.s; o = self.out.at[u, self.p.core]
        return self.rc(o, o, s.s7.at[u], s.r7.at[u], self.p.partner)
    def give(self, name, u, N, dev):
        @pl.when(u + N < self.n)
        def _(): pl.semaphore_signal(getattr(self.s, name), inc=1, device_id=dev, device_id_type=MESH)
    def take(self, name, u, N):
        @pl.when(u >= N)
        def _(): pl.semaphore_wait(getattr(self.s, name), 1)
    def send0(self, u):
        self.take('c0', u, self.N0)
        self.k0(u).start()
    def A(self, u):
        s = self.s; p = self.p; w = self.w(u); i = lax.rem(u, self.N0)
        self.k0(u).wait()
        s.W[w] = s.W[w] + s.L0[i]
        self.give('c0', u, self.N0, p.partner)
        self.take('c1', u, self.N1)
        self.k1(u).start()
    def B(self, u):
        s = self.s; p = self.p; w = self.w(u); i = lax.rem(u, self.N1)
        self.k1(u).wait_recv()
        rows = pl.ds(p.b1 * 192, 192)
        s.W[w, rows] = s.W[w, rows] + s.L1[i]
        self.give('c1', u, self.N1, p.n1)
        @pl.when(p.end)
        def _():
            self.take('cA', u, self.NZ)
            self.kz(u, p.fh, 'LA', 'rA', p.near, 0).start()
    def zadd(self, u, h, L, r):
        s = self.s; w = self.w(u); i = lax.rem(u, self.NZ)
        self.kz(u, h, L, r, self.p.near, 0).wait_recv()
        rows = pl.ds(self.zrow(h), 96)
        s.W[w, rows] = s.W[w, rows] + getattr(s, L)[i]
    def C1(self, u):
        p = self.p
        @pl.when(p.mid)
        def _():
            self.zadd(u, p.fh, 'LA', 'rA')
            self.give('cA', u, self.NZ, p.near)
            self.take('cB', u, self.NZ)
            self.kz(u, p.fh, 'LB', 'rB', p.far, 0).start()
    def C2(self, u):
        p = self.p
        @pl.when(p.mid)
        def _():
            self.zadd(u, p.bh, 'LB', 'rB')
            self.give('cB', u, self.NZ, p.far)
            self.take('cA', u, self.NZ)
            self.kz(u, p.bh, 'LA', 'rA', p.near, 1).start()
    def C3(self, u):
        p = self.p
        @pl.when(p.end)
        def _():
            self.zadd(u, p.bh, 'LA', 'rA')
            self.give('cA', u, self.NZ, p.near)
            self.take('c3', u, self.N3)
            self.k3(u).start()
    def E(self, u):
        s = self.s; p = self.p; w = self.w(u); i = lax.rem(u, self.N3)
        @pl.when(p.end)
        def _():
            self.k3(u).wait()
            rows = pl.ds(self.zrow(p.bh), 96)
            s.W[w, rows] = s.W[w, rows] + s.L3[i]
            self.give('c3', u, self.N3, p.n2)
            self.kg(u, p.bh, 'gA', p.near, 0, self.held(u)).start()
            self.k6(u, p.bh, self.held(u)).start()
            self.kl(u).start()
    def K(self, u):
        p = self.p
        self.k1(u).wait_send()
        self.kz(u, p.fh, 'LB', 'rB', p.far, 0).wait_send()
        @pl.when(p.mid)
        def _(): self.kz(u, p.bh, 'LA', 'rA', p.near, 1).wait_send()
        @pl.when(p.end)
        def _():
            self.kl(u).wait()
            self.kg(u, p.bh, 'gA', p.near, 0, self.held(u)).wait_send()
            self.k6(u, p.bh, self.held(u)).wait_send()
    def F1(self, u):
        p = self.p
        @pl.when(p.mid)
        def _():
            self.kg(u, p.bh, 'gA', p.near, 0).wait_recv()
            self.kg(u, p.bh, 'gB', p.far, 0).start()
            self.k6(u, p.bh).start()
    def F2(self, u):
        p = self.p
        @pl.when(p.mid)
        def _():
            self.kg(u, p.fh, 'gB', p.far, 1).wait_recv()
            self.kg(u, p.fh, 'gA', p.near, 1).start()
            self.k6(u, p.fh).start()
    def F3(self, u):
        p = self.p
        @pl.when(p.end)
        def _():
            self.kg(u, p.fh, 'gA', p.near, 1).wait_recv()
            self.k6(u, p.fh).start()
    def G(self, u):
        for h in (0, 1): self.k6(u, h).wait_recv()
        self.k7(u).start()
    def H(self, u):
        p = self.p
        self.k7(u).wait()
        self.k6(u, p.fh).wait_send()
        @pl.when(p.mid)
        def _():
            self.k6(u, p.bh).wait_send()
            self.kg(u, p.bh, 'gB', p.far, 0).wait_send()
            self.kg(u, p.fh, 'gA', p.near, 1).wait_send()
    def step(self, t):
        for st in ORDER:
            at = t - self.off[st]
            late = at >= self.first + self.pause
            u = jnp.where(late, at - self.pause, at)
            f = getattr(self, st)
            live = (at >= 0) & ((at < self.first) | late) & (u < self.n)
            pl.when(live)(lambda f=f, u=u: f(u))


def spread(values, gain):
    scale = lax.rsqrt(jnp.mean(values * values, axis=-1, keepdims=True) + epsilon)
    return values * scale * gain, scale


def dot_nn(a, b):
    return jnp.dot(a, b, preferred_element_type=jnp.float32)


def dot_nt(a, b):
    return lax.dot_general(a, b, (((1,), (1,)), ((), ())), preferred_element_type=jnp.float32)


def dot_tn(a, b):
    return lax.dot_general(a, b, (((0,), (0,)), ((), ())), preferred_element_type=jnp.float32)


def exact(a, b, dims):
    return lax.dot_general(
        a, b, (dims, ((), ())), precision=lax.Precision.HIGHEST,
        preferred_element_type=jnp.float32,
    )


class Layer:
    def __init__(self, plan, sizes):
        self.plan = plan
        self.z = sizes

    def scratch(self):
        z = self.z
        n, mem, d, ff = z.n, z.mem, z.d, z.ff
        all_rows = n + mem
        b16 = lambda *s: pltpu.VMEM(s, jnp.bfloat16)
        f32 = lambda *s: pltpu.VMEM(s, jnp.float32)
        L = z.L
        pairs = z.heads // 2
        DMA = pltpu.SemaphoreType.DMA
        own = dict(
            xb=b16(n, d), cb=b16(n, d), bk=b16(z.bank, 2, d),
            wq=b16(d, d), wk=b16(d, d), wv=b16(d, d), wo=b16(d, d),
            wib=b16(2, d, d), wub=b16(2, d, d),
            nall=b16(all_rows, d), qs=b16(n, d), ks=b16(all_rows, d), vs=b16(all_rows, d),
            att=b16(n, d), hid=f32(n, d), n2=b16(n, d), n2T=b16(d, n),
            oacc=f32(n, d), gacc=f32(n, d),
            act=b16(n, d), gib=b16(n, d),
            bias=f32(pairs, 2 * L, L), lse=f32(z.rows, 2 * L, 128),
            mq=b16(2 * L, 128), mk=b16(L, 128), mm=b16(z.slots, 128),
            dB=f32(pairs, 2 * L, L), dq=b16(n, d),
            seg=pltpu.VMEM((8, L), jnp.int32),
            sm=f32(16, d), lines=f32(16, 2 * L),
            isem=DMA((16,)), wsem=DMA((2, 2)), osem=DMA((6,)),
        )
        if self.plan is not None:
            own.update(self.plan.scratch())
            own.update(P=f32(self.plan.NP, BLK, BLK), L5=f32(5, 16, d), s5=DMA((5,)), r5=DMA((5,)))
        else:
            own.update(W=f32(2, BLK, BLK), P=f32(2, BLK, BLK), esem=DMA((2,)))
        return own

    def slots(self, u):
        if self.plan is None:
            return lax.rem(u, 2), lax.rem(u, 2)
        return self.plan.w(u), lax.rem(u, self.plan.NP)

    def emit(self, u):
        s = self.s
        if self.plan is not None:
            self.plan.send0(u)
            return
        w, p = self.slots(u)
        one = pltpu.make_async_copy(s.W.at[w], self.out.at[u, 0], s.esem.at[0])
        two = pltpu.make_async_copy(s.P.at[p], self.out.at[u, 1], s.esem.at[1])
        one.start()
        two.start()
        one.wait()
        two.wait()

    def emit_cols(self, u, value):
        s = self.s
        w, p = self.slots(u)

        @pl.when(self.core == 0)
        def _():
            s.W[w] = value[:, :BLK]
            s.P[p] = value[:, BLK:]

        @pl.when(self.core != 0)
        def _():
            s.W[w] = value[:, BLK:]
            s.P[p] = value[:, :BLK]

        self.emit(u)

    def step(self, t):
        if self.plan is not None:
            self.plan.step(t)

    def kernel(self, names, *refs):
        z = self.z
        ins = SimpleNamespace(**dict(zip(INS, refs)))
        outs = SimpleNamespace(**dict(zip(OUTS, refs[18:])))
        s = SimpleNamespace(**dict(zip(names, refs[24:])))
        s.gb, s.dk, s.dv = s.wub.at[0], s.wib.at[0], s.wib.at[1]
        s.dkm, s.dvm = s.wub.at[1, pl.ds(0, z.mem)], s.wub.at[1, pl.ds(z.mem, z.mem)]
        self.s, self.ins, self.outs, self.out = s, ins, outs, outs.out
        if self.plan is not None:
            self.plan.bind(s, outs.out, lambda u: s.P.at[lax.rem(u, self.plan.NP)])
            self.core = self.plan.p.core
        else:
            self.core = jnp.int32(0)
        self.load()
        if self.plan is not None:
            self.plan.entry()
        self.front()
        self.ffn()
        self.middle()
        self.attn_back()
        self.back()

    def load(self):
        s, i, z = self.s, self.ins, self.z
        n0 = z.n0
        cp = pltpu.make_async_copy
        sem = lambda k: s.isem.at[k]
        d = z.d
        self.c = SimpleNamespace(
            x0=cp(i.tok, s.xb.at[pl.ds(0, n0)], sem(0)),
            x1=cp(i.side, s.xb.at[pl.ds(n0, z.n - n0)], sem(1)),
            bk=cp(i.bank, s.bk, sem(2)),
            wq=cp(i.wq, s.wq, sem(3)), wk=cp(i.wk, s.wk, sem(4)),
            wv=cp(i.wv, s.wv, sem(5)), wo=cp(i.wo, s.wo, sem(6)),
            c0=cp(i.cot, s.cb.at[pl.ds(0, n0)], sem(7)),
            c1=cp(i.scot, s.cb.at[pl.ds(n0, z.n - n0)], sem(8)),
        )
        for k in ("x0", "x1", "bk", "wq", "wk", "wv", "wo"):
            getattr(self.c, k).start()
        for k in self.wcopy(0):
            k.start()
        self.c.c0.start()
        self.c.c1.start()

    def wcopy(self, c):
        s, i, d = self.s, self.ins, self.z.d
        slot = lax.rem(c, 2) if not isinstance(c, int) else c % 2
        cols = pl.ds(c * d if isinstance(c, int) else pl.multiple_of(c * d, d), d)
        return (
            pltpu.make_async_copy(i.wi.at[:, cols], s.wib.at[slot], s.wsem.at[slot, 0]),
            pltpu.make_async_copy(i.wu.at[cols, :], s.wub.at[slot], s.wsem.at[slot, 1]),
        )

    def tile(self, k):
        return pl.ds(pl.multiple_of(k * 256, 256), 256)

    def memory(self):
        s, z = self.s, self.z
        entries = lax.broadcasted_iota(jnp.int32, (z.mem // 2, z.bank), 1)
        hot = jnp.where(entries == self.ins.idx[...], 1.0, 0.0).astype(jnp.bfloat16)
        return tuple(dot_nn(hot, s.bk[:, part, :]) for part in range(2))

    def mem_rows(self, r, part):
        z = self.z
        return pl.ds(z.n + r * z.slots + part * (z.slots // 2), z.slots // 2)

    def heads(self, value):
        lane = lax.broadcasted_iota(jnp.int32, (1, 128), 1)
        first = jnp.where(lane < 64, 1.0, 0.0).astype(jnp.bfloat16)
        second = jnp.where(lane < 64, 0.0, 1.0).astype(jnp.bfloat16)
        return jnp.concatenate([value * first, value * second], axis=0)

    def merge(self, value):
        rows = value.shape[0] // 2
        lane = lax.broadcasted_iota(jnp.int32, (rows, 128), 1)
        return jnp.where(lane < 64, value[:rows], value[rows:])

    def slot_mask(self):
        s, z = self.s, self.z
        lane = lax.broadcasted_iota(jnp.int32, (z.slots, 128), 1)
        slot = lax.broadcasted_iota(jnp.int32, (z.slots, 128), 0)
        slot = jnp.where(slot >= z.slots // 2, slot - z.slots // 2, slot)
        each = z.slots // 2 // z.questions
        hit = (slot >= lane * each) & (slot < (lane + 1) * each)
        s.mm[...] = jnp.where(hit, 1.0, 0.0).astype(jnp.bfloat16)

    def masks(self, r):
        s, z = self.s, self.z
        L = z.L
        row = s.seg[pl.ds(r, 1), :].astype(jnp.float32)
        down = jnp.broadcast_to(row, (L, L)).T[:, :128]
        lane = lax.broadcasted_iota(jnp.int32, (L, 128), 1)
        own = down == lane.astype(jnp.float32)
        s.mk[...] = jnp.where(own, 1.0, 0.0).astype(jnp.bfloat16)
        outside = jnp.where(own | (lane >= z.questions), 0.0, masked_value).astype(jnp.bfloat16)
        s.mq[pl.ds(0, L), :] = outside
        s.mq[pl.ds(L, L), :] = outside

    def spans(self, r, j):
        z = self.z
        rows = pl.ds(pl.multiple_of(r * z.L, z.L), z.L)
        mem = pl.ds(pl.multiple_of(z.n + r * z.slots, 32), z.slots)
        lanes = pl.ds(pl.multiple_of(j * 128, 128), 128)
        return rows, mem, lanes

    def scores(self, r, j, has_mem):
        s = self.s
        rows, mem, lanes = self.spans(r, j)
        q2 = self.heads(s.qs[rows, lanes])
        wide = jnp.concatenate([q2, s.mq[...]], axis=1)
        st = dot_nt(wide, jnp.concatenate([s.ks[rows, lanes], s.mk[...]], axis=1)) + s.bias[j]
        sm = None
        if has_mem:
            sm = dot_nt(wide, jnp.concatenate([s.ks[mem, lanes], s.mm[...]], axis=1))
        return q2, st, sm

    def fwd_pair(self, r, j, has_mem):
        s, z = self.s, self.z
        rows, mem, lanes = self.spans(r, j)
        q2, st, sm = self.scores(r, j, has_mem)
        top = jnp.max(st, axis=1, keepdims=True)
        if has_mem:
            top = jnp.maximum(top, jnp.max(sm, axis=1, keepdims=True))
        et = jnp.exp(st - top).astype(jnp.bfloat16)
        ones = jnp.ones((z.L, 128), jnp.bfloat16)
        mixed = dot_nn(et, jnp.concatenate([s.vs[rows, lanes], ones], axis=1))
        if has_mem:
            em = jnp.exp(sm - top).astype(jnp.bfloat16)
            ones = ones[: z.slots]
            mixed = mixed + dot_nn(em, jnp.concatenate([s.vs[mem, lanes], ones], axis=1))
        total = mixed[:, 128:]
        s.att[rows, lanes] = self.merge(mixed[:, :128] / total).astype(jnp.bfloat16)
        lane = lax.broadcasted_iota(jnp.int32, (2 * z.L, 128), 1)
        s.lse[r] = jnp.where(lane == j, top + jnp.log(total), s.lse[r])

    def front(self):
        s, z, i = self.s, self.z, self.ins
        L, d, n = z.L, z.d, z.n
        offs = i.offs[...]
        spots = offs.shape[1]
        bucket = lax.broadcasted_iota(jnp.int32, (i.btab.shape[1], spots), 0)
        hot = jnp.where(bucket == offs, 1.0, 0.0)
        line = exact(i.btab[...], hot, ((1,), (0,)))
        line = jnp.concatenate([line, jnp.zeros((line.shape[0], 2 * L - spots), jnp.float32)], 1)
        for h in range(z.heads):
            wide = jnp.broadcast_to(line[h : h + 1], (L, 2 * L))
            turned = pltpu.roll(wide, L + 1, 1, stride=1, stride_axis=0)
            s.bias[h // 2, pl.ds((h % 2) * L, L), :] = turned[:, :L]
        self.slot_mask()
        s.seg[pl.ds(0, z.main), :] = i.segm[...]
        s.seg[pl.ds(z.main, z.rows - z.main), :] = i.segs[...]
        g1 = i.g1[...].reshape(1, d)
        self.c.x0.wait()
        self.c.x1.wait()

        def norm_row(r, carry):
            rows = pl.ds(pl.multiple_of(r * L, L), L)
            s.nall[rows, :] = spread(s.xb[rows, :].astype(jnp.float32), g1)[0].astype(jnp.bfloat16)
            return carry

        lax.fori_loop(0, z.rows, norm_row, 0)
        self.c.bk.wait()
        half = z.slots // 2
        for part, memory in enumerate(self.memory()):
            normed = spread(memory, g1)[0].astype(jnp.bfloat16)
            for r in range(z.main):
                s.nall[self.mem_rows(r, part), :] = normed[r * half : (r + 1) * half]
        for k in ("wq", "wk", "wv"):
            getattr(self.c, k).wait()

        def project(k, carry):
            cols = self.tile(k)
            s.qs[:, cols] = dot_nn(s.nall[pl.ds(0, n), :], s.wq[:, cols]).astype(jnp.bfloat16)
            s.ks[:, cols] = dot_nn(s.nall[...], s.wk[:, cols]).astype(jnp.bfloat16)
            s.vs[:, cols] = dot_nn(s.nall[...], s.wv[:, cols]).astype(jnp.bfloat16)
            return carry

        lax.fori_loop(0, d // 256, project, 0)
        pairs = z.heads // 2

        def row(has_mem, r, carry):
            self.masks(r)

            def pair(j, inner):
                self.fwd_pair(r, j, has_mem)
                return inner

            return lax.fori_loop(0, pairs, pair, carry, unroll=FWD_UNROLL)

        lax.fori_loop(0, z.main, functools.partial(row, True), 0)
        lax.fori_loop(z.main, z.rows, functools.partial(row, False), 0)
        self.c.wo.wait()

        def attn_out(k, carry):
            cols = self.tile(k)
            s.hid[:, cols] = s.xb[:, cols].astype(jnp.float32) + dot_nn(s.att[...], s.wo[:, cols])
            return carry

        lax.fori_loop(0, d // 256, attn_out, 0)
        g2 = i.g2[...].reshape(1, d)

        def norm_two(r, carry):
            rows = pl.ds(pl.multiple_of(r * L, L), L)
            s.n2[rows, :] = spread(s.hid[rows, :], g2)[0].astype(jnp.bfloat16)
            return carry

        lax.fori_loop(0, z.rows, norm_two, 0)

    def ffn(self):
        s, z, i = self.s, self.z, self.ins
        d, n = z.d, z.n
        chunks = z.ff // d
        self.c.c0.wait()
        self.c.c1.wait()
        root = 0.7978845608028654

        def chunk(c, carry):
            slot = lax.rem(c, 2)
            for k in self.wcopy(c):
                k.wait()

            @pl.when(c + 1 < chunks)
            def _():
                for k in self.wcopy(c + 1):
                    k.start()

            def part(k, inner):
                cols = self.tile(k)
                v = dot_nn(s.n2[...], s.wib[slot, :, cols])
                ga = dot_nt(s.cb[...], s.wub[slot, cols, :])
                square = v * v
                th = jnp.tanh(root * v * (1.0 + 0.044715 * square))
                half = 0.5 * (1.0 + th)
                s.act[:, cols] = (v * half).astype(jnp.bfloat16)
                slope = half + (0.5 * root) * v * (1.0 - th * th) * (1.0 + 0.134145 * square)
                s.gib[:, cols] = (ga * slope).astype(jnp.bfloat16)

                @pl.when(k == 1)
                def _():
                    outer(0, inner)

                return inner

            def outer(k, inner):
                u = 4 * c + k
                cols = pl.ds(k * BLK, BLK)
                self.emit_cols(u, dot_tn(s.act[:, cols], s.cb[...]))
                self.step(u)
                return inner

            def gather(k, inner):
                cols = self.tile(k)
                po = dot_nn(s.act[...], s.wub[slot, :, cols])
                pg = dot_nt(s.gib[...], s.wib[slot, cols, :])

                @pl.when(c == 0)
                def _():
                    s.oacc[:, cols] = po
                    s.gacc[:, cols] = pg

                @pl.when(c > 0)
                def _():
                    s.oacc[:, cols] = s.oacc[:, cols] + po
                    s.gacc[:, cols] = s.gacc[:, cols] + pg

                return inner

            lax.fori_loop(0, d // 256, part, 0)
            lax.fori_loop(0, d // 256, gather, 0)
            outer(1, 0)

            @pl.when(c == 0)
            def _():
                s.n2T[...] = s.n2[...].T

            def inner_grad(k, inner):
                self.inner_unit(4 * c + 2 + k, k)
                self.step(4 * c + 2 + k)
                return inner

            @pl.when(c + 1 < chunks)
            def _():
                lax.fori_loop(0, 2, inner_grad, 0)

            return carry

        lax.fori_loop(0, chunks, chunk, 0)

    def inner_unit(self, u, k):
        s = self.s
        w, p = self.slots(u)
        cols = pl.ds(pl.multiple_of(k * BLK, BLK), BLK)
        mine = pl.ds(pl.multiple_of(self.core * BLK, BLK), BLK)
        other = pl.ds(pl.multiple_of((1 - self.core) * BLK, BLK), BLK)
        s.P[p] = dot_nn(s.n2T[other, :], s.gib[:, cols])
        s.W[w] = dot_nn(s.n2T[mine, :], s.gib[:, cols])
        self.emit(u)

    def out_unit(self, u, k):
        s = self.s
        cols = pl.ds(pl.multiple_of(k * BLK, BLK), BLK)
        self.emit_cols(u, dot_tn(s.att[:, cols], s.gb[...]))

    def middle(self):
        s, z, i = self.s, self.z, self.ins
        L, d, n, n0 = z.L, z.d, z.n, z.n0
        g2 = i.g2[...].reshape(1, d)

        def row(r, gain):
            rows = pl.ds(pl.multiple_of(r * L, L), L)
            hid = s.hid[rows, :]
            s.dq[rows, :] = (hid + s.oacc[rows, :]).astype(jnp.bfloat16)
            scale = lax.rsqrt(jnp.mean(hid * hid, axis=-1, keepdims=True) + epsilon)
            grad = s.gacc[rows, :]
            gain = gain + jnp.sum(grad * hid * scale, axis=0, keepdims=True)
            u = grad * g2
            average = jnp.mean(u * hid, axis=-1, keepdims=True)
            full = s.cb[rows, :].astype(jnp.float32) + scale * u - hid * (scale * scale * scale * average)
            s.gacc[rows, :] = full
            s.gb[rows, :] = full.astype(jnp.bfloat16)
            return gain

        gain = lax.fori_loop(0, z.rows, row, jnp.zeros((1, d), jnp.float32))
        s.sm[...] = jnp.zeros((16, d), jnp.float32)
        s.sm[pl.ds(13, 1), :] = gain
        self.o = (
            pltpu.make_async_copy(s.dq.at[pl.ds(0, n0)], self.outs.y, s.osem.at[0]),
            pltpu.make_async_copy(s.dq.at[pl.ds(n0, n - n0)], self.outs.sy, s.osem.at[1]),
        )
        for k in self.o:
            k.start()

        def back(k, carry):
            cols = self.tile(k)
            s.n2[:, cols] = dot_nt(s.gb[...], s.wo[cols, :]).astype(jnp.bfloat16)
            return carry

        lax.fori_loop(0, d // 256, back, 0)
        for k in self.o:
            k.wait()

    def bwd_pair(self, r, j, has_mem):
        s, z = self.s, self.z
        rows, mem, lanes = self.spans(r, j)
        q2, st, sm = self.scores(r, j, has_mem)
        lane = lax.broadcasted_iota(jnp.int32, (2 * z.L, 128), 1)
        lse = jnp.sum(jnp.where(lane == j, s.lse[r], 0.0), axis=1, keepdims=True)
        d2 = self.heads(s.n2[rows, lanes])
        pt = jnp.exp(st - lse)
        gt = dot_nt(d2, s.vs[rows, lanes])
        delta = jnp.sum(pt * gt, axis=1, keepdims=True)
        if has_mem:
            pm = jnp.exp(sm - lse)
            gm = dot_nt(d2, s.vs[mem, lanes])
            delta = delta + jnp.sum(pm * gm, axis=1, keepdims=True)
        dst = (pt * (gt - delta)).astype(jnp.bfloat16)
        grad_q = dot_nn(dst, s.ks[rows, lanes])
        s.dk[rows, lanes] = dot_tn(dst, q2).astype(jnp.bfloat16)
        s.dv[rows, lanes] = dot_tn(pt.astype(jnp.bfloat16), d2).astype(jnp.bfloat16)
        if has_mem:
            dsm = (pm * (gm - delta)).astype(jnp.bfloat16)
            grad_q = grad_q + dot_nn(dsm, s.ks[mem, lanes])
            slot = pl.ds(pl.multiple_of(r * z.slots, 32), z.slots)
            s.dkm[slot, lanes] = dot_tn(dsm, q2).astype(jnp.bfloat16)
            s.dvm[slot, lanes] = dot_tn(pm.astype(jnp.bfloat16), d2).astype(jnp.bfloat16)
        s.dq[rows, lanes] = self.merge(grad_q).astype(jnp.bfloat16)
        s.dB[j] = s.dB[j] + dst.astype(jnp.float32)

    def attn_back(self):
        s, z = self.s, self.z
        pairs = z.heads // 2
        first = 4 * (z.ff // z.d) - 2

        def clear(j, carry):
            s.dB[j] = jnp.zeros(s.dB.shape[1:], jnp.float32)
            return carry

        lax.fori_loop(0, pairs, clear, 0)

        def row(has_mem, r, carry):
            self.masks(r)

            def few(g, inner):
                def pair(k, last):
                    self.bwd_pair(r, g * 3 + k, has_mem)
                    return last

                lax.fori_loop(0, 3, pair, 0, unroll=BWD_UNROLL)
                if has_mem:
                    u = first + 2 * r + g

                    @pl.when(r == 0)
                    def _():
                        self.out_unit(u, g)

                    @pl.when(r > 0)
                    def _():
                        self.inner_unit(u, g)

                    self.step(u)
                return inner

            return lax.fori_loop(0, pairs // 3, few, carry)

        lax.fori_loop(0, z.main, functools.partial(row, True), 0)
        lax.fori_loop(z.main, z.rows, functools.partial(row, False), 0)

    def back(self):
        s, z, i = self.s, self.z, self.ins
        L, d, n, n0, mem = z.L, z.d, z.n, z.n0, z.mem
        first = 4 * (z.ff // d) + 2
        tok, mrows = pl.ds(0, n), pl.ds(n, mem)
        def difference(j):
            for side in range(2):
                grid = s.dB[j, pl.ds(side * L, L), :]
                wide = jnp.concatenate([grid, jnp.zeros((L, L), jnp.float32)], axis=1)
                wide = pltpu.roll(wide, L - 1, 1)
                half = L // 2
                while half:
                    wide = wide[:half] + pltpu.roll(wide[half:], 2 * L - half, 1)
                    half = half // 2
                s.lines[pl.ds(2 * j + side, 1), :] = wide

        u = first
        for grad, grad_mem in ((s.dq, None), (s.dk, s.dkm), (s.dv, s.dvm)):
            def one(k, carry, grad=grad, grad_mem=grad_mem, u=u):
                cols = pl.ds(pl.multiple_of(k * BLK, BLK), BLK)
                value = dot_tn(s.nall[tok, cols], grad[...])
                if grad_mem is not None:
                    value = value + dot_tn(s.nall[mrows, cols], grad_mem[...])
                self.emit_cols(u + k, value)
                self.step(u + k)
                difference(u - first + k)
                return carry

            lax.fori_loop(0, 2, one, 0)
            u = u + 2
        t = first + 6
        def grads(k, carry):
            cols = self.tile(k)
            self.step(t + k)
            s.hid[:, cols] = (
                dot_nt(s.dq[...], s.wq[cols, :])
                + dot_nt(s.dk[...], s.wk[cols, :])
                + dot_nt(s.dv[...], s.wv[cols, :])
            )
            s.oacc[pl.ds(0, mem), cols] = dot_nt(s.dkm[...], s.wk[cols, :]) + dot_nt(
                s.dvm[...], s.wv[cols, :]
            )
            return carry

        lax.fori_loop(0, d // 256, grads, 0)
        t = t + d // 256
        g1 = i.g1[...].reshape(1, d)

        def row(r, gain):
            rows = pl.ds(pl.multiple_of(r * L, L), L)
            x = s.xb[rows, :].astype(jnp.float32)
            scale = lax.rsqrt(jnp.mean(x * x, axis=-1, keepdims=True) + epsilon)
            grad = s.hid[rows, :]
            gain = gain + jnp.sum(grad * x * scale, axis=0, keepdims=True)
            v = grad * g1
            average = jnp.mean(v * x, axis=-1, keepdims=True)
            full = s.gacc[rows, :] + scale * v - x * (scale * scale * scale * average)
            s.gb[rows, :] = full.astype(jnp.bfloat16)
            self.step(t + r)
            return gain

        gain = lax.fori_loop(0, z.rows, row, jnp.zeros((1, d), jnp.float32))
        t = t + z.rows
        late = (
            pltpu.make_async_copy(s.gb.at[pl.ds(0, n0)], self.outs.gt, s.osem.at[2]),
            pltpu.make_async_copy(s.gb.at[pl.ds(n0, n - n0)], self.outs.sgt, s.osem.at[3]),
        )
        for k in late:
            k.start()
        half = z.slots // 2
        for part, memory in enumerate(self.memory()):
            scale = lax.rsqrt(jnp.mean(memory * memory, axis=-1, keepdims=True) + epsilon)
            unit = memory * scale
            for r in range(z.main):
                grad = s.oacc[pl.ds(r * z.slots + part * half, half), :]
                gain = gain + jnp.sum(grad * unit[r * half : (r + 1) * half], axis=0, keepdims=True)
        s.sm[pl.ds(12, 1), :] = gain
        offs = i.offs[...]
        bucket = lax.broadcasted_iota(jnp.int32, (128, offs.shape[1]), 0)
        hot = jnp.where(bucket == offs, 1.0, 0.0)
        s.sm[pl.ds(0, z.heads), pl.ds(0, 128)] = exact(
            s.lines[pl.ds(0, z.heads), pl.ds(0, offs.shape[1])], hot, ((1,), (1,))
        )
        if self.plan is not None:
            self.finish(t)
        for k in late:
            k.wait()
        self.outs.small[...] = s.sm[...]

    def steps_from(self, t, count):
        def one(k, carry):
            self.step(k)
            return carry

        lax.fori_loop(t, t + count, one, 0)
        return t + count

    def finish(self, t):
        plan, s = self.plan, self.s
        p = plan.p
        peers = (p.partner, p.xn, p.yn, p.near, p.far)
        for k, dev in enumerate(peers):
            copy = plan.rc(s.sm, s.L5.at[k], s.s5.at[k], s.r5.at[k], dev)
            copy.start()
            t = self.steps_from(t, SMALL_GAP)
            copy.wait()
            s.sm[...] = s.sm[...] + s.L5[k]

        def rest(k, carry):
            self.step(k)
            return carry

        lax.fori_loop(t, plan.steps, rest, 0)


def place_units(
    sizes, units, y, gt, sy, sgt, small,
    oy, ogt, osy, osgt, wq, wk, wv, wo, wi, wu, gb, gg1, gg2,
    hold, vy, vgt, vsy, vsgt, sem, late, rsem,
):
    d, ff = sizes.d, sizes.ff
    copies = []

    def put(u, half, ref, row, col):
        k = len(copies)
        place = ref.at[pl.ds(row, BLK), pl.ds(col, BLK)]
        copies.append(
            (
                pltpu.make_async_copy(units.at[u, half], hold.at[k], sem.at[k]),
                pltpu.make_async_copy(hold.at[k], place, late.at[k]),
            )
        )

    for c in range(ff // d):
        for k in range(2):
            for half in range(2):
                put(4 * c + k, half, wu, c * d + k * BLK, half * BLK)
                after = 2 if c + 1 < ff // d else 4
                put(4 * c + after + k, half, wi, half * BLK, c * d + k * BLK)
    for k in range(2):
        for half in range(2):
            put(4 * (ff // d) - 2 + k, half, wo, k * BLK, half * BLK)
    u = 4 * (ff // d) + 2
    for ref in (wq, wk, wv):
        for k in range(2):
            for half in range(2):
                put(u + k, half, ref, k * BLK, half * BLK)
        u = u + 2
    for k, (src, mid, dst) in enumerate(
        ((y, vy, oy), (gt, vgt, ogt), (sy, vsy, osy), (sgt, vsgt, osgt))
    ):
        copies.append(
            (
                pltpu.make_async_copy(src, mid, rsem.at[k, 0]),
                pltpu.make_async_copy(mid, dst, rsem.at[k, 1]),
            )
        )
    for fetch, store in copies:
        fetch.start()
    heads, buckets = gb.shape
    gb[...] = small[pl.ds(0, heads), pl.ds(0, buckets)]
    gg1[...] = small[12, :]
    gg2[...] = small[13, :]
    for fetch, store in copies:
        fetch.wait()
        store.start()
    for fetch, store in copies:
        store.wait()


def body(
    remote,
    tokens,
    segments,
    picked,
    offsets,
    memory_bank,
    side_tokens,
    side_segments,
    w_query,
    w_key,
    w_value,
    w_attn_out,
    w_inner,
    w_outer,
    bias_table,
    gain_one,
    gain_two,
    cotangent,
    side_cotangent,
):
    d, ff = w_inner.shape
    main, L = segments.shape
    heads = bias_table.shape[1]
    buckets = bias_table.shape[0]
    n0, n1 = tokens.shape[0], side_tokens.shape[0]
    slots = picked.shape[1] * picked.shape[2] * 2
    sizes = SimpleNamespace(
        n=n0 + n1, n0=n0, d=d, ff=ff, L=L, main=main, rows=main + side_segments.shape[0],
        heads=heads, slots=slots, mem=main * slots, questions=picked.shape[1],
        bank=memory_bank.shape[0],
    )
    units = 4 * (ff // d) + 8
    plan = Comm(units, GAPS) if remote else None
    layer = Layer(plan, sizes)
    scratch = layer.scratch()
    hbm = pl.BlockSpec(memory_space=pl.ANY)
    vmem = pl.BlockSpec(memory_space=pltpu.VMEM)
    shape = jax.ShapeDtypeStruct
    joined, output, grad_tokens, side_output, grad_side, small = pl.pallas_call(
        functools.partial(layer.kernel, list(scratch)),
        out_shape=(
            shape((units, 2, BLK, BLK), jnp.float32),
            shape(tokens.shape, jnp.bfloat16),
            shape(tokens.shape, jnp.bfloat16),
            shape(side_tokens.shape, jnp.bfloat16),
            shape(side_tokens.shape, jnp.bfloat16),
            shape((16, d), jnp.float32),
        ),
        in_specs=[hbm] * 11 + [vmem] * 7,
        out_specs=(hbm,) * 5 + (vmem,),
        scratch_shapes=list(scratch.values()),
        compiler_params=pltpu.CompilerParams(
            collective_id=0 if remote else None, has_side_effects=True, vmem_limit_bytes=VMEM_LIMIT
        ),
    )(
        tokens, side_tokens, cotangent, side_cotangent,
        memory_bank, w_query, w_key, w_value, w_attn_out, w_inner, w_outer,
        picked.reshape(-1, 1), segments, side_segments, offsets.reshape(1, -1), bias_table.T,
        gain_one, gain_two,
    )
    if not remote:
        joined = lax.psum(joined, AXES)
        small = lax.psum(small, AXES)
    square = shape((d, d), jnp.float32)
    wide, narrow = shape(tokens.shape, jnp.bfloat16), shape(side_tokens.shape, jnp.bfloat16)
    gain = shape((d,), jnp.float32)
    hold = pltpu.VMEM(tokens.shape, jnp.bfloat16), pltpu.VMEM(side_tokens.shape, jnp.bfloat16)
    outs = pl.pallas_call(
        functools.partial(place_units, sizes),
        out_shape=(
            wide, wide, narrow, narrow, square, square, square, square,
            shape((d, ff), jnp.float32), shape((ff, d), jnp.float32),
            shape((heads, buckets), jnp.float32), gain, gain,
        ),
        in_specs=[hbm] * 5 + [vmem],
        out_specs=(hbm,) * 10 + (vmem,) * 3,
        scratch_shapes=[
            pltpu.VMEM((2 * units, BLK, BLK), jnp.float32),
            hold[0], hold[0], hold[1], hold[1],
            pltpu.SemaphoreType.DMA((2 * units,)),
            pltpu.SemaphoreType.DMA((2 * units,)),
            pltpu.SemaphoreType.DMA((4, 2)),
        ],
        compiler_params=pltpu.CompilerParams(vmem_limit_bytes=VMEM_LIMIT),
    )(joined, output, grad_tokens, side_output, grad_side, small)
    output, grad_tokens, side_output, grad_side = outs[:4]
    return (output, grad_tokens, side_output, grad_side) + tuple(outs[4:10]) + (outs[10].T,) + tuple(outs[11:])


INS = ["tok", "side", "cot", "scot", "bank", "wq", "wk", "wv", "wo", "wi", "wu"]
INS = INS + ["idx", "segm", "segs", "offs", "btab", "g1", "g2"]
OUTS = ["out", "y", "gt", "sy", "sgt", "small"]
VMEM_LIMIT = 63 * 2**20
FWD_UNROLL = 6
BWD_UNROLL = 1
SMALL_GAP = 2


def solution(mesh):
    in_specs = (
        P(AXES, None),
        P(AXES, None),
        P(AXES, None, None),
        P(),
        P(),
        P(AXES, None),
        P(AXES, None),
        P(),
        P(),
        P(),
        P(),
        P(),
        P(),
        P(),
        P(),
        P(),
        P(AXES, None),
        P(AXES, None),
    )
    out_specs = (
        P(AXES, None),
        P(AXES, None),
        P(AXES, None),
        P(AXES, None),
        P(),
        P(),
        P(),
        P(),
        P(),
        P(),
        P(),
        P(),
        P(),
    )
    remote = dict(mesh.shape) == {'dp': 4, 'replica': 8}
    return jax.shard_map(functools.partial(body, remote), mesh=mesh, in_specs=in_specs, out_specs=out_specs, check_vma=False)
```

```python
import functools
from types import SimpleNamespace

import jax
import jax.numpy as jnp
from jax import lax
from jax.experimental import pallas as pl
from jax.experimental.pallas import tpu as pltpu
from jax.sharding import PartitionSpec as P

MESH = pl.DeviceIdType.MESH
epsilon = 1e-06
masked_value = -1e30
AXES = ("dp", "replica")

BLK = 384
STG = ["P", "A", "B", "C1", "C2", "C3", "E", "F1", "F2", "F3", "G", "H"]
GAPS = (1, 3, 1, 1, 2, 3, 2, 1, 2, 3, 1)
KEEP = 3
ORDER = STG[1:] + ["K"]
def offsets_of(gaps):
    o, a = {}, 0
    for s, g in zip(STG, (0,)+tuple(gaps)):
        a += g; o[s] = a
    return o

class Place:
    def __init__(self):
        dp = lax.axis_index("dp"); rep = lax.axis_index("replica")
        self.core = lax.rem(dp, 2); x = dp // 2; z = rep // 2; y = lax.rem(rep, 2)
        c = self.core
        self.partner = (dp + 1 - 2 * c, rep)
        xn = (dp + 2 - 4 * x, rep); yn = (dp, rep + 1 - 2 * y)
        pick = lambda a, b: tuple(jnp.where(c == 0, i, j) for i, j in zip(a, b))
        self.xn = xn; self.yn = yn
        self.n1 = pick(xn, yn); self.n2 = pick(yn, xn)
        self.b1 = jnp.where(c == 0, x, y); self.b2 = jnp.where(c == 0, y, x)
        self.end = (z == 0) | (z == 3)
        self.mid = (z == 1) | (z == 2)
        left = jnp.where(z < 2, 1, 0)
        near = z + 1 - 2 * lax.rem(z, 2)
        far = 3 - z
        self.near = (dp, near * 2 + y)
        self.far = (dp, far * 2 + y)
        self.fh = left
        self.bh = 1 - left

class Comm:
    NP = 4; N0 = 4; N1 = 8; NZ = 6; N3 = 6
    def __init__(self, units, gaps, first=0, pause=0):
        self.n = units; self.off = offsets_of(gaps)
        self.off["K"] = self.off["E"] + KEEP
        self.NW = self.off["K"] + 1
        self.first = first; self.pause = pause
        self.steps = units + pause + self.off['H']
    def scratch(self):
        n = self.n; D = pltpu.SemaphoreType.DMA; V = lambda *s: pltpu.VMEM(s, jnp.float32)
        return dict(
            W=V(self.NW, BLK, BLK), L0=V(self.N0, BLK, BLK), L1=V(self.N1, BLK//2, BLK),
            LA=V(self.NZ, BLK//4, BLK), LB=V(self.NZ, BLK//4, BLK), L3=V(self.N3, BLK//4, BLK),
            s0=D((self.N0,)), r0=D((self.N0,)), s1=D((self.NW,)), r1=D((self.N1,)),
            sz=D((self.NW, 2)), rA=D((self.NZ,)), rB=D((self.NZ,)), s3=D((self.NW,)), r3=D((self.N3,)),
            lo=D((self.NW,)), sg=D((n, 2)), gA=D((n,)), gB=D((n,)), s6=D((n, 2)), r6=D((n, 2)), s7=D((n,)), r7=D((n,)),
            c0=pltpu.SemaphoreType.REGULAR, c1=pltpu.SemaphoreType.REGULAR,
            cA=pltpu.SemaphoreType.REGULAR, cB=pltpu.SemaphoreType.REGULAR, c3=pltpu.SemaphoreType.REGULAR)
    def bind(self, s, out, src0):
        self.s = s; self.out = out; self.src0 = src0; self.p = Place()
    def entry(self):
        p = self.p; b = pltpu.get_barrier_semaphore()
        for d in (p.partner, p.xn, p.yn, p.near, p.far):
            pl.semaphore_signal(b, inc=1, device_id=d, device_id_type=MESH)
        pl.semaphore_wait(b, 5)
    def rc(self, src, dst, ss, rs, dev):
        return pltpu.make_async_remote_copy(src_ref=src, dst_ref=dst, send_sem=ss, recv_sem=rs, device_id=dev, device_id_type=MESH)
    def k0(self, u):
        s = self.s; i = lax.rem(u, self.N0)
        return self.rc(self.src0(u), s.L0.at[i], s.s0.at[i], s.r0.at[i], self.p.partner)
    def w(self, u): return lax.rem(u, self.NW)
    def k1(self, u):
        s = self.s; w = self.w(u); i = lax.rem(u, self.N1)
        return self.rc(s.W.at[w, pl.ds((1 - self.p.b1) * 192, 192)], s.L1.at[i], s.s1.at[w], s.r1.at[i], self.p.n1)
    def zrow(self, h): return self.p.b1 * 192 + h * 96
    def kz(self, u, h, L, r, dev, j):
        s = self.s; w = self.w(u); i = lax.rem(u, self.NZ)
        return self.rc(s.W.at[w, pl.ds(self.zrow(h), 96)], getattr(s, L).at[i], s.sz.at[w, j], getattr(s, r).at[i], dev)
    def k3(self, u):
        s = self.s; w = self.w(u); i = lax.rem(u, self.N3)
        return self.rc(self.held(u), s.L3.at[i], s.s3.at[w], s.r3.at[i], self.p.n2)
    def held(self, u): return self.s.W.at[self.w(u), pl.ds(self.zrow(self.p.bh), 96)]
    def kl(self, u):
        return pltpu.make_async_copy(self.held(u), self.piece(u, self.p.bh), self.s.lo.at[self.w(u)])
    def piece(self, u, h): return self.out.at[u, self.p.core, pl.ds(self.zrow(h), 96)]
    def kg(self, u, h, r, dev, j, src=None):
        s = self.s
        return self.rc(self.piece(u, h) if src is None else src, self.piece(u, h), s.sg.at[u, j], getattr(s, r).at[u], dev)
    def k6(self, u, h, src=None):
        s = self.s
        return self.rc(self.piece(u, h) if src is None else src, self.piece(u, h), s.s6.at[u, h], s.r6.at[u, h], self.p.n1)
    def k7(self, u):
        s = self.s; o = self.out.at[u, self.p.core]
        return self.rc(o, o, s.s7.at[u], s.r7.at[u], self.p.partner)
    def give(self, name, u, N, dev):
        @pl.when(u + N < self.n)
        def _(): pl.semaphore_signal(getattr(self.s, name), inc=1, device_id=dev, device_id_type=MESH)
    def take(self, name, u, N):
        @pl.when(u >= N)
        def _(): pl.semaphore_wait(getattr(self.s, name), 1)
    def send0(self, u):
        self.take('c0', u, self.N0)
        self.k0(u).start()
    def A(self, u):
        s = self.s; p = self.p; w = self.w(u); i = lax.rem(u, self.N0)
        self.k0(u).wait()
        s.W[w] = s.W[w] + s.L0[i]
        self.give('c0', u, self.N0, p.partner)
        self.take('c1', u, self.N1)
        self.k1(u).start()
    def B(self, u):
        s = self.s; p = self.p; w = self.w(u); i = lax.rem(u, self.N1)
        self.k1(u).wait_recv()
        rows = pl.ds(p.b1 * 192, 192)
        s.W[w, rows] = s.W[w, rows] + s.L1[i]
        self.give('c1', u, self.N1, p.n1)
        @pl.when(p.end)
        def _():
            self.take('cA', u, self.NZ)
            self.kz(u, p.fh, 'LA', 'rA', p.near, 0).start()
    def zadd(self, u, h, L, r):
        s = self.s; w = self.w(u); i = lax.rem(u, self.NZ)
        self.kz(u, h, L, r, self.p.near, 0).wait_recv()
        rows = pl.ds(self.zrow(h), 96)
        s.W[w, rows] = s.W[w, rows] + getattr(s, L)[i]
    def C1(self, u):
        p = self.p
        @pl.when(p.mid)
        def _():
            self.zadd(u, p.fh, 'LA', 'rA')
            self.give('cA', u, self.NZ, p.near)
            self.take('cB', u, self.NZ)
            self.kz(u, p.fh, 'LB', 'rB', p.far, 0).start()
    def C2(self, u):
        p = self.p
        @pl.when(p.mid)
        def _():
            self.zadd(u, p.bh, 'LB', 'rB')
            self.give('cB', u, self.NZ, p.far)
            self.take('cA', u, self.NZ)
            self.kz(u, p.bh, 'LA', 'rA', p.near, 1).start()
    def C3(self, u):
        p = self.p
        @pl.when(p.end)
        def _():
            self.zadd(u, p.bh, 'LA', 'rA')
            self.give('cA', u, self.NZ, p.near)
            self.take('c3', u, self.N3)
            self.k3(u).start()
    def E(self, u):
        s = self.s; p = self.p; w = self.w(u); i = lax.rem(u, self.N3)
        @pl.when(p.end)
        def _():
            self.k3(u).wait()
            rows = pl.ds(self.zrow(p.bh), 96)
            s.W[w, rows] = s.W[w, rows] + s.L3[i]
            self.give('c3', u, self.N3, p.n2)
            self.kg(u, p.bh, 'gA', p.near, 0, self.held(u)).start()
            self.k6(u, p.bh, self.held(u)).start()
            self.kl(u).start()
    def K(self, u):
        p = self.p
        self.k1(u).wait_send()
        self.kz(u, p.fh, 'LB', 'rB', p.far, 0).wait_send()
        @pl.when(p.mid)
        def _(): self.kz(u, p.bh, 'LA', 'rA', p.near, 1).wait_send()
        @pl.when(p.end)
        def _():
            self.kl(u).wait()
            self.kg(u, p.bh, 'gA', p.near, 0, self.held(u)).wait_send()
            self.k6(u, p.bh, self.held(u)).wait_send()
    def F1(self, u):
        p = self.p
        @pl.when(p.mid)
        def _():
            self.kg(u, p.bh, 'gA', p.near, 0).wait_recv()
            self.kg(u, p.bh, 'gB', p.far, 0).start()
            self.k6(u, p.bh).start()
    def F2(self, u):
        p = self.p
        @pl.when(p.mid)
        def _():
            self.kg(u, p.fh, 'gB', p.far, 1).wait_recv()
            self.kg(u, p.fh, 'gA', p.near, 1).start()
            self.k6(u, p.fh).start()
    def F3(self, u):
        p = self.p
        @pl.when(p.end)
        def _():
            self.kg(u, p.fh, 'gA', p.near, 1).wait_recv()
            self.k6(u, p.fh).start()
    def G(self, u):
        for h in (0, 1): self.k6(u, h).wait_recv()
        self.k7(u).start()
    def H(self, u):
        p = self.p
        self.k7(u).wait()
        self.k6(u, p.fh).wait_send()
        @pl.when(p.mid)
        def _():
            self.k6(u, p.bh).wait_send()
            self.kg(u, p.bh, 'gB', p.far, 0).wait_send()
            self.kg(u, p.fh, 'gA', p.near, 1).wait_send()
    def step(self, t):
        for st in ORDER:
            at = t - self.off[st]
            late = at >= self.first + self.pause
            u = jnp.where(late, at - self.pause, at)
            f = getattr(self, st)
            live = (at >= 0) & ((at < self.first) | late) & (u < self.n)
            pl.when(live)(lambda f=f, u=u: f(u))


def spread(values, gain):
    scale = lax.rsqrt(jnp.mean(values * values, axis=-1, keepdims=True) + epsilon)
    return values * scale * gain, scale


def dot_nn(a, b):
    return jnp.dot(a, b, preferred_element_type=jnp.float32)


def dot_nt(a, b):
    return lax.dot_general(a, b, (((1,), (1,)), ((), ())), preferred_element_type=jnp.float32)


def dot_tn(a, b):
    return lax.dot_general(a, b, (((0,), (0,)), ((), ())), preferred_element_type=jnp.float32)


def exact(a, b, dims):
    return lax.dot_general(
        a, b, (dims, ((), ())), precision=lax.Precision.HIGHEST,
        preferred_element_type=jnp.float32,
    )


class Layer:
    def __init__(self, plan, sizes):
        self.plan = plan
        self.z = sizes

    def scratch(self):
        z = self.z
        n, mem, d, ff = z.n, z.mem, z.d, z.ff
        all_rows = n + mem
        b16 = lambda *s: pltpu.VMEM(s, jnp.bfloat16)
        f32 = lambda *s: pltpu.VMEM(s, jnp.float32)
        L = z.L
        pairs = z.heads // 2
        DMA = pltpu.SemaphoreType.DMA
        own = dict(
            xb=b16(n, d), cb=b16(n, d), bk=b16(z.bank, 2, d),
            wq=b16(d, d), wk=b16(d, d), wv=b16(d, d), wo=b16(d, d),
            wib=b16(2, d, d), wub=b16(2, d, d),
            nall=b16(all_rows, d), qs=b16(n, d), ks=b16(all_rows, d), vs=b16(all_rows, d),
            att=b16(n, d), hid=f32(n, d), n2=b16(n, d), n2T=b16(d, n),
            oacc=f32(n, d), gacc=f32(n, d),
            act=b16(n, d), gib=b16(n, d),
            bias=f32(pairs, 2 * L, L), lse=f32(z.rows, 2 * L, 128),
            mq=b16(2 * L, 128), mk=b16(L, 128), mm=b16(z.slots, 128),
            dB=f32(pairs, 2 * L, L), dq=b16(n, d),
            seg=pltpu.VMEM((8, L), jnp.int32),
            sm=f32(16, d), lines=f32(16, 2 * L),
            isem=DMA((16,)), wsem=DMA((2, 2)), osem=DMA((6,)),
        )
        if self.plan is not None:
            own.update(self.plan.scratch())
            own.update(P=f32(self.plan.NP, BLK, BLK), L5=f32(5, 16, d), s5=DMA((5,)), r5=DMA((5,)))
        else:
            own.update(W=f32(2, BLK, BLK), P=f32(2, BLK, BLK), esem=DMA((2,)))
        return own

    def slots(self, u):
        if self.plan is None:
            return lax.rem(u, 2), lax.rem(u, 2)
        return self.plan.w(u), lax.rem(u, self.plan.NP)

    def emit(self, u):
        s = self.s
        if self.plan is not None:
            self.plan.send0(u)
            return
        w, p = self.slots(u)
        one = pltpu.make_async_copy(s.W.at[w], self.out.at[u, 0], s.esem.at[0])
        two = pltpu.make_async_copy(s.P.at[p], self.out.at[u, 1], s.esem.at[1])
        one.start()
        two.start()
        one.wait()
        two.wait()

    def emit_cols(self, u, value):
        s = self.s
        w, p = self.slots(u)

        @pl.when(self.core == 0)
        def _():
            s.W[w] = value[:, :BLK]
            s.P[p] = value[:, BLK:]

        @pl.when(self.core != 0)
        def _():
            s.W[w] = value[:, BLK:]
            s.P[p] = value[:, :BLK]

        self.emit(u)

    def step(self, t):
        if self.plan is not None:
            self.plan.step(t)

    def kernel(self, names, *refs):
        z = self.z
        ins = SimpleNamespace(**dict(zip(INS, refs)))
        outs = SimpleNamespace(**dict(zip(OUTS, refs[18:])))
        s = SimpleNamespace(**dict(zip(names, refs[24:])))
        s.gb, s.dk, s.dv = s.wub.at[0], s.wib.at[0], s.wib.at[1]
        s.dkm, s.dvm = s.wub.at[1, pl.ds(0, z.mem)], s.wub.at[1, pl.ds(z.mem, z.mem)]
        self.s, self.ins, self.outs, self.out = s, ins, outs, outs.out
        if self.plan is not None:
            self.plan.bind(s, outs.out, lambda u: s.P.at[lax.rem(u, self.plan.NP)])
            self.core = self.plan.p.core
        else:
            self.core = jnp.int32(0)
        self.load()
        if self.plan is not None:
            self.plan.entry()
        self.front()
        self.ffn()
        self.middle()
        self.attn_back()
        self.back()

    def load(self):
        s, i, z = self.s, self.ins, self.z
        n0 = z.n0
        cp = pltpu.make_async_copy
        sem = lambda k: s.isem.at[k]
        d = z.d
        self.c = SimpleNamespace(
            x0=cp(i.tok, s.xb.at[pl.ds(0, n0)], sem(0)),
            x1=cp(i.side, s.xb.at[pl.ds(n0, z.n - n0)], sem(1)),
            bk=cp(i.bank, s.bk, sem(2)),
            wq=cp(i.wq, s.wq, sem(3)), wk=cp(i.wk, s.wk, sem(4)),
            wv=cp(i.wv, s.wv, sem(5)), wo=cp(i.wo, s.wo, sem(6)),
            c0=cp(i.cot, s.cb.at[pl.ds(0, n0)], sem(7)),
            c1=cp(i.scot, s.cb.at[pl.ds(n0, z.n - n0)], sem(8)),
        )
        for k in ("x0", "x1", "bk", "wq", "wk", "wv", "wo"):
            getattr(self.c, k).start()
        for k in self.wcopy(0):
            k.start()
        self.c.c0.start()
        self.c.c1.start()

    def wcopy(self, c):
        s, i, d = self.s, self.ins, self.z.d
        slot = lax.rem(c, 2) if not isinstance(c, int) else c % 2
        cols = pl.ds(c * d if isinstance(c, int) else pl.multiple_of(c * d, d), d)
        return (
            pltpu.make_async_copy(i.wi.at[:, cols], s.wib.at[slot], s.wsem.at[slot, 0]),
            pltpu.make_async_copy(i.wu.at[cols, :], s.wub.at[slot], s.wsem.at[slot, 1]),
        )

    def tile(self, k):
        return pl.ds(pl.multiple_of(k * 256, 256), 256)

    def memory(self):
        s, z = self.s, self.z
        items = z.mem // 2
        picked = self.ins.idx[...].astype(jnp.float32).reshape(z.main * z.questions, z.top)
        item = lax.broadcasted_iota(jnp.int32, (items, z.main * z.questions), 0)
        question = lax.broadcasted_iota(jnp.int32, (items, z.main * z.questions), 1)
        mine = (item >= question * z.top) & (item < (question + 1) * z.top)
        lines = exact(jnp.where(mine, 1.0, 0.0), picked, ((1,), (0,)))
        base = jnp.sum(jnp.where(mine, question * z.top, 0).astype(jnp.float32), 1, keepdims=True)
        place = lax.broadcasted_iota(jnp.int32, (items, z.top), 0).astype(jnp.float32) - base
        lane = lax.broadcasted_iota(jnp.int32, (items, z.top), 1).astype(jnp.float32)
        index = jnp.sum(jnp.where(place == lane, lines, 0.0), axis=1, keepdims=True)
        entries = lax.broadcasted_iota(jnp.int32, (items, z.bank), 1).astype(jnp.float32)
        hot = jnp.where(entries == index, 1.0, 0.0).astype(jnp.bfloat16)
        return tuple(dot_nn(hot, s.bk[:, part, :]) for part in range(2))

    def mem_rows(self, r, part):
        z = self.z
        return pl.ds(z.n + r * z.slots + part * (z.slots // 2), z.slots // 2)

    def heads(self, value):
        lane = lax.broadcasted_iota(jnp.int32, (1, 128), 1)
        first = jnp.where(lane < 64, 1.0, 0.0).astype(jnp.bfloat16)
        second = jnp.where(lane < 64, 0.0, 1.0).astype(jnp.bfloat16)
        return jnp.concatenate([value * first, value * second], axis=0)

    def merge(self, value):
        rows = value.shape[0] // 2
        lane = lax.broadcasted_iota(jnp.int32, (rows, 128), 1)
        return jnp.where(lane < 64, value[:rows], value[rows:])

    def slot_mask(self):
        s, z = self.s, self.z
        lane = lax.broadcasted_iota(jnp.int32, (z.slots, 128), 1)
        slot = lax.broadcasted_iota(jnp.int32, (z.slots, 128), 0)
        slot = jnp.where(slot >= z.slots // 2, slot - z.slots // 2, slot)
        each = z.slots // 2 // z.questions
        hit = (slot >= lane * each) & (slot < (lane + 1) * each)
        s.mm[...] = jnp.where(hit, 1.0, 0.0).astype(jnp.bfloat16)

    def masks(self, r):
        s, z = self.s, self.z
        L = z.L
        row = s.seg[pl.ds(r, 1), :].astype(jnp.float32)
        down = jnp.broadcast_to(row, (L, L)).T[:, :128]
        lane = lax.broadcasted_iota(jnp.int32, (L, 128), 1)
        own = down == lane.astype(jnp.float32)
        s.mk[...] = jnp.where(own, 1.0, 0.0).astype(jnp.bfloat16)
        outside = jnp.where(own | (lane >= z.questions), 0.0, masked_value).astype(jnp.bfloat16)
        s.mq[pl.ds(0, L), :] = outside
        s.mq[pl.ds(L, L), :] = outside

    def spans(self, r, j):
        z = self.z
        rows = pl.ds(pl.multiple_of(r * z.L, z.L), z.L)
        mem = pl.ds(pl.multiple_of(z.n + r * z.slots, 32), z.slots)
        lanes = pl.ds(pl.multiple_of(j * 128, 128), 128)
        return rows, mem, lanes

    def scores(self, r, j, has_mem):
        s = self.s
        rows, mem, lanes = self.spans(r, j)
        q2 = self.heads(s.qs[rows, lanes])
        wide = jnp.concatenate([q2, s.mq[...]], axis=1)
        st = dot_nt(wide, jnp.concatenate([s.ks[rows, lanes], s.mk[...]], axis=1)) + s.bias[j]
        sm = None
        if has_mem:
            sm = dot_nt(wide, jnp.concatenate([s.ks[mem, lanes], s.mm[...]], axis=1))
        return q2, st, sm

    def fwd_pair(self, r, j, has_mem):
        s, z = self.s, self.z
        rows, mem, lanes = self.spans(r, j)
        q2, st, sm = self.scores(r, j, has_mem)
        top = jnp.max(st, axis=1, keepdims=True)
        if has_mem:
            top = jnp.maximum(top, jnp.max(sm, axis=1, keepdims=True))
        et = jnp.exp(st - top).astype(jnp.bfloat16)
        ones = jnp.ones((z.L, 128), jnp.bfloat16)
        mixed = dot_nn(et, jnp.concatenate([s.vs[rows, lanes], ones], axis=1))
        if has_mem:
            em = jnp.exp(sm - top).astype(jnp.bfloat16)
            ones = ones[: z.slots]
            mixed = mixed + dot_nn(em, jnp.concatenate([s.vs[mem, lanes], ones], axis=1))
        total = mixed[:, 128:]
        s.att[rows, lanes] = self.merge(mixed[:, :128] / total).astype(jnp.bfloat16)
        lane = lax.broadcasted_iota(jnp.int32, (2 * z.L, 128), 1)
        s.lse[r] = jnp.where(lane == j, top + jnp.log(total), s.lse[r])

    def front(self):
        s, z, i = self.s, self.z, self.ins
        L, d, n = z.L, z.d, z.n
        offs = i.offs[...]
        spots = offs.shape[1]
        bucket = lax.broadcasted_iota(jnp.int32, (i.btab.shape[1], spots), 0)
        hot = jnp.where(bucket == offs, 1.0, 0.0)
        line = exact(i.btab[...], hot, ((1,), (0,)))
        line = jnp.concatenate([line, jnp.zeros((line.shape[0], 2 * L - spots), jnp.float32)], 1)
        for h in range(z.heads):
            wide = jnp.broadcast_to(line[h : h + 1], (L, 2 * L))
            turned = pltpu.roll(wide, L + 1, 1, stride=1, stride_axis=0)
            s.bias[h // 2, pl.ds((h % 2) * L, L), :] = turned[:, :L]
        self.slot_mask()
        s.seg[pl.ds(0, z.main), :] = i.segm[...]
        s.seg[pl.ds(z.main, z.rows - z.main), :] = i.segs[...]
        g1 = i.g1[...].reshape(1, d)
        self.c.x0.wait()
        self.c.x1.wait()

        def norm_row(r, carry):
            rows = pl.ds(pl.multiple_of(r * L, L), L)
            s.nall[rows, :] = spread(s.xb[rows, :].astype(jnp.float32), g1)[0].astype(jnp.bfloat16)
            return carry

        lax.fori_loop(0, z.rows, norm_row, 0)
        self.c.bk.wait()
        half = z.slots // 2
        for part, memory in enumerate(self.memory()):
            normed = spread(memory, g1)[0].astype(jnp.bfloat16)
            for r in range(z.main):
                s.nall[self.mem_rows(r, part), :] = normed[r * half : (r + 1) * half]
        for k in ("wq", "wk", "wv"):
            getattr(self.c, k).wait()

        def project(k, carry):
            cols = self.tile(k)
            s.qs[:, cols] = dot_nn(s.nall[pl.ds(0, n), :], s.wq[:, cols]).astype(jnp.bfloat16)
            s.ks[:, cols] = dot_nn(s.nall[...], s.wk[:, cols]).astype(jnp.bfloat16)
            s.vs[:, cols] = dot_nn(s.nall[...], s.wv[:, cols]).astype(jnp.bfloat16)
            return carry

        lax.fori_loop(0, d // 256, project, 0)
        pairs = z.heads // 2

        def row(has_mem, r, carry):
            self.masks(r)

            def pair(j, inner):
                self.fwd_pair(r, j, has_mem)
                return inner

            return lax.fori_loop(0, pairs, pair, carry, unroll=FWD_UNROLL)

        lax.fori_loop(0, z.main, functools.partial(row, True), 0)
        lax.fori_loop(z.main, z.rows, functools.partial(row, False), 0)
        self.c.wo.wait()

        def attn_out(k, carry):
            cols = self.tile(k)
            s.hid[:, cols] = s.xb[:, cols].astype(jnp.float32) + dot_nn(s.att[...], s.wo[:, cols])
            return carry

        lax.fori_loop(0, d // 256, attn_out, 0)
        g2 = i.g2[...].reshape(1, d)

        def norm_two(r, carry):
            rows = pl.ds(pl.multiple_of(r * L, L), L)
            s.n2[rows, :] = spread(s.hid[rows, :], g2)[0].astype(jnp.bfloat16)
            return carry

        lax.fori_loop(0, z.rows, norm_two, 0)

    def ffn(self):
        s, z, i = self.s, self.z, self.ins
        d, n = z.d, z.n
        chunks = z.ff // d
        self.c.c0.wait()
        self.c.c1.wait()
        root = 0.7978845608028654

        def chunk(c, carry):
            slot = lax.rem(c, 2)
            for k in self.wcopy(c):
                k.wait()

            @pl.when(c + 1 < chunks)
            def _():
                for k in self.wcopy(c + 1):
                    k.start()

            def part(k, inner):
                cols = self.tile(k)
                v = dot_nn(s.n2[...], s.wib[slot, :, cols])
                ga = dot_nt(s.cb[...], s.wub[slot, cols, :])
                square = v * v
                th = jnp.tanh(root * v * (1.0 + 0.044715 * square))
                half = 0.5 * (1.0 + th)
                s.act[:, cols] = (v * half).astype(jnp.bfloat16)
                slope = half + (0.5 * root) * v * (1.0 - th * th) * (1.0 + 0.134145 * square)
                s.gib[:, cols] = (ga * slope).astype(jnp.bfloat16)

                @pl.when(k == 1)
                def _():
                    outer(0, inner)

                return inner

            def outer(k, inner):
                u = 4 * c + k
                cols = pl.ds(k * BLK, BLK)
                self.emit_cols(u, dot_tn(s.act[:, cols], s.cb[...]))
                self.step(u)
                return inner

            def gather(k, inner):
                cols = self.tile(k)
                po = dot_nn(s.act[...], s.wub[slot, :, cols])
                pg = dot_nt(s.gib[...], s.wib[slot, cols, :])

                @pl.when(c == 0)
                def _():
                    s.oacc[:, cols] = po
                    s.gacc[:, cols] = pg

                @pl.when(c > 0)
                def _():
                    s.oacc[:, cols] = s.oacc[:, cols] + po
                    s.gacc[:, cols] = s.gacc[:, cols] + pg

                return inner

            lax.fori_loop(0, d // 256, part, 0)
            lax.fori_loop(0, d // 256, gather, 0)
            outer(1, 0)

            @pl.when(c == 0)
            def _():
                s.n2T[...] = s.n2[...].T

            def inner_grad(k, inner):
                self.inner_unit(4 * c + 2 + k, k)
                self.step(4 * c + 2 + k)
                return inner

            @pl.when(c + 1 < chunks)
            def _():
                lax.fori_loop(0, 2, inner_grad, 0)

            return carry

        lax.fori_loop(0, chunks, chunk, 0)

    def inner_unit(self, u, k):
        s = self.s
        w, p = self.slots(u)
        cols = pl.ds(pl.multiple_of(k * BLK, BLK), BLK)
        mine = pl.ds(pl.multiple_of(self.core * BLK, BLK), BLK)
        other = pl.ds(pl.multiple_of((1 - self.core) * BLK, BLK), BLK)
        s.P[p] = dot_nn(s.n2T[other, :], s.gib[:, cols])
        s.W[w] = dot_nn(s.n2T[mine, :], s.gib[:, cols])
        self.emit(u)

    def out_unit(self, u, k):
        s = self.s
        cols = pl.ds(pl.multiple_of(k * BLK, BLK), BLK)
        self.emit_cols(u, dot_tn(s.att[:, cols], s.gb[...]))

    def middle(self):
        s, z, i = self.s, self.z, self.ins
        L, d, n, n0 = z.L, z.d, z.n, z.n0
        g2 = i.g2[...].reshape(1, d)

        def row(r, gain):
            rows = pl.ds(pl.multiple_of(r * L, L), L)
            hid = s.hid[rows, :]
            s.dq[rows, :] = (hid + s.oacc[rows, :]).astype(jnp.bfloat16)
            scale = lax.rsqrt(jnp.mean(hid * hid, axis=-1, keepdims=True) + epsilon)
            grad = s.gacc[rows, :]
            gain = gain + jnp.sum(grad * hid * scale, axis=0, keepdims=True)
            u = grad * g2
            average = jnp.mean(u * hid, axis=-1, keepdims=True)
            full = s.cb[rows, :].astype(jnp.float32) + scale * u - hid * (scale * scale * scale * average)
            s.gacc[rows, :] = full
            s.gb[rows, :] = full.astype(jnp.bfloat16)
            return gain

        gain = lax.fori_loop(0, z.rows, row, jnp.zeros((1, d), jnp.float32))
        s.sm[...] = jnp.zeros((16, d), jnp.float32)
        s.sm[pl.ds(13, 1), :] = gain
        self.o = (
            pltpu.make_async_copy(s.dq.at[pl.ds(0, n0)], self.outs.y, s.osem.at[0]),
            pltpu.make_async_copy(s.dq.at[pl.ds(n0, n - n0)], self.outs.sy, s.osem.at[1]),
        )
        for k in self.o:
            k.start()

        def back(k, carry):
            cols = self.tile(k)
            s.n2[:, cols] = dot_nt(s.gb[...], s.wo[cols, :]).astype(jnp.bfloat16)
            return carry

        lax.fori_loop(0, d // 256, back, 0)
        for k in self.o:
            k.wait()

    def bwd_pair(self, r, j, has_mem):
        s, z = self.s, self.z
        rows, mem, lanes = self.spans(r, j)
        q2, st, sm = self.scores(r, j, has_mem)
        lane = lax.broadcasted_iota(jnp.int32, (2 * z.L, 128), 1)
        lse = jnp.sum(jnp.where(lane == j, s.lse[r], 0.0), axis=1, keepdims=True)
        d2 = self.heads(s.n2[rows, lanes])
        pt = jnp.exp(st - lse)
        gt = dot_nt(d2, s.vs[rows, lanes])
        delta = jnp.sum(pt * gt, axis=1, keepdims=True)
        if has_mem:
            pm = jnp.exp(sm - lse)
            gm = dot_nt(d2, s.vs[mem, lanes])
            delta = delta + jnp.sum(pm * gm, axis=1, keepdims=True)
        dst = (pt * (gt - delta)).astype(jnp.bfloat16)
        grad_q = dot_nn(dst, s.ks[rows, lanes])
        s.dk[rows, lanes] = dot_tn(dst, q2).astype(jnp.bfloat16)
        s.dv[rows, lanes] = dot_tn(pt.astype(jnp.bfloat16), d2).astype(jnp.bfloat16)
        if has_mem:
            dsm = (pm * (gm - delta)).astype(jnp.bfloat16)
            grad_q = grad_q + dot_nn(dsm, s.ks[mem, lanes])
            slot = pl.ds(pl.multiple_of(r * z.slots, 32), z.slots)
            s.dkm[slot, lanes] = dot_tn(dsm, q2).astype(jnp.bfloat16)
            s.dvm[slot, lanes] = dot_tn(pm.astype(jnp.bfloat16), d2).astype(jnp.bfloat16)
        s.dq[rows, lanes] = self.merge(grad_q).astype(jnp.bfloat16)
        s.dB[j] = s.dB[j] + dst.astype(jnp.float32)

    def attn_back(self):
        s, z = self.s, self.z
        pairs = z.heads // 2
        first = 4 * (z.ff // z.d) - 2

        def clear(j, carry):
            s.dB[j] = jnp.zeros(s.dB.shape[1:], jnp.float32)
            return carry

        lax.fori_loop(0, pairs, clear, 0)

        def row(has_mem, r, carry):
            self.masks(r)

            def few(g, inner):
                def pair(k, last):
                    self.bwd_pair(r, g * 3 + k, has_mem)
                    return last

                lax.fori_loop(0, 3, pair, 0, unroll=BWD_UNROLL)
                if has_mem:
                    u = first + 2 * r + g

                    @pl.when(r == 0)
                    def _():
                        self.out_unit(u, g)

                    @pl.when(r > 0)
                    def _():
                        self.inner_unit(u, g)

                    self.step(u)
                return inner

            return lax.fori_loop(0, pairs // 3, few, carry)

        lax.fori_loop(0, z.main, functools.partial(row, True), 0)
        lax.fori_loop(z.main, z.rows, functools.partial(row, False), 0)

    def back(self):
        s, z, i = self.s, self.z, self.ins
        L, d, n, n0, mem = z.L, z.d, z.n, z.n0, z.mem
        first = 4 * (z.ff // d) + 2
        tok, mrows = pl.ds(0, n), pl.ds(n, mem)
        def difference(j):
            for side in range(2):
                grid = s.dB[j, pl.ds(side * L, L), :]
                wide = jnp.concatenate([grid, jnp.zeros((L, L), jnp.float32)], axis=1)
                wide = pltpu.roll(wide, L - 1, 1)
                half = L // 2
                while half:
                    wide = wide[:half] + pltpu.roll(wide[half:], 2 * L - half, 1)
                    half = half // 2
                s.lines[pl.ds(2 * j + side, 1), :] = wide

        g1 = i.g1[...].reshape(1, d)

        def grads(k):
            cols = self.tile(k)
            s.hid[:, cols] = (
                dot_nt(s.dq[...], s.wq[cols, :])
                + dot_nt(s.dk[...], s.wk[cols, :])
                + dot_nt(s.dv[...], s.wv[cols, :])
            )
            s.oacc[pl.ds(0, mem), cols] = dot_nt(s.dkm[...], s.wk[cols, :]) + dot_nt(
                s.dvm[...], s.wv[cols, :]
            )

        def row(r):
            rows = pl.ds(pl.multiple_of(r * L, L), L)
            x = s.xb[rows, :].astype(jnp.float32)
            scale = lax.rsqrt(jnp.mean(x * x, axis=-1, keepdims=True) + epsilon)
            grad = s.hid[rows, :]
            part = jnp.sum(grad * x * scale, axis=0, keepdims=True)
            s.sm[pl.ds(12, 1), :] = s.sm[pl.ds(12, 1), :] + part
            v = grad * g1
            average = jnp.mean(v * x, axis=-1, keepdims=True)
            full = s.gacc[rows, :] + scale * v - x * (scale * scale * scale * average)
            s.gb[rows, :] = full.astype(jnp.bfloat16)

        tiles = d // 256

        def rest_of(j):
            difference(j)
            pl.when(j < tiles)(lambda: grads(j))
            pl.when(j >= tiles)(lambda: row(j - tiles))

        u = first
        for grad, grad_mem in ((s.dq, None), (s.dk, s.dkm), (s.dv, s.dvm)):
            def one(k, carry, grad=grad, grad_mem=grad_mem, u=u):
                cols = pl.ds(pl.multiple_of(k * BLK, BLK), BLK)
                value = dot_tn(s.nall[tok, cols], grad[...])
                if grad_mem is not None:
                    value = value + dot_tn(s.nall[mrows, cols], grad_mem[...])
                self.emit_cols(u + k, value)
                self.step(u + k)
                rest_of(u - first + k)
                return carry

            lax.fori_loop(0, 2, one, 0)
            u = u + 2
        t = first + 6
        gain = s.sm[pl.ds(12, 1), :]
        late = (
            pltpu.make_async_copy(s.gb.at[pl.ds(0, n0)], self.outs.gt, s.osem.at[2]),
            pltpu.make_async_copy(s.gb.at[pl.ds(n0, n - n0)], self.outs.sgt, s.osem.at[3]),
        )
        for k in late:
            k.start()
        half = z.slots // 2
        for part, memory in enumerate(self.memory()):
            scale = lax.rsqrt(jnp.mean(memory * memory, axis=-1, keepdims=True) + epsilon)
            unit = memory * scale
            for r in range(z.main):
                grad = s.oacc[pl.ds(r * z.slots + part * half, half), :]
                gain = gain + jnp.sum(grad * unit[r * half : (r + 1) * half], axis=0, keepdims=True)
        s.sm[pl.ds(12, 1), :] = gain
        offs = i.offs[...]
        bucket = lax.broadcasted_iota(jnp.int32, (128, offs.shape[1]), 0)
        hot = jnp.where(bucket == offs, 1.0, 0.0)
        s.sm[pl.ds(0, z.heads), pl.ds(0, 128)] = exact(
            s.lines[pl.ds(0, z.heads), pl.ds(0, offs.shape[1])], hot, ((1,), (1,))
        )
        if self.plan is not None:
            self.finish(t)
        for k in late:
            k.wait()
        self.outs.small[...] = s.sm[...]

    def steps_from(self, t, count):
        def one(k, carry):
            self.step(k)
            return carry

        lax.fori_loop(t, t + count, one, 0)
        return t + count

    def finish(self, t):
        plan, s = self.plan, self.s
        p = plan.p
        peers = (p.partner, p.xn, p.yn, p.near, p.far)
        for k, dev in enumerate(peers):
            copy = plan.rc(s.sm, s.L5.at[k], s.s5.at[k], s.r5.at[k], dev)
            copy.start()
            t = self.steps_from(t, SMALL_GAP)
            copy.wait()
            s.sm[...] = s.sm[...] + s.L5[k]

        def rest(k, carry):
            self.step(k)
            return carry

        lax.fori_loop(t, plan.steps, rest, 0)


def place_units(
    sizes, units, y, gt, sy, sgt, small,
    oy, ogt, osy, osgt, wq, wk, wv, wo, wi, wu, gb, gg1, gg2,
    hold, vy, vgt, vsy, vsgt, sem, late, rsem,
):
    d, ff = sizes.d, sizes.ff
    copies = []

    def put(u, half, ref, row, col):
        k = len(copies)
        place = ref.at[pl.ds(row, BLK), pl.ds(col, BLK)]
        copies.append(
            (
                pltpu.make_async_copy(units.at[u, half], hold.at[k], sem.at[k]),
                pltpu.make_async_copy(hold.at[k], place, late.at[k]),
            )
        )

    for c in range(ff // d):
        for k in range(2):
            for half in range(2):
                put(4 * c + k, half, wu, c * d + k * BLK, half * BLK)
                after = 2 if c + 1 < ff // d else 4
                put(4 * c + after + k, half, wi, half * BLK, c * d + k * BLK)
    for k in range(2):
        for half in range(2):
            put(4 * (ff // d) - 2 + k, half, wo, k * BLK, half * BLK)
    u = 4 * (ff // d) + 2
    for ref in (wq, wk, wv):
        for k in range(2):
            for half in range(2):
                put(u + k, half, ref, k * BLK, half * BLK)
        u = u + 2
    for k, (src, mid, dst) in enumerate(
        ((y, vy, oy), (gt, vgt, ogt), (sy, vsy, osy), (sgt, vsgt, osgt))
    ):
        copies.append(
            (
                pltpu.make_async_copy(src, mid, rsem.at[k, 0]),
                pltpu.make_async_copy(mid, dst, rsem.at[k, 1]),
            )
        )
    for fetch, store in copies:
        fetch.start()
    heads, buckets = gb.shape
    gb[...] = small[pl.ds(0, heads), pl.ds(0, buckets)]
    gg1[...] = small[12, :]
    gg2[...] = small[13, :]
    for fetch, store in copies:
        fetch.wait()
        store.start()
    for fetch, store in copies:
        store.wait()


def body(
    remote,
    tokens,
    segments,
    picked,
    offsets,
    memory_bank,
    side_tokens,
    side_segments,
    w_query,
    w_key,
    w_value,
    w_attn_out,
    w_inner,
    w_outer,
    bias_table,
    gain_one,
    gain_two,
    cotangent,
    side_cotangent,
):
    d, ff = w_inner.shape
    main, L = segments.shape
    heads = bias_table.shape[1]
    buckets = bias_table.shape[0]
    n0, n1 = tokens.shape[0], side_tokens.shape[0]
    slots = picked.shape[1] * picked.shape[2] * 2
    sizes = SimpleNamespace(
        n=n0 + n1, n0=n0, d=d, ff=ff, L=L, main=main, rows=main + side_segments.shape[0],
        heads=heads, slots=slots, mem=main * slots, questions=picked.shape[1], top=picked.shape[2],
        bank=memory_bank.shape[0],
    )
    units = 4 * (ff // d) + 8
    plan = Comm(units, GAPS) if remote else None
    layer = Layer(plan, sizes)
    scratch = layer.scratch()
    hbm = pl.BlockSpec(memory_space=pl.ANY)
    vmem = pl.BlockSpec(memory_space=pltpu.VMEM)
    shape = jax.ShapeDtypeStruct
    joined, output, grad_tokens, side_output, grad_side, small = pl.pallas_call(
        functools.partial(layer.kernel, list(scratch)),
        out_shape=(
            shape((units, 2, BLK, BLK), jnp.float32),
            shape(tokens.shape, jnp.bfloat16),
            shape(tokens.shape, jnp.bfloat16),
            shape(side_tokens.shape, jnp.bfloat16),
            shape(side_tokens.shape, jnp.bfloat16),
            shape((16, d), jnp.float32),
        ),
        in_specs=[hbm] * 11 + [vmem] * 7,
        out_specs=(hbm,) * 5 + (vmem,),
        scratch_shapes=list(scratch.values()),
        compiler_params=pltpu.CompilerParams(
            collective_id=0 if remote else None, has_side_effects=True, vmem_limit_bytes=VMEM_LIMIT
        ),
    )(
        tokens, side_tokens, cotangent, side_cotangent,
        memory_bank, w_query, w_key, w_value, w_attn_out, w_inner, w_outer,
        picked, segments, side_segments, offsets.reshape(1, -1), bias_table.T,
        gain_one, gain_two,
    )
    if not remote:
        joined = lax.psum(joined, AXES)
        small = lax.psum(small, AXES)
    square = shape((d, d), jnp.float32)
    wide, narrow = shape(tokens.shape, jnp.bfloat16), shape(side_tokens.shape, jnp.bfloat16)
    gain = shape((d,), jnp.float32)
    hold = pltpu.VMEM(tokens.shape, jnp.bfloat16), pltpu.VMEM(side_tokens.shape, jnp.bfloat16)
    outs = pl.pallas_call(
        functools.partial(place_units, sizes),
        out_shape=(
            wide, wide, narrow, narrow, square, square, square, square,
            shape((d, ff), jnp.float32), shape((ff, d), jnp.float32),
            shape((heads, buckets), jnp.float32), gain, gain,
        ),
        in_specs=[hbm] * 5 + [vmem],
        out_specs=(hbm,) * 10 + (vmem,) * 3,
        scratch_shapes=[
            pltpu.VMEM((2 * units, BLK, BLK), jnp.float32),
            hold[0], hold[0], hold[1], hold[1],
            pltpu.SemaphoreType.DMA((2 * units,)),
            pltpu.SemaphoreType.DMA((2 * units,)),
            pltpu.SemaphoreType.DMA((4, 2)),
        ],
        compiler_params=pltpu.CompilerParams(vmem_limit_bytes=VMEM_LIMIT),
    )(joined, output, grad_tokens, side_output, grad_side, small)
    output, grad_tokens, side_output, grad_side = outs[:4]
    return (output, grad_tokens, side_output, grad_side) + tuple(outs[4:10]) + (outs[10].T,) + tuple(outs[11:])


INS = ["tok", "side", "cot", "scot", "bank", "wq", "wk", "wv", "wo", "wi", "wu"]
INS = INS + ["idx", "segm", "segs", "offs", "btab", "g1", "g2"]
OUTS = ["out", "y", "gt", "sy", "sgt", "small"]
VMEM_LIMIT = 63 * 2**20
FWD_UNROLL = 6
BWD_UNROLL = 1
SMALL_GAP = 3


def solution(mesh):
    in_specs = (
        P(AXES, None),
        P(AXES, None),
        P(AXES, None, None),
        P(),
        P(),
        P(AXES, None),
        P(AXES, None),
        P(),
        P(),
        P(),
        P(),
        P(),
        P(),
        P(),
        P(),
        P(),
        P(AXES, None),
        P(AXES, None),
    )
    out_specs = (
        P(AXES, None),
        P(AXES, None),
        P(AXES, None),
        P(AXES, None),
        P(),
        P(),
        P(),
        P(),
        P(),
        P(),
        P(),
        P(),
        P(),
    )
    remote = dict(mesh.shape) == {'dp': 4, 'replica': 8}
    return jax.shard_map(functools.partial(body, remote), mesh=mesh, in_specs=in_specs, out_specs=out_specs, check_vma=False)
```

```python
import functools
from types import SimpleNamespace

import jax
import jax.numpy as jnp
from jax import lax
from jax.experimental import pallas as pl
from jax.experimental.pallas import tpu as pltpu
from jax.sharding import PartitionSpec as P

MESH = pl.DeviceIdType.MESH
epsilon = 1e-06
masked_value = -1e30
AXES = ("dp", "replica")

BLK = 384
STG = ["P", "A", "B", "C1", "C2", "C3", "E", "F1", "F2", "F3", "G", "H"]
GAPS = (1, 3, 1, 1, 2, 3, 2, 1, 2, 3, 1)
KEEP = 3
ORDER = STG[1:] + ["K"]
def offsets_of(gaps):
    o, a = {}, 0
    for s, g in zip(STG, (0,)+tuple(gaps)):
        a += g; o[s] = a
    return o

class Place:
    def __init__(self):
        dp = lax.axis_index("dp"); rep = lax.axis_index("replica")
        self.core = lax.rem(dp, 2); x = dp // 2; z = rep // 2; y = lax.rem(rep, 2)
        c = self.core
        self.partner = (dp + 1 - 2 * c, rep)
        xn = (dp + 2 - 4 * x, rep); yn = (dp, rep + 1 - 2 * y)
        pick = lambda a, b: tuple(jnp.where(c == 0, i, j) for i, j in zip(a, b))
        self.xn = xn; self.yn = yn
        self.n1 = pick(xn, yn); self.n2 = pick(yn, xn)
        self.b1 = jnp.where(c == 0, x, y); self.b2 = jnp.where(c == 0, y, x)
        self.end = (z == 0) | (z == 3)
        self.mid = (z == 1) | (z == 2)
        left = jnp.where(z < 2, 1, 0)
        near = z + 1 - 2 * lax.rem(z, 2)
        far = 3 - z
        self.near = (dp, near * 2 + y)
        self.far = (dp, far * 2 + y)
        self.fh = left
        self.bh = 1 - left

class Comm:
    NP = 4; N0 = 4; N1 = 8; NZ = 6; N3 = 6
    def __init__(self, units, gaps, first=0, pause=0):
        self.n = units; self.off = offsets_of(gaps)
        self.off["K"] = self.off["E"] + KEEP
        self.NW = self.off["K"] + 1
        self.first = first; self.pause = pause
        self.steps = units + pause + self.off['H']
    def scratch(self):
        n = self.n; D = pltpu.SemaphoreType.DMA; V = lambda *s: pltpu.VMEM(s, jnp.float32)
        return dict(
            W=V(self.NW, BLK, BLK), L0=V(self.N0, BLK, BLK), L1=V(self.N1, BLK//2, BLK),
            LA=V(self.NZ, BLK//4, BLK), LB=V(self.NZ, BLK//4, BLK), L3=V(self.N3, BLK//4, BLK),
            s0=D((self.N0,)), r0=D((self.N0,)), s1=D((self.NW,)), r1=D((self.N1,)),
            sz=D((self.NW, 2)), rA=D((self.NZ,)), rB=D((self.NZ,)), s3=D((self.NW,)), r3=D((self.N3,)),
            lo=D((self.NW,)), sg=D((n, 2)), gA=D((n,)), gB=D((n,)), s6=D((n, 2)), r6=D((n, 2)), s7=D((n, 2)), r7=D((n, 2)),
            c0=pltpu.SemaphoreType.REGULAR, c1=pltpu.SemaphoreType.REGULAR,
            cA=pltpu.SemaphoreType.REGULAR, cB=pltpu.SemaphoreType.REGULAR, c3=pltpu.SemaphoreType.REGULAR)
    def bind(self, s, out, src0):
        self.s = s; self.out = out; self.src0 = src0; self.p = Place()
    def entry(self):
        p = self.p; b = pltpu.get_barrier_semaphore()
        for d in (p.partner, p.xn, p.yn, p.near, p.far):
            pl.semaphore_signal(b, inc=1, device_id=d, device_id_type=MESH)
        pl.semaphore_wait(b, 5)
    def rc(self, src, dst, ss, rs, dev):
        return pltpu.make_async_remote_copy(src_ref=src, dst_ref=dst, send_sem=ss, recv_sem=rs, device_id=dev, device_id_type=MESH)
    def k0(self, u):
        s = self.s; i = lax.rem(u, self.N0)
        return self.rc(self.src0(u), s.L0.at[i], s.s0.at[i], s.r0.at[i], self.p.partner)
    def w(self, u): return lax.rem(u, self.NW)
    def k1(self, u):
        s = self.s; w = self.w(u); i = lax.rem(u, self.N1)
        return self.rc(s.W.at[w, pl.ds((1 - self.p.b1) * 192, 192)], s.L1.at[i], s.s1.at[w], s.r1.at[i], self.p.n1)
    def zrow(self, h): return self.p.b1 * 192 + h * 96
    def kz(self, u, h, L, r, dev, j):
        s = self.s; w = self.w(u); i = lax.rem(u, self.NZ)
        return self.rc(s.W.at[w, pl.ds(self.zrow(h), 96)], getattr(s, L).at[i], s.sz.at[w, j], getattr(s, r).at[i], dev)
    def k3(self, u):
        s = self.s; w = self.w(u); i = lax.rem(u, self.N3)
        return self.rc(self.held(u), s.L3.at[i], s.s3.at[w], s.r3.at[i], self.p.n2)
    def held(self, u): return self.s.W.at[self.w(u), pl.ds(self.zrow(self.p.bh), 96)]
    def kl(self, u):
        return pltpu.make_async_copy(self.held(u), self.piece(u, self.p.bh), self.s.lo.at[self.w(u)])
    def piece(self, u, h): return self.out.at[u, self.p.core, pl.ds(self.zrow(h), 96)]
    def kg(self, u, h, r, dev, j, src=None):
        s = self.s
        return self.rc(self.piece(u, h) if src is None else src, self.piece(u, h), s.sg.at[u, j], getattr(s, r).at[u], dev)
    def k6(self, u, h, src=None):
        s = self.s
        return self.rc(self.piece(u, h) if src is None else src, self.piece(u, h), s.s6.at[u, h], s.r6.at[u, h], self.p.n1)
    def k7(self, u, j):
        s = self.s
        half = self.p.b1 if j == 0 else 1 - self.p.b1
        o = self.out.at[u, self.p.core, pl.ds(half * 192, 192)]
        return self.rc(o, o, s.s7.at[u, j], s.r7.at[u, j], self.p.partner)
    def give(self, name, u, N, dev):
        @pl.when(u + N < self.n)
        def _(): pl.semaphore_signal(getattr(self.s, name), inc=1, device_id=dev, device_id_type=MESH)
    def take(self, name, u, N):
        @pl.when(u >= N)
        def _(): pl.semaphore_wait(getattr(self.s, name), 1)
    def send0(self, u):
        self.take('c0', u, self.N0)
        self.k0(u).start()
    def A(self, u):
        s = self.s; p = self.p; w = self.w(u); i = lax.rem(u, self.N0)
        self.k0(u).wait()
        s.W[w] = s.W[w] + s.L0[i]
        self.give('c0', u, self.N0, p.partner)
        self.take('c1', u, self.N1)
        self.k1(u).start()
    def B(self, u):
        s = self.s; p = self.p; w = self.w(u); i = lax.rem(u, self.N1)
        self.k1(u).wait_recv()
        rows = pl.ds(p.b1 * 192, 192)
        s.W[w, rows] = s.W[w, rows] + s.L1[i]
        self.give('c1', u, self.N1, p.n1)
        @pl.when(p.end)
        def _():
            self.take('cA', u, self.NZ)
            self.kz(u, p.fh, 'LA', 'rA', p.near, 0).start()
    def zadd(self, u, h, L, r):
        s = self.s; w = self.w(u); i = lax.rem(u, self.NZ)
        self.kz(u, h, L, r, self.p.near, 0).wait_recv()
        rows = pl.ds(self.zrow(h), 96)
        s.W[w, rows] = s.W[w, rows] + getattr(s, L)[i]
    def C1(self, u):
        p = self.p
        @pl.when(p.mid)
        def _():
            self.zadd(u, p.fh, 'LA', 'rA')
            self.give('cA', u, self.NZ, p.near)
            self.take('cB', u, self.NZ)
            self.kz(u, p.fh, 'LB', 'rB', p.far, 0).start()
    def C2(self, u):
        p = self.p
        @pl.when(p.mid)
        def _():
            self.zadd(u, p.bh, 'LB', 'rB')
            self.give('cB', u, self.NZ, p.far)
            self.take('cA', u, self.NZ)
            self.kz(u, p.bh, 'LA', 'rA', p.near, 1).start()
    def C3(self, u):
        p = self.p
        @pl.when(p.end)
        def _():
            self.zadd(u, p.bh, 'LA', 'rA')
            self.give('cA', u, self.NZ, p.near)
            self.take('c3', u, self.N3)
            self.k3(u).start()
    def E(self, u):
        s = self.s; p = self.p; w = self.w(u); i = lax.rem(u, self.N3)
        @pl.when(p.end)
        def _():
            self.k3(u).wait()
            rows = pl.ds(self.zrow(p.bh), 96)
            s.W[w, rows] = s.W[w, rows] + s.L3[i]
            self.give('c3', u, self.N3, p.n2)
            self.kg(u, p.bh, 'gA', p.near, 0, self.held(u)).start()
            self.k6(u, p.bh, self.held(u)).start()
            self.kl(u).start()
    def K(self, u):
        p = self.p
        self.k1(u).wait_send()
        self.kz(u, p.fh, 'LB', 'rB', p.far, 0).wait_send()
        @pl.when(p.mid)
        def _(): self.kz(u, p.bh, 'LA', 'rA', p.near, 1).wait_send()
        @pl.when(p.end)
        def _():
            self.kl(u).wait()
            self.kg(u, p.bh, 'gA', p.near, 0, self.held(u)).wait_send()
            self.k6(u, p.bh, self.held(u)).wait_send()
    def F1(self, u):
        p = self.p
        @pl.when(p.mid)
        def _():
            self.kg(u, p.bh, 'gA', p.near, 0).wait_recv()
            self.kg(u, p.bh, 'gB', p.far, 0).start()
            self.k6(u, p.bh).start()
    def F2(self, u):
        p = self.p
        @pl.when(p.mid)
        def _():
            self.kg(u, p.fh, 'gB', p.far, 1).wait_recv()
            self.kg(u, p.fh, 'gA', p.near, 1).start()
            self.k6(u, p.fh).start()
    def F3(self, u):
        p = self.p
        @pl.when(p.end)
        def _():
            self.kg(u, p.fh, 'gA', p.near, 1).wait_recv()
            self.k6(u, p.fh).start()
        self.k7(u, 0).start()
    def G(self, u):
        for h in (0, 1): self.k6(u, h).wait_recv()
        self.k7(u, 1).start()
    def H(self, u):
        p = self.p
        self.k7(u, 0).wait()
        self.k7(u, 1).wait()
        self.k6(u, p.fh).wait_send()
        @pl.when(p.mid)
        def _():
            self.k6(u, p.bh).wait_send()
            self.kg(u, p.bh, 'gB', p.far, 0).wait_send()
            self.kg(u, p.fh, 'gA', p.near, 1).wait_send()
    def step(self, t):
        for st in ORDER:
            at = t - self.off[st]
            late = at >= self.first + self.pause
            u = jnp.where(late, at - self.pause, at)
            f = getattr(self, st)
            live = (at >= 0) & ((at < self.first) | late) & (u < self.n)
            pl.when(live)(lambda f=f, u=u: f(u))


def spread(values, gain):
    scale = lax.rsqrt(jnp.mean(values * values, axis=-1, keepdims=True) + epsilon)
    return values * scale * gain, scale


def dot_nn(a, b):
    return jnp.dot(a, b, preferred_element_type=jnp.float32)


def dot_nt(a, b):
    return lax.dot_general(a, b, (((1,), (1,)), ((), ())), preferred_element_type=jnp.float32)


def dot_tn(a, b):
    return lax.dot_general(a, b, (((0,), (0,)), ((), ())), preferred_element_type=jnp.float32)


def exact(a, b, dims):
    return lax.dot_general(
        a, b, (dims, ((), ())), precision=lax.Precision.HIGHEST,
        preferred_element_type=jnp.float32,
    )


class Layer:
    def __init__(self, plan, sizes):
        self.plan = plan
        self.z = sizes

    def scratch(self):
        z = self.z
        n, mem, d, ff = z.n, z.mem, z.d, z.ff
        all_rows = n + mem
        b16 = lambda *s: pltpu.VMEM(s, jnp.bfloat16)
        f32 = lambda *s: pltpu.VMEM(s, jnp.float32)
        L = z.L
        pairs = z.heads // 2
        DMA = pltpu.SemaphoreType.DMA
        own = dict(
            xb=b16(n, d), cb=b16(n, d), bk=b16(z.bank, 2, d),
            wq=b16(d, d), wk=b16(d, d), wv=b16(d, d), wo=b16(d, d),
            wib=b16(2, d, d), wub=b16(2, d, d),
            nall=b16(all_rows, d), qs=b16(n, d), ks=b16(all_rows, d), vs=b16(all_rows, d),
            att=b16(n, d), hid=f32(n, d), n2=b16(n, d), n2T=b16(d, n),
            oacc=f32(n, d), gacc=f32(n, d),
            act=b16(n, d), gib=b16(n, d),
            bias=f32(pairs, 2 * L, L), lse=f32(z.rows, 2 * L, 128),
            mq=b16(2 * L, 128), mk=b16(L, 128), mm=b16(z.slots, 128),
            dB=f32(pairs, 2 * L, L), dq=b16(n, d),
            seg=pltpu.VMEM((8, L), jnp.int32),
            sm=f32(16, d), lines=f32(16, 2 * L),
            isem=DMA((16,)), wsem=DMA((2, 2)), osem=DMA((6,)),
        )
        if self.plan is not None:
            own.update(self.plan.scratch())
            own.update(P=f32(self.plan.NP, BLK, BLK), L5=f32(5, 16, d), s5=DMA((5,)), r5=DMA((5,)))
        else:
            own.update(W=f32(2, BLK, BLK), P=f32(2, BLK, BLK), esem=DMA((2,)))
        return own

    def slots(self, u):
        if self.plan is None:
            return lax.rem(u, 2), lax.rem(u, 2)
        return self.plan.w(u), lax.rem(u, self.plan.NP)

    def emit(self, u):
        s = self.s
        if self.plan is not None:
            self.plan.send0(u)
            return
        w, p = self.slots(u)
        one = pltpu.make_async_copy(s.W.at[w], self.out.at[u, 0], s.esem.at[0])
        two = pltpu.make_async_copy(s.P.at[p], self.out.at[u, 1], s.esem.at[1])
        one.start()
        two.start()
        one.wait()
        two.wait()

    def emit_cols(self, u, value):
        s = self.s
        w, p = self.slots(u)

        @pl.when(self.core == 0)
        def _():
            s.W[w] = value[:, :BLK]
            s.P[p] = value[:, BLK:]

        @pl.when(self.core != 0)
        def _():
            s.W[w] = value[:, BLK:]
            s.P[p] = value[:, :BLK]

        self.emit(u)

    def step(self, t):
        if self.plan is not None:
            self.plan.step(t)

    def kernel(self, names, *refs):
        z = self.z
        ins = SimpleNamespace(**dict(zip(INS, refs)))
        outs = SimpleNamespace(**dict(zip(OUTS, refs[18:])))
        s = SimpleNamespace(**dict(zip(names, refs[24:])))
        s.gb, s.dk, s.dv = s.wub.at[0], s.wib.at[0], s.wib.at[1]
        s.dkm, s.dvm = s.wub.at[1, pl.ds(0, z.mem)], s.wub.at[1, pl.ds(z.mem, z.mem)]
        self.s, self.ins, self.outs, self.out = s, ins, outs, outs.out
        if self.plan is not None:
            self.plan.bind(s, outs.out, lambda u: s.P.at[lax.rem(u, self.plan.NP)])
            self.core = self.plan.p.core
        else:
            self.core = jnp.int32(0)
        self.load()
        if self.plan is not None:
            self.plan.entry()
        self.front()
        self.ffn()
        self.middle()
        self.attn_back()
        self.back()

    def load(self):
        s, i, z = self.s, self.ins, self.z
        n0 = z.n0
        cp = pltpu.make_async_copy
        sem = lambda k: s.isem.at[k]
        d = z.d
        self.c = SimpleNamespace(
            x0=cp(i.tok, s.xb.at[pl.ds(0, n0)], sem(0)),
            x1=cp(i.side, s.xb.at[pl.ds(n0, z.n - n0)], sem(1)),
            bk=cp(i.bank, s.bk, sem(2)),
            wq=cp(i.wq, s.wq, sem(3)), wk=cp(i.wk, s.wk, sem(4)),
            wv=cp(i.wv, s.wv, sem(5)), wo=cp(i.wo, s.wo, sem(6)),
            c0=cp(i.cot, s.cb.at[pl.ds(0, n0)], sem(7)),
            c1=cp(i.scot, s.cb.at[pl.ds(n0, z.n - n0)], sem(8)),
        )
        for k in ("x0", "x1", "bk", "wq", "wk", "wv", "wo"):
            getattr(self.c, k).start()
        for k in self.wcopy(0):
            k.start()
        self.c.c0.start()
        self.c.c1.start()

    def wcopy(self, c):
        s, i, d = self.s, self.ins, self.z.d
        slot = lax.rem(c, 2) if not isinstance(c, int) else c % 2
        cols = pl.ds(c * d if isinstance(c, int) else pl.multiple_of(c * d, d), d)
        return (
            pltpu.make_async_copy(i.wi.at[:, cols], s.wib.at[slot], s.wsem.at[slot, 0]),
            pltpu.make_async_copy(i.wu.at[cols, :], s.wub.at[slot], s.wsem.at[slot, 1]),
        )

    def tile(self, k):
        return pl.ds(pl.multiple_of(k * 256, 256), 256)

    def memory(self):
        s, z = self.s, self.z
        items = z.mem // 2
        picked = self.ins.idx[...].astype(jnp.float32).reshape(z.main * z.questions, z.top)
        item = lax.broadcasted_iota(jnp.int32, (items, z.main * z.questions), 0)
        question = lax.broadcasted_iota(jnp.int32, (items, z.main * z.questions), 1)
        mine = (item >= question * z.top) & (item < (question + 1) * z.top)
        lines = exact(jnp.where(mine, 1.0, 0.0), picked, ((1,), (0,)))
        base = jnp.sum(jnp.where(mine, question * z.top, 0).astype(jnp.float32), 1, keepdims=True)
        place = lax.broadcasted_iota(jnp.int32, (items, z.top), 0).astype(jnp.float32) - base
        lane = lax.broadcasted_iota(jnp.int32, (items, z.top), 1).astype(jnp.float32)
        index = jnp.sum(jnp.where(place == lane, lines, 0.0), axis=1, keepdims=True)
        entries = lax.broadcasted_iota(jnp.int32, (items, z.bank), 1).astype(jnp.float32)
        hot = jnp.where(entries == index, 1.0, 0.0).astype(jnp.bfloat16)
        return tuple(dot_nn(hot, s.bk[:, part, :]) for part in range(2))

    def mem_rows(self, r, part):
        z = self.z
        return pl.ds(z.n + r * z.slots + part * (z.slots // 2), z.slots // 2)

    def heads(self, value):
        lane = lax.broadcasted_iota(jnp.int32, (1, 128), 1)
        first = jnp.where(lane < 64, 1.0, 0.0).astype(jnp.bfloat16)
        second = jnp.where(lane < 64, 0.0, 1.0).astype(jnp.bfloat16)
        return jnp.concatenate([value * first, value * second], axis=0)

    def merge(self, value):
        rows = value.shape[0] // 2
        lane = lax.broadcasted_iota(jnp.int32, (rows, 128), 1)
        return jnp.where(lane < 64, value[:rows], value[rows:])

    def slot_mask(self):
        s, z = self.s, self.z
        lane = lax.broadcasted_iota(jnp.int32, (z.slots, 128), 1)
        slot = lax.broadcasted_iota(jnp.int32, (z.slots, 128), 0)
        slot = jnp.where(slot >= z.slots // 2, slot - z.slots // 2, slot)
        each = z.slots // 2 // z.questions
        hit = (slot >= lane * each) & (slot < (lane + 1) * each)
        s.mm[...] = jnp.where(hit, 1.0, 0.0).astype(jnp.bfloat16)

    def masks(self, r):
        s, z = self.s, self.z
        L = z.L
        row = s.seg[pl.ds(r, 1), :].astype(jnp.float32)
        down = jnp.broadcast_to(row, (L, L)).T[:, :128]
        lane = lax.broadcasted_iota(jnp.int32, (L, 128), 1)
        own = down == lane.astype(jnp.float32)
        s.mk[...] = jnp.where(own, 1.0, 0.0).astype(jnp.bfloat16)
        outside = jnp.where(own | (lane >= z.questions), 0.0, masked_value).astype(jnp.bfloat16)
        s.mq[pl.ds(0, L), :] = outside
        s.mq[pl.ds(L, L), :] = outside

    def spans(self, r, j):
        z = self.z
        rows = pl.ds(pl.multiple_of(r * z.L, z.L), z.L)
        mem = pl.ds(pl.multiple_of(z.n + r * z.slots, 32), z.slots)
        lanes = pl.ds(pl.multiple_of(j * 128, 128), 128)
        return rows, mem, lanes

    def scores(self, r, j, has_mem):
        s = self.s
        rows, mem, lanes = self.spans(r, j)
        q2 = self.heads(s.qs[rows, lanes])
        wide = jnp.concatenate([q2, s.mq[...]], axis=1)
        st = dot_nt(wide, jnp.concatenate([s.ks[rows, lanes], s.mk[...]], axis=1)) + s.bias[j]
        sm = None
        if has_mem:
            sm = dot_nt(wide, jnp.concatenate([s.ks[mem, lanes], s.mm[...]], axis=1))
        return q2, st, sm

    def fwd_pair(self, r, j, has_mem):
        s, z = self.s, self.z
        rows, mem, lanes = self.spans(r, j)
        q2, st, sm = self.scores(r, j, has_mem)
        top = jnp.max(st, axis=1, keepdims=True)
        if has_mem:
            top = jnp.maximum(top, jnp.max(sm, axis=1, keepdims=True))
        et = jnp.exp(st - top).astype(jnp.bfloat16)
        ones = jnp.ones((z.L, 128), jnp.bfloat16)
        mixed = dot_nn(et, jnp.concatenate([s.vs[rows, lanes], ones], axis=1))
        if has_mem:
            em = jnp.exp(sm - top).astype(jnp.bfloat16)
            ones = ones[: z.slots]
            mixed = mixed + dot_nn(em, jnp.concatenate([s.vs[mem, lanes], ones], axis=1))
        total = mixed[:, 128:]
        s.att[rows, lanes] = self.merge(mixed[:, :128] / total).astype(jnp.bfloat16)
        lane = lax.broadcasted_iota(jnp.int32, (2 * z.L, 128), 1)
        s.lse[r] = jnp.where(lane == j, top + jnp.log(total), s.lse[r])

    def front(self):
        s, z, i = self.s, self.z, self.ins
        L, d, n = z.L, z.d, z.n
        offs = i.offs[...]
        spots = offs.shape[1]
        bucket = lax.broadcasted_iota(jnp.int32, (i.btab.shape[1], spots), 0)
        hot = jnp.where(bucket == offs, 1.0, 0.0)
        line = exact(i.btab[...], hot, ((1,), (0,)))
        line = jnp.concatenate([line, jnp.zeros((line.shape[0], 2 * L - spots), jnp.float32)], 1)
        for h in range(z.heads):
            wide = jnp.broadcast_to(line[h : h + 1], (L, 2 * L))
            turned = pltpu.roll(wide, L + 1, 1, stride=1, stride_axis=0)
            s.bias[h // 2, pl.ds((h % 2) * L, L), :] = turned[:, :L]
        self.slot_mask()
        s.seg[pl.ds(0, z.main), :] = i.segm[...]
        s.seg[pl.ds(z.main, z.rows - z.main), :] = i.segs[...]
        g1 = i.g1[...].reshape(1, d)
        self.c.x0.wait()
        self.c.x1.wait()

        def norm_row(r, carry):
            rows = pl.ds(pl.multiple_of(r * L, L), L)
            s.nall[rows, :] = spread(s.xb[rows, :].astype(jnp.float32), g1)[0].astype(jnp.bfloat16)
            return carry

        lax.fori_loop(0, z.rows, norm_row, 0)
        self.c.bk.wait()
        half = z.slots // 2
        for part, memory in enumerate(self.memory()):
            normed = spread(memory, g1)[0].astype(jnp.bfloat16)
            for r in range(z.main):
                s.nall[self.mem_rows(r, part), :] = normed[r * half : (r + 1) * half]
        for k in ("wq", "wk", "wv"):
            getattr(self.c, k).wait()

        def project(k, carry):
            cols = self.tile(k)
            s.qs[:, cols] = dot_nn(s.nall[pl.ds(0, n), :], s.wq[:, cols]).astype(jnp.bfloat16)
            s.ks[:, cols] = dot_nn(s.nall[...], s.wk[:, cols]).astype(jnp.bfloat16)
            s.vs[:, cols] = dot_nn(s.nall[...], s.wv[:, cols]).astype(jnp.bfloat16)
            return carry

        lax.fori_loop(0, d // 256, project, 0)
        pairs = z.heads // 2

        def row(has_mem, r, carry):
            self.masks(r)

            def pair(j, inner):
                self.fwd_pair(r, j, has_mem)
                return inner

            return lax.fori_loop(0, pairs, pair, carry, unroll=FWD_UNROLL)

        lax.fori_loop(0, z.main, functools.partial(row, True), 0)
        lax.fori_loop(z.main, z.rows, functools.partial(row, False), 0)
        self.c.wo.wait()

        def attn_out(k, carry):
            cols = self.tile(k)
            s.hid[:, cols] = s.xb[:, cols].astype(jnp.float32) + dot_nn(s.att[...], s.wo[:, cols])
            return carry

        lax.fori_loop(0, d // 256, attn_out, 0)
        g2 = i.g2[...].reshape(1, d)

        def norm_two(r, carry):
            rows = pl.ds(pl.multiple_of(r * L, L), L)
            s.n2[rows, :] = spread(s.hid[rows, :], g2)[0].astype(jnp.bfloat16)
            return carry

        lax.fori_loop(0, z.rows, norm_two, 0)

    def ffn(self):
        s, z, i = self.s, self.z, self.ins
        d, n = z.d, z.n
        chunks = z.ff // d
        self.c.c0.wait()
        self.c.c1.wait()
        root = 0.7978845608028654

        def chunk(c, carry):
            slot = lax.rem(c, 2)
            for k in self.wcopy(c):
                k.wait()

            @pl.when(c + 1 < chunks)
            def _():
                for k in self.wcopy(c + 1):
                    k.start()

            def part(k, inner):
                cols = self.tile(k)
                v = dot_nn(s.n2[...], s.wib[slot, :, cols])
                ga = dot_nt(s.cb[...], s.wub[slot, cols, :])
                square = v * v
                th = jnp.tanh(root * v * (1.0 + 0.044715 * square))
                half = 0.5 * (1.0 + th)
                s.act[:, cols] = (v * half).astype(jnp.bfloat16)
                slope = half + (0.5 * root) * v * (1.0 - th * th) * (1.0 + 0.134145 * square)
                s.gib[:, cols] = (ga * slope).astype(jnp.bfloat16)

                @pl.when(k == 1)
                def _():
                    outer(0, inner)

                return inner

            def outer(k, inner):
                u = 4 * c + k
                cols = pl.ds(k * BLK, BLK)
                self.emit_cols(u, dot_tn(s.act[:, cols], s.cb[...]))
                self.step(u)
                return inner

            def gather(k, inner):
                cols = self.tile(k)
                po = dot_nn(s.act[...], s.wub[slot, :, cols])
                pg = dot_nt(s.gib[...], s.wib[slot, cols, :])

                @pl.when(c == 0)
                def _():
                    s.oacc[:, cols] = po
                    s.gacc[:, cols] = pg

                @pl.when(c > 0)
                def _():
                    s.oacc[:, cols] = s.oacc[:, cols] + po
                    s.gacc[:, cols] = s.gacc[:, cols] + pg

                return inner

            lax.fori_loop(0, d // 256, part, 0)
            lax.fori_loop(0, d // 256, gather, 0)
            outer(1, 0)

            @pl.when(c == 0)
            def _():
                s.n2T[...] = s.n2[...].T

            def inner_grad(k, inner):
                self.inner_unit(4 * c + 2 + k, k)
                self.step(4 * c + 2 + k)
                return inner

            @pl.when(c + 1 < chunks)
            def _():
                lax.fori_loop(0, 2, inner_grad, 0)

            return carry

        lax.fori_loop(0, chunks, chunk, 0)

    def inner_unit(self, u, k):
        s = self.s
        w, p = self.slots(u)
        cols = pl.ds(pl.multiple_of(k * BLK, BLK), BLK)
        mine = pl.ds(pl.multiple_of(self.core * BLK, BLK), BLK)
        other = pl.ds(pl.multiple_of((1 - self.core) * BLK, BLK), BLK)
        s.P[p] = dot_nn(s.n2T[other, :], s.gib[:, cols])
        s.W[w] = dot_nn(s.n2T[mine, :], s.gib[:, cols])
        self.emit(u)

    def out_unit(self, u, k):
        s = self.s
        cols = pl.ds(pl.multiple_of(k * BLK, BLK), BLK)
        self.emit_cols(u, dot_tn(s.att[:, cols], s.gb[...]))

    def middle(self):
        s, z, i = self.s, self.z, self.ins
        L, d, n, n0 = z.L, z.d, z.n, z.n0
        g2 = i.g2[...].reshape(1, d)

        def row(r, gain):
            rows = pl.ds(pl.multiple_of(r * L, L), L)
            hid = s.hid[rows, :]
            s.dq[rows, :] = (hid + s.oacc[rows, :]).astype(jnp.bfloat16)
            scale = lax.rsqrt(jnp.mean(hid * hid, axis=-1, keepdims=True) + epsilon)
            grad = s.gacc[rows, :]
            gain = gain + jnp.sum(grad * hid * scale, axis=0, keepdims=True)
            u = grad * g2
            average = jnp.mean(u * hid, axis=-1, keepdims=True)
            full = s.cb[rows, :].astype(jnp.float32) + scale * u - hid * (scale * scale * scale * average)
            s.gacc[rows, :] = full
            s.gb[rows, :] = full.astype(jnp.bfloat16)
            return gain

        gain = lax.fori_loop(0, z.rows, row, jnp.zeros((1, d), jnp.float32))
        s.sm[...] = jnp.zeros((16, d), jnp.float32)
        s.sm[pl.ds(13, 1), :] = gain
        self.o = (
            pltpu.make_async_copy(s.dq.at[pl.ds(0, n0)], self.outs.y, s.osem.at[0]),
            pltpu.make_async_copy(s.dq.at[pl.ds(n0, n - n0)], self.outs.sy, s.osem.at[1]),
        )
        for k in self.o:
            k.start()

        def back(k, carry):
            cols = self.tile(k)
            s.n2[:, cols] = dot_nt(s.gb[...], s.wo[cols, :]).astype(jnp.bfloat16)
            return carry

        lax.fori_loop(0, d // 256, back, 0)
        for k in self.o:
            k.wait()

    def bwd_pair(self, r, j, has_mem):
        s, z = self.s, self.z
        rows, mem, lanes = self.spans(r, j)
        q2, st, sm = self.scores(r, j, has_mem)
        lane = lax.broadcasted_iota(jnp.int32, (2 * z.L, 128), 1)
        lse = jnp.sum(jnp.where(lane == j, s.lse[r], 0.0), axis=1, keepdims=True)
        d2 = self.heads(s.n2[rows, lanes])
        pt = jnp.exp(st - lse)
        gt = dot_nt(d2, s.vs[rows, lanes])
        delta = jnp.sum(pt * gt, axis=1, keepdims=True)
        if has_mem:
            pm = jnp.exp(sm - lse)
            gm = dot_nt(d2, s.vs[mem, lanes])
            delta = delta + jnp.sum(pm * gm, axis=1, keepdims=True)
        dst = (pt * (gt - delta)).astype(jnp.bfloat16)
        grad_q = dot_nn(dst, s.ks[rows, lanes])
        s.dk[rows, lanes] = dot_tn(dst, q2).astype(jnp.bfloat16)
        s.dv[rows, lanes] = dot_tn(pt.astype(jnp.bfloat16), d2).astype(jnp.bfloat16)
        if has_mem:
            dsm = (pm * (gm - delta)).astype(jnp.bfloat16)
            grad_q = grad_q + dot_nn(dsm, s.ks[mem, lanes])
            slot = pl.ds(pl.multiple_of(r * z.slots, 32), z.slots)
            s.dkm[slot, lanes] = dot_tn(dsm, q2).astype(jnp.bfloat16)
            s.dvm[slot, lanes] = dot_tn(pm.astype(jnp.bfloat16), d2).astype(jnp.bfloat16)
        s.dq[rows, lanes] = self.merge(grad_q).astype(jnp.bfloat16)
        s.dB[j] = s.dB[j] + dst.astype(jnp.float32)

    def attn_back(self):
        s, z = self.s, self.z
        pairs = z.heads // 2
        first = 4 * (z.ff // z.d) - 2

        def clear(j, carry):
            s.dB[j] = jnp.zeros(s.dB.shape[1:], jnp.float32)
            return carry

        lax.fori_loop(0, pairs, clear, 0)

        def row(has_mem, r, carry):
            self.masks(r)

            def few(g, inner):
                def pair(k, last):
                    self.bwd_pair(r, g * 3 + k, has_mem)
                    return last

                lax.fori_loop(0, 3, pair, 0, unroll=BWD_UNROLL)
                if has_mem:
                    u = first + 2 * r + g

                    @pl.when(r == 0)
                    def _():
                        self.out_unit(u, g)

                    @pl.when(r > 0)
                    def _():
                        self.inner_unit(u, g)

                    self.step(u)
                return inner

            return lax.fori_loop(0, pairs // 3, few, carry)

        lax.fori_loop(0, z.main, functools.partial(row, True), 0)
        lax.fori_loop(z.main, z.rows, functools.partial(row, False), 0)

    def back(self):
        s, z, i = self.s, self.z, self.ins
        L, d, n, n0, mem = z.L, z.d, z.n, z.n0, z.mem
        first = 4 * (z.ff // d) + 2
        tok, mrows = pl.ds(0, n), pl.ds(n, mem)
        def difference(j):
            for side in range(2):
                grid = s.dB[j, pl.ds(side * L, L), :]
                wide = jnp.concatenate([grid, jnp.zeros((L, L), jnp.float32)], axis=1)
                wide = pltpu.roll(wide, L - 1, 1)
                half = L // 2
                while half:
                    wide = wide[:half] + pltpu.roll(wide[half:], 2 * L - half, 1)
                    half = half // 2
                s.lines[pl.ds(2 * j + side, 1), :] = wide

        g1 = i.g1[...].reshape(1, d)

        def grads(k):
            cols = self.tile(k)
            s.hid[:, cols] = (
                dot_nt(s.dq[...], s.wq[cols, :])
                + dot_nt(s.dk[...], s.wk[cols, :])
                + dot_nt(s.dv[...], s.wv[cols, :])
            )
            s.oacc[pl.ds(0, mem), cols] = dot_nt(s.dkm[...], s.wk[cols, :]) + dot_nt(
                s.dvm[...], s.wv[cols, :]
            )

        def row(r):
            rows = pl.ds(pl.multiple_of(r * L, L), L)
            x = s.xb[rows, :].astype(jnp.float32)
            scale = lax.rsqrt(jnp.mean(x * x, axis=-1, keepdims=True) + epsilon)
            grad = s.hid[rows, :]
            part = jnp.sum(grad * x * scale, axis=0, keepdims=True)
            s.sm[pl.ds(12, 1), :] = s.sm[pl.ds(12, 1), :] + part
            v = grad * g1
            average = jnp.mean(v * x, axis=-1, keepdims=True)
            full = s.gacc[rows, :] + scale * v - x * (scale * scale * scale * average)
            s.gb[rows, :] = full.astype(jnp.bfloat16)

        tiles = d // 256

        def rest_of(j):
            difference(j)
            pl.when(j < tiles)(lambda: grads(j))
            pl.when(j >= tiles)(lambda: row(j - tiles))

        u = first
        for grad, grad_mem in ((s.dq, None), (s.dk, s.dkm), (s.dv, s.dvm)):
            def one(k, carry, grad=grad, grad_mem=grad_mem, u=u):
                cols = pl.ds(pl.multiple_of(k * BLK, BLK), BLK)
                value = dot_tn(s.nall[tok, cols], grad[...])
                if grad_mem is not None:
                    value = value + dot_tn(s.nall[mrows, cols], grad_mem[...])
                self.emit_cols(u + k, value)
                self.step(u + k)
                rest_of(u - first + k)
                return carry

            lax.fori_loop(0, 2, one, 0)
            u = u + 2
        t = first + 6
        gain = s.sm[pl.ds(12, 1), :]
        late = (
            pltpu.make_async_copy(s.gb.at[pl.ds(0, n0)], self.outs.gt, s.osem.at[2]),
            pltpu.make_async_copy(s.gb.at[pl.ds(n0, n - n0)], self.outs.sgt, s.osem.at[3]),
        )
        for k in late:
            k.start()
        half = z.slots // 2
        for part, memory in enumerate(self.memory()):
            scale = lax.rsqrt(jnp.mean(memory * memory, axis=-1, keepdims=True) + epsilon)
            unit = memory * scale
            for r in range(z.main):
                grad = s.oacc[pl.ds(r * z.slots + part * half, half), :]
                gain = gain + jnp.sum(grad * unit[r * half : (r + 1) * half], axis=0, keepdims=True)
        s.sm[pl.ds(12, 1), :] = gain
        offs = i.offs[...]
        bucket = lax.broadcasted_iota(jnp.int32, (128, offs.shape[1]), 0)
        hot = jnp.where(bucket == offs, 1.0, 0.0)
        s.sm[pl.ds(0, z.heads), pl.ds(0, 128)] = exact(
            s.lines[pl.ds(0, z.heads), pl.ds(0, offs.shape[1])], hot, ((1,), (1,))
        )
        if self.plan is not None:
            self.finish(t)
        for k in late:
            k.wait()
        self.outs.small[...] = s.sm[...]

    def steps_from(self, t, count):
        def one(k, carry):
            self.step(k)
            return carry

        lax.fori_loop(t, t + count, one, 0)
        return t + count

    def finish(self, t):
        plan, s = self.plan, self.s
        p = plan.p
        peers = (p.partner, p.xn, p.yn, p.near, p.far)
        for k, dev in enumerate(peers):
            copy = plan.rc(s.sm, s.L5.at[k], s.s5.at[k], s.r5.at[k], dev)
            copy.start()
            t = self.steps_from(t, SMALL_GAP)
            copy.wait()
            s.sm[...] = s.sm[...] + s.L5[k]

        def rest(k, carry):
            self.step(k)
            return carry

        lax.fori_loop(t, plan.steps, rest, 0)


def place_units(
    sizes, units, y, gt, sy, sgt, small,
    oy, ogt, osy, osgt, wq, wk, wv, wo, wi, wu, gb, gg1, gg2,
    hold, vy, vgt, vsy, vsgt, sem, late, rsem,
):
    d, ff = sizes.d, sizes.ff
    copies = []

    def put(u, half, ref, row, col):
        k = len(copies)
        place = ref.at[pl.ds(row, BLK), pl.ds(col, BLK)]
        copies.append(
            (
                pltpu.make_async_copy(units.at[u, half], hold.at[k], sem.at[k]),
                pltpu.make_async_copy(hold.at[k], place, late.at[k]),
            )
        )

    for c in range(ff // d):
        for k in range(2):
            for half in range(2):
                put(4 * c + k, half, wu, c * d + k * BLK, half * BLK)
                after = 2 if c + 1 < ff // d else 4
                put(4 * c + after + k, half, wi, half * BLK, c * d + k * BLK)
    for k in range(2):
        for half in range(2):
            put(4 * (ff // d) - 2 + k, half, wo, k * BLK, half * BLK)
    u = 4 * (ff // d) + 2
    for ref in (wq, wk, wv):
        for k in range(2):
            for half in range(2):
                put(u + k, half, ref, k * BLK, half * BLK)
        u = u + 2
    for k, (src, mid, dst) in enumerate(
        ((y, vy, oy), (gt, vgt, ogt), (sy, vsy, osy), (sgt, vsgt, osgt))
    ):
        copies.append(
            (
                pltpu.make_async_copy(src, mid, rsem.at[k, 0]),
                pltpu.make_async_copy(mid, dst, rsem.at[k, 1]),
            )
        )
    for fetch, store in copies:
        fetch.start()
    heads, buckets = gb.shape
    gb[...] = small[pl.ds(0, heads), pl.ds(0, buckets)]
    gg1[...] = small[12, :]
    gg2[...] = small[13, :]
    for fetch, store in copies:
        fetch.wait()
        store.start()
    for fetch, store in copies:
        store.wait()


def body(
    remote,
    tokens,
    segments,
    picked,
    offsets,
    memory_bank,
    side_tokens,
    side_segments,
    w_query,
    w_key,
    w_value,
    w_attn_out,
    w_inner,
    w_outer,
    bias_table,
    gain_one,
    gain_two,
    cotangent,
    side_cotangent,
):
    d, ff = w_inner.shape
    main, L = segments.shape
    heads = bias_table.shape[1]
    buckets = bias_table.shape[0]
    n0, n1 = tokens.shape[0], side_tokens.shape[0]
    slots = picked.shape[1] * picked.shape[2] * 2
    sizes = SimpleNamespace(
        n=n0 + n1, n0=n0, d=d, ff=ff, L=L, main=main, rows=main + side_segments.shape[0],
        heads=heads, slots=slots, mem=main * slots, questions=picked.shape[1], top=picked.shape[2],
        bank=memory_bank.shape[0],
    )
    units = 4 * (ff // d) + 8
    plan = Comm(units, GAPS) if remote else None
    layer = Layer(plan, sizes)
    scratch = layer.scratch()
    hbm = pl.BlockSpec(memory_space=pl.ANY)
    vmem = pl.BlockSpec(memory_space=pltpu.VMEM)
    shape = jax.ShapeDtypeStruct
    joined, output, grad_tokens, side_output, grad_side, small = pl.pallas_call(
        functools.partial(layer.kernel, list(scratch)),
        out_shape=(
            shape((units, 2, BLK, BLK), jnp.float32),
            shape(tokens.shape, jnp.bfloat16),
            shape(tokens.shape, jnp.bfloat16),
            shape(side_tokens.shape, jnp.bfloat16),
            shape(side_tokens.shape, jnp.bfloat16),
            shape((16, d), jnp.float32),
        ),
        in_specs=[hbm] * 11 + [vmem] * 7,
        out_specs=(hbm,) * 5 + (vmem,),
        scratch_shapes=list(scratch.values()),
        compiler_params=pltpu.CompilerParams(
            collective_id=0 if remote else None, has_side_effects=True, vmem_limit_bytes=VMEM_LIMIT
        ),
    )(
        tokens, side_tokens, cotangent, side_cotangent,
        memory_bank, w_query, w_key, w_value, w_attn_out, w_inner, w_outer,
        picked, segments, side_segments, offsets.reshape(1, -1), bias_table.T,
        gain_one, gain_two,
    )
    if not remote:
        joined = lax.psum(joined, AXES)
        small = lax.psum(small, AXES)
    square = shape((d, d), jnp.float32)
    wide, narrow = shape(tokens.shape, jnp.bfloat16), shape(side_tokens.shape, jnp.bfloat16)
    gain = shape((d,), jnp.float32)
    hold = pltpu.VMEM(tokens.shape, jnp.bfloat16), pltpu.VMEM(side_tokens.shape, jnp.bfloat16)
    outs = pl.pallas_call(
        functools.partial(place_units, sizes),
        out_shape=(
            wide, wide, narrow, narrow, square, square, square, square,
            shape((d, ff), jnp.float32), shape((ff, d), jnp.float32),
            shape((heads, buckets), jnp.float32), gain, gain,
        ),
        in_specs=[hbm] * 5 + [vmem],
        out_specs=(hbm,) * 10 + (vmem,) * 3,
        scratch_shapes=[
            pltpu.VMEM((2 * units, BLK, BLK), jnp.float32),
            hold[0], hold[0], hold[1], hold[1],
            pltpu.SemaphoreType.DMA((2 * units,)),
            pltpu.SemaphoreType.DMA((2 * units,)),
            pltpu.SemaphoreType.DMA((4, 2)),
        ],
        compiler_params=pltpu.CompilerParams(vmem_limit_bytes=VMEM_LIMIT),
    )(joined, output, grad_tokens, side_output, grad_side, small)
    output, grad_tokens, side_output, grad_side = outs[:4]
    return (output, grad_tokens, side_output, grad_side) + tuple(outs[4:10]) + (outs[10].T,) + tuple(outs[11:])


INS = ["tok", "side", "cot", "scot", "bank", "wq", "wk", "wv", "wo", "wi", "wu"]
INS = INS + ["idx", "segm", "segs", "offs", "btab", "g1", "g2"]
OUTS = ["out", "y", "gt", "sy", "sgt", "small"]
VMEM_LIMIT = 63 * 2**20
FWD_UNROLL = 6
BWD_UNROLL = 1
SMALL_GAP = 3


def solution(mesh):
    in_specs = (
        P(AXES, None),
        P(AXES, None),
        P(AXES, None, None),
        P(),
        P(),
        P(AXES, None),
        P(AXES, None),
        P(),
        P(),
        P(),
        P(),
        P(),
        P(),
        P(),
        P(),
        P(),
        P(AXES, None),
        P(AXES, None),
    )
    out_specs = (
        P(AXES, None),
        P(AXES, None),
        P(AXES, None),
        P(AXES, None),
        P(),
        P(),
        P(),
        P(),
        P(),
        P(),
        P(),
        P(),
        P(),
    )
    remote = dict(mesh.shape) == {'dp': 4, 'replica': 8}
    return jax.shard_map(functools.partial(body, remote), mesh=mesh, in_specs=in_specs, out_specs=out_specs, check_vma=False)
```
